32 devices in a mesh: depth: 2 (over core), scan: 16 (over z, y, x).
Axes of the slice: x: 2, y: 2, z: 4, core: 2. Of those that a mesh axis runs over, the one named last changes fastest.
Arguments:
- objects: float32 [6, 2, 2048, 256], P('depth', None, 'scan')
- probe: float32 [2, 128, 128], replicated, may hold values from -6 to 6
- row_offsets: int32 [32], P('scan'), may hold values from 0 to 2048, as said below
- col_offsets: int32 [32], P('scan'), may hold values from 0 to 128, as said below
- intensity: float32 [32, 128, 128], P('scan'), may hold values from 0.1 to 4
Outputs:
- object_grad: float32 [6, 2, 2048, 256], P('depth', None, 'scan')
- probe_grad: float32 [2, 128, 128], P(None, 'depth')
The draws below stay inside these ranges and needn't reach their ends.
Inputs may be any that keep to these rules, and one draw needn't show every extreme that they name: `row_offsets`: position i is measured by scan index i // 2; its row offset lies from (i // 2) * 128 to (i // 2 + 1) * 128, both ends included, and on every scan index one of its positions has the upper end. `col_offsets`: some position has column offset 0 and some has the largest.
All inputs are finite; a program needn't handle non-finite values.
Results may differ from the reference program's by a relative error of at most 0.0003.
Values sent between devices are 32-bit elements; how exact they have to be, the bound alone decides.
No kernel may reach another device: no remote copies, remote signals or barrier semaphores. Data moves between devices by JAX's collectives and lax.ppermute only.
A program may use at most 64 MiB of HBM per device.

```python
import math
import jax
import jax.numpy as jnp
from jax import lax

WIN = 128
WAVES = 2
TILE_R = 128
OBJ_COLS = 256
SLICES = 6
OBJ_ROWS = 2048
POSITIONS = 32


def draw_objects(key, part):
    key_amp, key_phase = jax.random.split(jax.random.fold_in(key, 11))
    plane_shape = (SLICES, OBJ_ROWS, OBJ_COLS)
    amplitude = jax.random.uniform(key_amp, plane_shape, jnp.float32, 0.8, 1.2)
    phase_value = jax.random.uniform(key_phase, plane_shape, jnp.float32, -math.pi, math.pi)
    return jnp.stack([amplitude * jnp.cos(phase_value), amplitude * jnp.sin(phase_value)], axis=1)


def draw_row_offsets(key, part):
    key_local, key_pick = jax.random.split(jax.random.fold_in(key, 23))
    local_rows = jax.random.randint(key_local, (POSITIONS,), 0, TILE_R + 1, jnp.int32)
    owner = jnp.arange(POSITIONS, dtype=jnp.int32) // WAVES
    picked = jax.random.randint(key_pick, (POSITIONS // WAVES,), 0, WAVES, jnp.int32)
    forced = jnp.arange(POSITIONS, dtype=jnp.int32) % WAVES == picked[owner]
    local_rows = jnp.where(forced, TILE_R, local_rows)
    return owner * TILE_R + local_rows


def draw_col_offsets(key, part):
    key_cols, key_perm = jax.random.split(jax.random.fold_in(key, 37))
    columns = jax.random.randint(key_cols, (POSITIONS,), 0, OBJ_COLS - WIN + 1, jnp.int32)
    order = jax.random.permutation(key_perm, POSITIONS)
    columns = columns.at[order[0]].set(OBJ_COLS - WIN)
    columns = columns.at[order[1]].set(0)
    return columns


def block_levels(stream_key, extent, shards, least, largest):
    def one(dim, shards_of):
        draws = jax.random.uniform(jax.random.fold_in(jax.random.fold_in(stream_key, 6), dim), (shards_of,), jnp.float32, least / len(shards), largest / len(shards))
        return jnp.repeat(jnp.exp(draws), extent[dim] // shards_of).reshape((-1,) + (1,) * (len(extent) - dim - 1))

    gain = one(*shards[0])
    for cut in shards[1:]:
        gain = gain * one(*cut)
    return gain


def gaussian(key, shape, spread, most, held_as=jnp.bfloat16):
    return jnp.clip(spread * jax.random.normal(key, shape, jnp.float32), -most, most).astype(held_as)


def setup_inputs(seed: int = 0) -> dict:
    key_of = jax.random.split(jax.random.key(seed), 6)
    return {
        "objects": draw_objects(jax.random.fold_in(key_of[5], 71), 0),
        "probe": gaussian(key_of[1], (2, WIN, WIN), 1.0, 6.0, jnp.float32),
        "row_offsets": draw_row_offsets(jax.random.fold_in(key_of[5], 71), 0),
        "col_offsets": draw_col_offsets(jax.random.fold_in(key_of[5], 71), 0),
        "intensity": jnp.clip(jnp.exp(math.log(4.0) - 3.6888794 * jax.random.uniform(key_of[4], (POSITIONS, WIN, WIN), jnp.float32) ** block_levels(key_of[4], (POSITIONS, WIN, WIN), ((0, 16),), -0.2, 0.2)), 0.1, 4.0),
    }


PROPAGATION = 0.5


def reference(objects, probe, row_offsets, col_offsets, intensity):
    slab_total = objects.shape[0]
    object_rows = objects.shape[2]
    window_width = probe.shape[-1]
    extended = jnp.concatenate([objects, objects[:, :, :window_width, :]], axis=2)
    grid_index = jnp.arange(window_width, dtype=jnp.int32)
    frequency = jnp.where(grid_index < window_width // 2, grid_index, grid_index - window_width)
    squared = frequency[:, None] ** 2 + frequency[None, :] ** 2
    phase_angle = squared.astype(probe.dtype) * (PROPAGATION * math.pi / window_width)
    factor = lax.complex(jnp.cos(phase_angle), -jnp.sin(phase_angle))
    start_wave = lax.complex(probe[0], probe[1])
    window_shape = (slab_total, 2, window_width, window_width)

    def forward_fft(values):
        return jnp.fft.fft2(values, norm="ortho")

    def inverse_fft(values):
        return jnp.fft.ifft2(values, norm="ortho")

    def one_position(loop_state, position):
        accum, probe_sum = loop_state
        row_start, col_start, measured = position
        corner = (jnp.int32(0), jnp.int32(0), row_start.astype(jnp.int32), col_start.astype(jnp.int32))
        window = lax.dynamic_slice(extended, corner, window_shape)
        layers = lax.complex(window[:, 0], window[:, 1])

        def forward(wave, layer_now):
            return inverse_fft(factor * forward_fft(wave * layer_now)), wave

        exit_wave, inputs = lax.scan(forward, start_wave, layers)
        far_wave = forward_fft(exit_wave)
        misfit = far_wave.real ** 2 + far_wave.imag ** 2 - measured
        back_start = inverse_fft(2.0 * misfit * far_wave)

        def backward(gradient, pair):
            layer_now, wave_in = pair
            chi_grad = inverse_fft(jnp.conj(factor) * forward_fft(gradient))
            return jnp.conj(layer_now) * chi_grad, jnp.conj(wave_in) * chi_grad

        first_grad, layer_grads = lax.scan(backward, back_start, (layers, inputs), reverse=True)
        update = jnp.stack([layer_grads.real, layer_grads.imag], axis=1)
        accum = lax.dynamic_update_slice(accum, lax.dynamic_slice(accum, corner, window_shape) + update, corner)
        return (accum, probe_sum + first_grad), None

    accum_start = jnp.zeros(extended.shape, objects.dtype)
    probe_start = lax.complex(jnp.zeros_like(probe[0]), jnp.zeros_like(probe[0]))
    (accum, probe_sum), unused = lax.scan(one_position, (accum_start, probe_start), (row_offsets, col_offsets, intensity))
    object_grad = accum[:, :, :object_rows, :].at[:, :, :window_width, :].add(accum[:, :, object_rows:, :])
    probe_grad = jnp.stack([probe_sum.real, probe_sum.imag])
    return object_grad, probe_grad
```

```python
import math

import jax
import jax.numpy as jnp
import ml_dtypes
import numpy as np
from jax import lax
from jax.experimental import pallas as pl
from jax.experimental.pallas import tpu as pltpu
from jax.sharding import PartitionSpec as P

PROPAGATION = 0.5
VMEM_LIMIT = 48 * 1024 * 1024


def block_form(matrix):
    return np.block([[matrix.real, -matrix.imag], [matrix.imag, matrix.real]])


def constant_tables(width):
    grid = np.arange(width)
    frequency = np.where(grid < width // 2, grid, grid - width)
    dft = np.exp(-2j * np.pi * ((grid[:, None] * grid[None, :]) % width) / width) / math.sqrt(width)
    chirp = np.exp(-1j * PROPAGATION * np.pi * frequency.astype(np.float64) ** 2 / width)
    step = dft.conj() @ (chirp[:, None] * dft)
    step = 0.5 * (step + step.T)
    full = np.stack([block_form(m) for m in (step, step.conj(), dft, dft.conj())])
    high = full.astype(np.float32).astype(ml_dtypes.bfloat16)
    low = (full - high.astype(np.float64)).astype(np.float32).astype(ml_dtypes.bfloat16)
    return np.stack([high, low], axis=1)


def halves(x):
    high = x.astype(jnp.bfloat16)
    return high, (x - high.astype(jnp.float32)).astype(jnp.bfloat16)


def dot(a, b):
    return jnp.dot(a, b, preferred_element_type=jnp.float32)


def times_right(x, high, low):
    x_high, x_low = halves(x)
    return dot(x_high, high) + (dot(x_low, high) + dot(x_high, low))


def times_left(high, low, x):
    x_high, x_low = halves(x)
    return dot(high, x_high) + (dot(high, x_low) + dot(low, x_high))


def both_sides(re, im, tables, which):
    n = re.shape[0]
    y = times_right(jnp.concatenate([re, im], axis=1), tables[which ^ 1, 0], tables[which ^ 1, 1])
    y = jnp.concatenate([y[:, :n], y[:, n:]], axis=0)
    z = times_left(tables[which, 0], tables[which, 1], y)
    return z[:n], z[n:]


def cut_kernel(scal, obj, mine, other, halo):
    slab, _, rows, cols = obj.shape
    width = mine.shape[-1]
    for s in range(slab):
        for p in range(2):
            tile = obj[s, p]
            for k, out in enumerate((mine, other, halo)):
                row, col = scal[2 * k], scal[2 * k + 1]
                part = pltpu.roll(tile, lax.rem(cols - col, cols), 1)[:, :width]
                out[s, p] = pltpu.roll(part, lax.rem(rows - row, rows), 0)


def wave_kernel(depth_count, scal, tables, probe, measured, *rest):
    own_parts = rest[:depth_count]
    halo_parts = rest[depth_count : 2 * depth_count]
    grads = rest[2 * depth_count : 3 * depth_count]
    probe_parts = rest[3 * depth_count : 4 * depth_count]
    layers, waves = rest[4 * depth_count :]
    slab = own_parts[0].shape[0]
    n = probe.shape[-1]
    count = slab * depth_count
    split, depth = scal[0], scal[1]
    inside = lax.broadcasted_iota(jnp.int32, (n, n), 0) < n - split
    for j in range(depth_count):
        base = lax.rem(depth - j + depth_count, depth_count) * slab
        for s in range(slab):
            layers[base + s] = own_parts[j][s]
    for q in range(depth_count):
        for s in range(slab):
            for p in range(2):
                layers[q * slab + s, p] = jnp.where(inside, layers[q * slab + s, p], halo_parts[q][s, p])

    def enter(s, re, im):
        waves[s, 0] = re
        waves[s, 1] = im
        o_re, o_im = layers[s, 0], layers[s, 1]
        return re * o_re - im * o_im, re * o_im + im * o_re

    def forward(s, wave):
        return both_sides(*enter(s, *wave), tables, 0)

    wave = lax.fori_loop(0, count - 1, forward, (probe[0], probe[1]), unroll=True if count <= 8 else 1)
    far_re, far_im = both_sides(*enter(count - 1, *wave), tables, 2)
    misfit = 2.0 * (far_re * far_re + far_im * far_im - measured[...])
    chi = both_sides(misfit * far_re, misfit * far_im, tables, 3)

    def leave(s, chi_re, chi_im):
        w_re, w_im = waves[s, 0], waves[s, 1]
        o_re, o_im = layers[s, 0], layers[s, 1]
        waves[s, 0] = w_re * chi_re + w_im * chi_im
        waves[s, 1] = w_re * chi_im - w_im * chi_re
        return o_re * chi_re + o_im * chi_im, o_re * chi_im - o_im * chi_re

    def backward(t, chi):
        return both_sides(*leave(count - 1 - t, *chi), tables, 1)

    chi = lax.fori_loop(0, count - 1, backward, chi, unroll=True if count <= 8 else 1)
    grad = leave(0, *chi)
    for j in range(depth_count):
        base = lax.rem(depth + j, depth_count) * slab
        for s in range(slab):
            grads[j][s] = waves[base + s]
    rows = n // depth_count
    waves[0, 0] = jnp.where(depth < 2, grad[0], 0.0)
    waves[0, 1] = jnp.where(depth < 2, grad[1], 0.0)
    for j in range(depth_count):
        start = pl.multiple_of(lax.rem(depth + j, depth_count) * rows, rows)
        for p in range(2):
            probe_parts[j][p] = waves[0, p, pl.ds(start, rows), :]


def place_kernel(scal, *refs):
    *parts, out = refs
    slab, _, rows, cols = out.shape
    width = parts[0].shape[-1]
    row_index = lax.broadcasted_iota(jnp.int32, (rows, width), 0)
    blank = jnp.zeros((rows, cols - width), jnp.float32)
    masks = [(row_index >= scal[4 * k + 2]) & (row_index < scal[4 * k + 3]) for k in range(len(parts))]
    for s in range(slab):
        for p in range(2):
            total = None
            for k, part in enumerate(parts):
                x = pltpu.roll(part[s, p], scal[4 * k], 0)
                x = jnp.where(masks[k], x, 0.0)
                x = pltpu.roll(jnp.concatenate([x, blank], axis=1), scal[4 * k + 1], 1)
                total = x if total is None else total + x
            out[s, p] = total


def call(kernel, name, scalars, arrays, outs, scratch=()):
    vmem = pl.BlockSpec(memory_space=pltpu.VMEM)
    moved = sum(math.prod(x.shape) * x.dtype.itemsize for x in (*arrays, *outs))
    return pl.pallas_call(
        kernel,
        name=name,
        out_shape=outs,
        in_specs=[pl.BlockSpec(memory_space=pltpu.SMEM)] + [vmem] * len(arrays),
        out_specs=[vmem] * len(outs),
        scratch_shapes=scratch,
        compiler_params=pltpu.CompilerParams(vmem_limit_bytes=VMEM_LIMIT),
        cost_estimate=pl.CostEstimate(flops=moved, bytes_accessed=moved, transcendentals=0),
    )(scalars, *arrays)


def total_over(x, axis):
    count = lax.axis_size(axis)
    if count & (count - 1):
        return lax.psum(x, axis)
    step = 1
    while step < count:
        x = x + lax.ppermute(x, axis, [(i, i ^ step) for i in range(count)])
        step *= 2
    return x


def body(objects, probe, row_offsets, col_offsets, intensity):
    slab, _, tile_rows, cols = objects.shape
    n = probe.shape[-1]
    depth_count, scan_count = lax.axis_size("depth"), lax.axis_size("scan")
    depth, scan = lax.axis_index("depth"), lax.axis_index("scan")
    f32 = jnp.float32
    ahead = [(i, (i + 1) % scan_count) for i in range(scan_count)]

    local = row_offsets - scan * tile_rows
    second = local[1] == tile_rows
    row_b = jnp.where(second, local[0], local[1])
    col_b = jnp.where(second, col_offsets[0], col_offsets[1])
    col_a = jnp.where(second, col_offsets[1], col_offsets[0])
    sent = lax.ppermute(jnp.stack([col_a, row_b, col_b]), "scan", ahead)
    col_a, row_p, col_p = sent[0], sent[1], sent[2]
    measured_a = lax.ppermute(jnp.where(second, intensity[1], intensity[0]), "scan", ahead)
    measured_b = jnp.where(second, intensity[0], intensity[1])

    on_a = depth == 0
    zero = jnp.zeros_like(col_a)
    row_mine, col_mine = jnp.where(on_a, zero, row_b), jnp.where(on_a, col_a, col_b)
    row_other, col_other = jnp.where(on_a, row_b, zero), jnp.where(on_a, col_b, col_a)
    window = jax.ShapeDtypeStruct((slab, 2, n, n), f32)
    mine, other, halo = call(
        cut_kernel,
        "cut",
        jnp.stack([row_mine, col_mine, row_other, col_other, row_p, col_p]),
        [objects],
        [window] * 3,
    )

    own = [mine]
    for j in range(1, depth_count):
        target = lax.rem(depth + j, depth_count)
        payload = other if depth_count == 2 else jnp.where((target == 0) | (depth == 0), other, mine)
        route = [((t - j) % depth_count, t) for t in (0, 1)]
        own.append(lax.ppermute(payload, "depth", route))

    def across(x, source, target, shift):
        route = [(source * scan_count + i, target * scan_count + (i + shift) % scan_count) for i in range(scan_count)]
        return lax.ppermute(x, ("depth", "scan"), route)

    halos = [across(halo, q, 1, -1) for q in range(depth_count)]

    split = jnp.where(on_a, zero, row_b)
    measured = jnp.where(on_a, measured_a, measured_b)
    tables = jnp.asarray(constant_tables(n))
    parts = call(
        lambda *refs: wave_kernel(depth_count, *refs),
        "wave",
        jnp.stack([split, depth]),
        [tables, probe, measured, *own, *halos],
        [window] * depth_count + [jax.ShapeDtypeStruct((2, n // depth_count, n), f32)] * depth_count,
        [pltpu.VMEM((slab * depth_count, 2, n, n), f32)] * 2,
    )
    grads, probe_parts = parts[:depth_count], parts[depth_count:]

    back = [grads[0]]
    probe_grad = probe_parts[0]
    for j in range(1, depth_count):
        back.append(lax.ppermute(grads[j], "depth", [(t, (t + j) % depth_count) for t in (0, 1)]))
        probe_grad = probe_grad + lax.ppermute(
            probe_parts[j], "depth", [(t, (t + j) % depth_count) for t in range(depth_count)]
        )
    spill = [across(grads[(q - 1) % depth_count], 1, q, 1) for q in range(depth_count)]
    arrived = spill[0]
    for q in range(1, depth_count):
        arrived = jnp.where(depth == q, spill[q], arrived)

    where_to = []
    for j in range(depth_count):
        is_a = depth == j
        is_b = lax.rem(depth + depth_count - 1, depth_count) == j
        row = jnp.where(is_a, zero, row_b)
        col = jnp.where(is_a, col_a, col_b)
        first = jnp.where(is_a, zero, row_b)
        last = jnp.where(is_a | is_b, zero + tile_rows, zero)
        where_to += [lax.rem(row, tile_rows), col, first, last]
    where_to += [lax.rem(row_p, tile_rows), col_p, zero, row_p]
    (object_grad,) = call(
        place_kernel,
        "place",
        jnp.stack(where_to),
        [*back, arrived],
        [jax.ShapeDtypeStruct(objects.shape, f32)],
    )
    return object_grad, total_over(probe_grad, "scan")


def solution(mesh):
    in_specs = (P("depth", None, "scan", None), P(), P("scan"), P("scan"), P("scan", None, None))
    out_specs = (P("depth", None, "scan", None), P(None, "depth", None))
    return jax.shard_map(body, mesh=mesh, in_specs=in_specs, out_specs=out_specs, check_vma=False)
```

```python
import math

import jax
import jax.numpy as jnp
import ml_dtypes
import numpy as np
from jax import lax
from jax.experimental import pallas as pl
from jax.experimental.pallas import tpu as pltpu
from jax.sharding import PartitionSpec as P

PROPAGATION = 0.5
VMEM_LIMIT = 48 * 1024 * 1024


def block_form(matrix):
    return np.block([[matrix.real, -matrix.imag], [matrix.imag, matrix.real]])


def constant_tables(width):
    grid = np.arange(width)
    frequency = np.where(grid < width // 2, grid, grid - width)
    dft = np.exp(-2j * np.pi * ((grid[:, None] * grid[None, :]) % width) / width) / math.sqrt(width)
    chirp = np.exp(-1j * PROPAGATION * np.pi * frequency.astype(np.float64) ** 2 / width)
    step = dft.conj() @ (chirp[:, None] * dft)
    step = 0.5 * (step + step.T)
    full = np.stack([block_form(m) for m in (step, step.conj(), dft, dft.conj())])
    high = full.astype(np.float32).astype(ml_dtypes.bfloat16)
    low = (full - high.astype(np.float64)).astype(np.float32).astype(ml_dtypes.bfloat16)
    return np.stack([high, low], axis=1)


def halves(x):
    high = x.astype(jnp.bfloat16)
    return high, (x - high.astype(jnp.float32)).astype(jnp.bfloat16)


def dot(a, b):
    return jnp.dot(a, b, preferred_element_type=jnp.float32)


def times_right(x, high, low):
    x_high, x_low = halves(x)
    return dot(x_high, high) + (dot(x_low, high) + dot(x_high, low))


def times_left(high, low, x):
    x_high, x_low = halves(x)
    return dot(high, x_high) + (dot(high, x_low) + dot(low, x_high))


def both_sides(re, im, tables, which):
    n = re.shape[0]
    y = times_right(jnp.concatenate([re, im], axis=1), tables[which ^ 1, 0], tables[which ^ 1, 1])
    y = jnp.concatenate([y[:, :n], y[:, n:]], axis=0)
    z = times_left(tables[which, 0], tables[which, 1], y)
    return z[:n], z[n:]


def share(rows, cols, tile_rows, chips_back):
    count = lax.axis_size("scan")
    base = lax.rem(lax.axis_index("scan") + count - chips_back, count) * tile_rows
    second = rows[1] - base == tile_rows
    a = jnp.where(second, 1, 0)
    return a, cols[a], rows[1 - a] - base, cols[1 - a]


def cut_kernel(rows_own, cols_own, rows_prev, cols_prev, obj, mine, other, halo):
    slab, _, rows, cols = obj.shape
    width = mine.shape[-1]
    on_a = lax.axis_index("depth") == 0
    _, _, row_b, col_b = share(rows_own, cols_own, rows, 0)
    _, col_a, row_p, col_p = share(rows_prev, cols_prev, rows, 1)
    row_mine, col_mine = jnp.where(on_a, 0, row_b), jnp.where(on_a, col_a, col_b)
    row_other, col_other = jnp.where(on_a, row_b, 0), jnp.where(on_a, col_b, col_a)
    corners = ((mine, row_mine, col_mine), (other, row_other, col_other), (halo, row_p, col_p))
    for s in range(slab):
        for p in range(2):
            tile = obj[s, p]
            for out, row, col in corners:
                part = pltpu.roll(tile, lax.rem(cols - col, cols), 1)[:, :width]
                out[s, p] = pltpu.roll(part, lax.rem(rows - row, rows), 0)


def wave_kernel(depth_count, rows_own, cols_own, rows_prev, cols_prev, tables, probe, near, far, *rest):
    own_parts = rest[:depth_count]
    halo_parts = rest[depth_count : 2 * depth_count]
    grads = rest[2 * depth_count : 3 * depth_count]
    probe_grad, layers, waves = rest[3 * depth_count :]
    slab = own_parts[0].shape[0]
    n = probe.shape[-1]
    count = slab * depth_count
    depth = lax.axis_index("depth")
    on_a = depth == 0
    a_own, _, row_b, _ = share(rows_own, cols_own, n, 0)
    a_prev, _, _, _ = share(rows_prev, cols_prev, n, 1)
    measured = jnp.where(on_a, far[a_prev], near[1 - a_own])
    split = jnp.where(on_a, 0, row_b)
    inside = lax.broadcasted_iota(jnp.int32, (n, n), 0) < n - split
    for j in range(depth_count):
        base = lax.rem(depth - j + depth_count, depth_count) * slab
        for s in range(slab):
            layers[base + s] = own_parts[j][s]
    for q in range(depth_count):
        for s in range(slab):
            for p in range(2):
                layers[q * slab + s, p] = jnp.where(inside, layers[q * slab + s, p], halo_parts[q][s, p])

    def enter(s, re, im):
        waves[s, 0] = re
        waves[s, 1] = im
        o_re, o_im = layers[s, 0], layers[s, 1]
        return re * o_re - im * o_im, re * o_im + im * o_re

    def forward(s, wave):
        return both_sides(*enter(s, *wave), tables, 0)

    wave = lax.fori_loop(0, count - 1, forward, (probe[0], probe[1]), unroll=True if count <= 8 else 1)
    far_re, far_im = both_sides(*enter(count - 1, *wave), tables, 2)
    misfit = 2.0 * (far_re * far_re + far_im * far_im - measured)
    chi = both_sides(misfit * far_re, misfit * far_im, tables, 3)

    def leave(s, chi_re, chi_im):
        w_re, w_im = waves[s, 0], waves[s, 1]
        o_re, o_im = layers[s, 0], layers[s, 1]
        waves[s, 0] = w_re * chi_re + w_im * chi_im
        waves[s, 1] = w_re * chi_im - w_im * chi_re
        return o_re * chi_re + o_im * chi_im, o_re * chi_im - o_im * chi_re

    def backward(t, chi):
        return both_sides(*leave(count - 1 - t, *chi), tables, 1)

    chi = lax.fori_loop(0, count - 1, backward, chi, unroll=True if count <= 8 else 1)
    grad = leave(0, *chi)
    for j in range(depth_count):
        base = lax.rem(depth + j, depth_count) * slab
        for s in range(slab):
            grads[j][s] = waves[base + s]
    rows = n // depth_count
    for k in range(depth_count):
        for p in range(2):
            probe_grad[k, p] = jnp.where(depth < 2, grad[p][k * rows : (k + 1) * rows], 0.0)


def place_kernel(depth_count, rows_own, cols_own, rows_prev, cols_prev, *refs):
    *parts, out = refs
    slab, _, rows, cols = out.shape
    width = parts[0].shape[-1]
    depth = lax.axis_index("depth")
    _, _, row_b, col_b = share(rows_own, cols_own, rows, 0)
    _, col_a, row_p, col_p = share(rows_prev, cols_prev, rows, 1)
    row_index = lax.broadcasted_iota(jnp.int32, (rows, width), 0)
    blank = jnp.zeros((rows, cols - width), jnp.float32)
    corners = []
    for j in range(depth_count):
        is_a = depth == j
        is_b = lax.rem(depth + depth_count - 1, depth_count) == j
        row = jnp.where(is_a, 0, row_b)
        last = jnp.where(is_a | is_b, rows, 0)
        corners.append((row, jnp.where(is_a, col_a, col_b), row, last))
    corners.append((row_p, col_p, 0, row_p))
    masks = [(row_index >= first) & (row_index < last) for _, _, first, last in corners]
    for s in range(slab):
        for p in range(2):
            total = None
            for (row, col, _, _), mask, part in zip(corners, masks, parts):
                x = jnp.where(mask, pltpu.roll(part[s, p], lax.rem(row, rows), 0), 0.0)
                x = pltpu.roll(jnp.concatenate([x, blank], axis=1), col, 1)
                total = x if total is None else total + x
            out[s, p] = total


def call(kernel, name, scalars, arrays, outs, scratch=()):
    vmem = pl.BlockSpec(memory_space=pltpu.VMEM)
    moved = sum(math.prod(x.shape) * x.dtype.itemsize for x in (*arrays, *outs))
    return pl.pallas_call(
        kernel,
        name=name,
        out_shape=outs,
        in_specs=[pl.BlockSpec(memory_space=pltpu.SMEM)] * len(scalars) + [vmem] * len(arrays),
        out_specs=[vmem] * len(outs),
        scratch_shapes=scratch,
        compiler_params=pltpu.CompilerParams(vmem_limit_bytes=VMEM_LIMIT),
        cost_estimate=pl.CostEstimate(flops=moved, bytes_accessed=moved, transcendentals=0),
    )(*scalars, *arrays)


def total_over(blocks):
    depth_count, _, rows, n = blocks.shape
    scan_count = lax.axis_size("scan")
    if (2 * rows) % (8 * scan_count) == 0:
        piece = 2 * rows // scan_count
        pieces = blocks.reshape(depth_count * scan_count, piece, n)
        pieces = lax.all_to_all(pieces, ("depth", "scan"), 0, 0, tiled=True)
        summed = jnp.broadcast_to(jnp.sum(pieces, axis=0), (scan_count, piece, n))
        return lax.all_to_all(summed, "scan", 0, 0, tiled=True).reshape(2, rows, n)
    block = lax.psum_scatter(blocks, "depth", scatter_dimension=0)
    if scan_count & (scan_count - 1):
        return lax.psum(block, "scan")
    step = 1
    while step < scan_count:
        block = block + lax.ppermute(block, "scan", [(i, i ^ step) for i in range(scan_count)])
        step *= 2
    return block


def body(objects, probe, row_offsets, col_offsets, intensity):
    slab = objects.shape[0]
    n = probe.shape[-1]
    depth_count, scan_count = lax.axis_size("depth"), lax.axis_size("scan")
    depth = lax.axis_index("depth")
    f32 = jnp.float32

    def across(x, source, target, shift):
        route = [(source * scan_count + i, target * scan_count + (i + shift) % scan_count) for i in range(scan_count)]
        return lax.ppermute(x, ("depth", "scan"), route)

    ahead = [(i, (i + 1) % scan_count) for i in range(scan_count)]
    rows_prev = lax.ppermute(row_offsets, "scan", ahead)
    cols_prev = lax.ppermute(col_offsets, "scan", ahead)
    far = across(intensity, 0, 0, 1)
    offsets = [row_offsets, col_offsets, rows_prev, cols_prev]

    window = jax.ShapeDtypeStruct((slab, 2, n, n), f32)
    mine, other, halo = call(cut_kernel, "cut", offsets, [objects], [window] * 3)

    own = [mine]
    for j in range(1, depth_count):
        target = lax.rem(depth + j, depth_count)
        payload = other if depth_count == 2 else jnp.where((target == 0) | (depth == 0), other, mine)
        route = [((t - j) % depth_count, t) for t in (0, 1)]
        own.append(lax.ppermute(payload, "depth", route))
    halos = [across(halo, q, 1, -1) for q in range(depth_count)]

    tables = jnp.asarray(constant_tables(n))
    *grads, probe_blocks = call(
        lambda *refs: wave_kernel(depth_count, *refs),
        "wave",
        offsets,
        [tables, probe, intensity, far, *own, *halos],
        [window] * depth_count + [jax.ShapeDtypeStruct((depth_count, 2, n // depth_count, n), f32)],
        [pltpu.VMEM((slab * depth_count, 2, n, n), f32)] * 2,
    )
    probe_grad = total_over(probe_blocks)

    back = [grads[0]]
    for j in range(1, depth_count):
        back.append(lax.ppermute(grads[j], "depth", [(t, (t + j) % depth_count) for t in (0, 1)]))
    spill = [across(grads[(q - 1) % depth_count], 1, q, 1) for q in range(depth_count)]
    arrived = spill[0]
    for q in range(1, depth_count):
        arrived = jnp.where(depth == q, spill[q], arrived)
    (object_grad,) = call(
        lambda *refs: place_kernel(depth_count, *refs),
        "place",
        offsets,
        [*back, arrived],
        [jax.ShapeDtypeStruct(objects.shape, f32)],
    )
    return object_grad, probe_grad


def solution(mesh):
    in_specs = (P("depth", None, "scan", None), P(), P("scan"), P("scan"), P("scan", None, None))
    out_specs = (P("depth", None, "scan", None), P(None, "depth", None))
    return jax.shard_map(body, mesh=mesh, in_specs=in_specs, out_specs=out_specs, check_vma=False)
```

```python
import math

import jax
import jax.numpy as jnp
import ml_dtypes
import numpy as np
from jax import lax
from jax.experimental import pallas as pl
from jax.experimental.pallas import tpu as pltpu
from jax.sharding import PartitionSpec as P

PROPAGATION = 0.5
VMEM_LIMIT = 48 * 1024 * 1024


def block_form(matrix):
    return np.block([[matrix.real, -matrix.imag], [matrix.imag, matrix.real]])


def constant_tables(width):
    grid = np.arange(width)
    frequency = np.where(grid < width // 2, grid, grid - width)
    dft = np.exp(-2j * np.pi * ((grid[:, None] * grid[None, :]) % width) / width) / math.sqrt(width)
    chirp = np.exp(-1j * PROPAGATION * np.pi * frequency.astype(np.float64) ** 2 / width)
    step = dft.conj() @ (chirp[:, None] * dft)
    step = 0.5 * (step + step.T)
    full = np.stack([block_form(m) for m in (step, step.conj(), dft, dft.conj())])
    high = full.astype(np.float32).astype(ml_dtypes.bfloat16)
    low = (full - high.astype(np.float64)).astype(np.float32).astype(ml_dtypes.bfloat16)
    return np.stack([high, low], axis=1)


def halves(x):
    high = x.astype(jnp.bfloat16)
    return high, (x - high.astype(jnp.float32)).astype(jnp.bfloat16)


def dot(a, b):
    return jnp.dot(a, b, preferred_element_type=jnp.float32)


def times_right(x, high, low):
    x_high, x_low = halves(x)
    return dot(x_high, high) + (dot(x_low, high) + dot(x_high, low))


def times_left(high, low, x):
    x_high, x_low = halves(x)
    return dot(high, x_high) + (dot(high, x_low) + dot(low, x_high))


def both_sides(re, im, tables, which):
    n = re.shape[0]
    y = times_right(jnp.concatenate([re, im], axis=1), tables[which ^ 1, 0], tables[which ^ 1, 1])
    y = jnp.concatenate([y[:, :n], y[:, n:]], axis=0)
    z = times_left(tables[which, 0], tables[which, 1], y)
    return z[:n], z[n:]


def share(offsets, tile_rows, chips_back):
    count = lax.axis_size("scan")
    base = lax.rem(lax.axis_index("scan") + count - chips_back, count) * tile_rows
    second = offsets[1] - base == tile_rows
    a = jnp.where(second, 1, 0)
    return a, offsets[2 + a], offsets[1 - a] - base, offsets[3 - a]


def cut(tile, row, col, width):
    rows, cols = tile.shape
    part = pltpu.roll(tile, lax.rem(cols - col, cols), 1)[:, :width]
    return pltpu.roll(part, lax.rem(rows - row, rows), 0)


def cut_kernel(offsets, offsets_prev, obj, mine, other):
    slab, _, rows, cols = obj.shape
    width = mine.shape[-1]
    on_a = lax.axis_index("depth") == 0
    _, _, row_b, col_b = share(offsets, rows, 0)
    _, col_a, _, _ = share(offsets_prev, rows, 1)
    row_mine, col_mine = jnp.where(on_a, 0, row_b), jnp.where(on_a, col_a, col_b)
    row_other, col_other = jnp.where(on_a, row_b, 0), jnp.where(on_a, col_b, col_a)
    for s in range(slab):
        for p in range(2):
            mine[s, p] = cut(obj[s, p], row_mine, col_mine, width)
            other[s, p] = cut(obj[s, p], row_other, col_other, width)


def wave_kernel(depth_count, offsets, offsets_prev, tables, probe, near, far, *rest):
    own_parts = rest[:depth_count]
    halo_parts = rest[depth_count : 2 * depth_count]
    grads = rest[2 * depth_count : 3 * depth_count]
    probe_parts = rest[3 * depth_count : 4 * depth_count]
    layers, waves = rest[4 * depth_count :]
    slab = own_parts[0].shape[0]
    n = probe.shape[-1]
    count = slab * depth_count
    depth = lax.axis_index("depth")
    on_a = depth == 0
    a_own, _, row_b, col_b = share(offsets, n, 0)
    a_prev, _, _, _ = share(offsets_prev, n, 1)
    measured = jnp.where(on_a, far[a_prev], near[1 - a_own])
    split = jnp.where(on_a, 0, row_b)
    inside = lax.broadcasted_iota(jnp.int32, (n, n), 0) < n - split
    for j in range(depth_count):
        base = lax.rem(depth - j + depth_count, depth_count) * slab
        for s in range(slab):
            layers[base + s] = own_parts[j][s]
    for q in range(depth_count):
        for s in range(slab):
            for p in range(2):
                below = cut(halo_parts[q][s, p], row_b, col_b, n)
                layers[q * slab + s, p] = jnp.where(inside, layers[q * slab + s, p], below)

    def enter(s, re, im):
        waves[s, 0] = re
        waves[s, 1] = im
        o_re, o_im = layers[s, 0], layers[s, 1]
        return re * o_re - im * o_im, re * o_im + im * o_re

    def forward(s, wave):
        return both_sides(*enter(s, *wave), tables, 0)

    wave = lax.fori_loop(0, count - 1, forward, (probe[0], probe[1]), unroll=True if count <= 8 else 1)
    far_re, far_im = both_sides(*enter(count - 1, *wave), tables, 2)
    misfit = 2.0 * (far_re * far_re + far_im * far_im - measured)
    chi = both_sides(misfit * far_re, misfit * far_im, tables, 3)

    def leave(s, chi_re, chi_im):
        w_re, w_im = waves[s, 0], waves[s, 1]
        o_re, o_im = layers[s, 0], layers[s, 1]
        waves[s, 0] = w_re * chi_re + w_im * chi_im
        waves[s, 1] = w_re * chi_im - w_im * chi_re
        return o_re * chi_re + o_im * chi_im, o_re * chi_im - o_im * chi_re

    def backward(t, chi):
        return both_sides(*leave(count - 1 - t, *chi), tables, 1)

    chi = lax.fori_loop(0, count - 1, backward, chi, unroll=True if count <= 8 else 1)
    grad = leave(0, *chi)
    for j in range(depth_count):
        base = lax.rem(depth + j, depth_count) * slab
        for s in range(slab):
            grads[j][s] = waves[base + s]
    rows = n // depth_count
    waves[0, 0] = jnp.where(depth < 2, grad[0], 0.0)
    waves[0, 1] = jnp.where(depth < 2, grad[1], 0.0)
    for j in range(depth_count):
        start = pl.multiple_of(lax.rem(depth + j, depth_count) * rows, rows)
        for p in range(2):
            probe_parts[j][p] = waves[0, p, pl.ds(start, rows), :]


def place_kernel(depth_count, offsets, offsets_prev, *refs):
    parts, spills, out = refs[:depth_count], refs[depth_count:-1], refs[-1]
    slab, _, rows, cols = out.shape
    width = parts[0].shape[-1]
    depth = lax.axis_index("depth")
    _, _, row_b, col_b = share(offsets, rows, 0)
    _, col_a, row_p, col_p = share(offsets_prev, rows, 1)
    row_index = lax.broadcasted_iota(jnp.int32, (rows, width), 0)
    blank = jnp.zeros((rows, cols - width), jnp.float32)
    corners = []
    for j in range(depth_count):
        is_a = depth == j
        is_b = lax.rem(depth + depth_count - 1, depth_count) == j
        row = jnp.where(is_a, 0, row_b)
        last = jnp.where(is_a | is_b, rows, 0)
        corners.append((row, jnp.where(is_a, col_a, col_b), row, last))
    masks = [(row_index >= first) & (row_index < last) for _, _, first, last in corners]

    def placed(x, row, col, mask):
        x = jnp.where(mask, pltpu.roll(x, lax.rem(row, rows), 0), 0.0)
        return pltpu.roll(jnp.concatenate([x, blank], axis=1), col, 1)

    for s in range(slab):
        for p in range(2):
            x = spills[0][s, p]
            for q in range(1, depth_count):
                x = jnp.where(depth == q, spills[q][s, p], x)
            total = placed(x, row_p, col_p, row_index < row_p)
            for (row, col, _, _), mask, part in zip(corners, masks, parts):
                total = total + placed(part[s, p], row, col, mask)
            out[s, p] = total


def call(kernel, name, scalars, arrays, outs, scratch=()):
    vmem = pl.BlockSpec(memory_space=pltpu.VMEM)
    moved = sum(math.prod(x.shape) * x.dtype.itemsize for x in (*arrays, *outs))
    return pl.pallas_call(
        kernel,
        name=name,
        out_shape=outs,
        in_specs=[pl.BlockSpec(memory_space=pltpu.SMEM)] * len(scalars) + [vmem] * len(arrays),
        out_specs=[vmem] * len(outs),
        scratch_shapes=scratch,
        compiler_params=pltpu.CompilerParams(vmem_limit_bytes=VMEM_LIMIT),
        cost_estimate=pl.CostEstimate(flops=moved, bytes_accessed=moved, transcendentals=0),
    )(*scalars, *arrays)


def total_over_scan(x):
    count = lax.axis_size("scan")
    if count & (count - 1):
        return lax.psum(x, "scan")
    step = 1
    while step < count:
        x = x + lax.ppermute(x, "scan", [(i, i ^ step) for i in range(count)])
        step *= 2
    return x


def body(objects, probe, row_offsets, col_offsets, intensity):
    slab = objects.shape[0]
    n = probe.shape[-1]
    depth_count, scan_count = lax.axis_size("depth"), lax.axis_size("scan")
    depth = lax.axis_index("depth")
    f32 = jnp.float32

    def across(x, source, target, shift):
        route = [(source * scan_count + i, target * scan_count + (i + shift) % scan_count) for i in range(scan_count)]
        return lax.ppermute(x, ("depth", "scan"), route)

    halos = [across(objects, q, 1, -1) for q in range(depth_count)]
    offsets = jnp.concatenate([row_offsets, col_offsets])
    offsets_prev = lax.ppermute(offsets, "scan", [(i, (i + 1) % scan_count) for i in range(scan_count)])
    far = across(intensity, 0, 0, 1)
    offsets = [offsets, offsets_prev]

    window = jax.ShapeDtypeStruct((slab, 2, n, n), f32)
    mine, other = call(cut_kernel, "cut", offsets, [objects], [window] * 2)

    own = [mine]
    for j in range(1, depth_count):
        target = lax.rem(depth + j, depth_count)
        payload = other if depth_count == 2 else jnp.where((target == 0) | (depth == 0), other, mine)
        route = [((t - j) % depth_count, t) for t in (0, 1)]
        own.append(lax.ppermute(payload, "depth", route))

    tables = jnp.asarray(constant_tables(n))
    parts = call(
        lambda *refs: wave_kernel(depth_count, *refs),
        "wave",
        offsets,
        [tables, probe, intensity, far, *own, *halos],
        [window] * depth_count + [jax.ShapeDtypeStruct((2, n // depth_count, n), f32)] * depth_count,
        [pltpu.VMEM((slab * depth_count, 2, n, n), f32)] * 2,
    )
    grads, probe_parts = parts[:depth_count], parts[depth_count:]

    back = [grads[0]]
    probe_grad = probe_parts[0]
    for j in range(1, depth_count):
        back.append(lax.ppermute(grads[j], "depth", [(t, (t + j) % depth_count) for t in (0, 1)]))
        probe_grad = probe_grad + lax.ppermute(
            probe_parts[j], "depth", [(t, (t + j) % depth_count) for t in range(depth_count)]
        )
    probe_grad = total_over_scan(probe_grad)
    spill = [across(grads[(q - 1) % depth_count], 1, q, 1) for q in range(depth_count)]
    (object_grad,) = call(
        lambda *refs: place_kernel(depth_count, *refs),
        "place",
        offsets,
        [*back, *spill],
        [jax.ShapeDtypeStruct(objects.shape, f32)],
    )
    return object_grad, probe_grad


def solution(mesh):
    in_specs = (P("depth", None, "scan", None), P(), P("scan"), P("scan"), P("scan", None, None))
    out_specs = (P("depth", None, "scan", None), P(None, "depth", None))
    return jax.shard_map(body, mesh=mesh, in_specs=in_specs, out_specs=out_specs, check_vma=False)
```

```python
import math

import jax
import jax.numpy as jnp
import ml_dtypes
import numpy as np
from jax import lax
from jax.experimental import pallas as pl
from jax.experimental.pallas import tpu as pltpu
from jax.sharding import PartitionSpec as P

PROPAGATION = 0.5
VMEM_LIMIT = 48 * 1024 * 1024


def block_form(matrix):
    return np.block([[matrix.real, -matrix.imag], [matrix.imag, matrix.real]])


def constant_tables(width):
    grid = np.arange(width)
    frequency = np.where(grid < width // 2, grid, grid - width)
    dft = np.exp(-2j * np.pi * ((grid[:, None] * grid[None, :]) % width) / width) / math.sqrt(width)
    chirp = np.exp(-1j * PROPAGATION * np.pi * frequency.astype(np.float64) ** 2 / width)
    step = dft.conj() @ (chirp[:, None] * dft)
    step = 0.5 * (step + step.T)
    full = np.stack([block_form(m) for m in (step, step.conj(), dft, dft.conj())])
    high = full.astype(np.float32).astype(ml_dtypes.bfloat16)
    low = (full - high.astype(np.float64)).astype(np.float32).astype(ml_dtypes.bfloat16)
    return np.stack([high, low], axis=1)


def halves(x):
    high = x.astype(jnp.bfloat16)
    return high, (x - high.astype(jnp.float32)).astype(jnp.bfloat16)


def dot(a, b):
    return jnp.dot(a, b, preferred_element_type=jnp.float32)


def times_right(x, high, low):
    x_high, x_low = halves(x)
    return dot(x_high, high) + (dot(x_low, high) + dot(x_high, low))


def times_left(high, low, x):
    x_high, x_low = halves(x)
    return dot(high, x_high) + (dot(high, x_low) + dot(low, x_high))


def both_sides(re, im, tables, which):
    n = re.shape[0]
    y = times_right(jnp.concatenate([re, im], axis=1), tables[which ^ 1, 0], tables[which ^ 1, 1])
    y = jnp.concatenate([y[:, :n], y[:, n:]], axis=0)
    z = times_left(tables[which, 0], tables[which, 1], y)
    return z[:n], z[n:]


def share(offsets, tile_rows, chips_back):
    count = lax.axis_size("scan")
    base = lax.rem(lax.axis_index("scan") + count - chips_back, count) * tile_rows
    second = offsets[1] - base == tile_rows
    a = jnp.where(second, 1, 0)
    return a, offsets[2 + a], offsets[1 - a] - base, offsets[3 - a]


def cut(tile, row, col, width):
    rows, cols = tile.shape
    part = pltpu.roll(tile, lax.rem(cols - col, cols), 1)[:, :width]
    return pltpu.roll(part, lax.rem(rows - row, rows), 0)


def own_kernel(offsets, objects, intensity, probe, tiles, window_b, measured_b, measured_a, start):
    slab, _, rows, _ = objects.shape
    a, _, row_b, col_b = share(offsets, rows, 0)
    measured_a[...] = intensity[a]
    measured_b[...] = intensity[1 - a]
    start[...] = probe[...]
    for s in range(slab):
        for p in range(2):
            tile = objects[s, p]
            tiles[s, p] = tile
            window_b[s, p] = cut(tile, row_b, col_b, window_b.shape[-1])


def prev_kernel(offsets_prev, tiles, window_b, window_a, halo, other):
    slab, _, rows, _ = tiles.shape
    width = halo.shape[-1]
    _, col_a, row_p, col_p = share(offsets_prev, rows, 1)
    on_a = lax.axis_index("depth") == 0
    for s in range(slab):
        for p in range(2):
            halo[s, p] = cut(tiles[s, p], row_p, col_p, width)
            window = cut(tiles[s, p], 0, col_a, width)
            window_a[s, p] = window
            other[s, p] = jnp.where(on_a, window_b[s, p], window)


def wave_kernel(depth_count, offsets, tables, probe, near, far, window_a, window_b, *rest):
    others, rest = rest[: depth_count - 1], rest[depth_count - 1 :]
    halos, rest = rest[:depth_count], rest[depth_count:]
    grads, probe_parts = rest[:depth_count], rest[depth_count : 2 * depth_count]
    layers, waves = rest[2 * depth_count :]
    slab = window_a.shape[0]
    n = probe.shape[-1]
    count = slab * depth_count
    depth = lax.axis_index("depth")
    on_a = depth == 0
    _, _, row_b, _ = share(offsets, n, 0)
    split = jnp.where(on_a, 0, row_b)
    inside = lax.broadcasted_iota(jnp.int32, (n, n), 0) < n - split
    for s in range(slab):
        for p in range(2):
            layers[depth * slab + s, p] = jnp.where(on_a, window_a[s, p], window_b[s, p])
    for j in range(1, depth_count):
        base = lax.rem(depth - j + depth_count, depth_count) * slab
        for s in range(slab):
            layers[base + s] = others[j - 1][s]
    for q in range(depth_count):
        for s in range(slab):
            for p in range(2):
                layers[q * slab + s, p] = jnp.where(inside, layers[q * slab + s, p], halos[q][s, p])

    def enter(s, re, im):
        waves[s, 0] = re
        waves[s, 1] = im
        o_re, o_im = layers[s, 0], layers[s, 1]
        return re * o_re - im * o_im, re * o_im + im * o_re

    def forward(s, wave):
        return both_sides(*enter(s, *wave), tables, 0)

    wave = lax.fori_loop(0, count - 1, forward, (probe[0], probe[1]), unroll=True if count <= 8 else 1)
    far_re, far_im = both_sides(*enter(count - 1, *wave), tables, 2)
    measured = jnp.where(on_a, far[...], near[...])
    misfit = 2.0 * (far_re * far_re + far_im * far_im - measured)
    chi = both_sides(misfit * far_re, misfit * far_im, tables, 3)

    def leave(s, chi_re, chi_im):
        w_re, w_im = waves[s, 0], waves[s, 1]
        o_re, o_im = layers[s, 0], layers[s, 1]
        waves[s, 0] = w_re * chi_re + w_im * chi_im
        waves[s, 1] = w_re * chi_im - w_im * chi_re
        return o_re * chi_re + o_im * chi_im, o_re * chi_im - o_im * chi_re

    def backward(t, chi):
        return both_sides(*leave(count - 1 - t, *chi), tables, 1)

    chi = lax.fori_loop(0, count - 1, backward, chi, unroll=True if count <= 8 else 1)
    grad = leave(0, *chi)
    for j in range(depth_count):
        base = lax.rem(depth + j, depth_count) * slab
        for s in range(slab):
            grads[j][s] = waves[base + s]
    rows = n // depth_count
    waves[0, 0] = jnp.where(depth < 2, grad[0], 0.0)
    waves[0, 1] = jnp.where(depth < 2, grad[1], 0.0)
    for j in range(depth_count):
        start = pl.multiple_of(lax.rem(depth + j, depth_count) * rows, rows)
        for p in range(2):
            probe_parts[j][p] = waves[0, p, pl.ds(start, rows), :]


def placed(x, row, col, mask, cols):
    x = jnp.where(mask, pltpu.roll(x, lax.rem(row, x.shape[0]), 0), 0.0)
    blank = jnp.zeros((x.shape[0], cols - x.shape[1]), x.dtype)
    return pltpu.roll(jnp.concatenate([x, blank], axis=1), col, 1)


def place_kernel(depth_count, offsets, offsets_prev, *refs):
    *parts, out = refs
    slab, _, rows, cols = out.shape
    depth = lax.axis_index("depth")
    _, _, row_b, col_b = share(offsets, rows, 0)
    _, col_a, _, _ = share(offsets_prev, rows, 1)
    row_index = lax.broadcasted_iota(jnp.int32, (rows, parts[0].shape[-1]), 0)
    corners = []
    for j in range(depth_count):
        is_a = depth == j
        is_b = lax.rem(depth + depth_count - 1, depth_count) == j
        row = jnp.where(is_a, 0, row_b)
        last = jnp.where(is_a | is_b, rows, 0)
        corners.append((row, jnp.where(is_a, col_a, col_b), (row_index >= row) & (row_index < last)))
    for s in range(slab):
        for p in range(2):
            total = None
            for (row, col, mask), part in zip(corners, parts):
                x = placed(part[s, p], row, col, mask, cols)
                total = x if total is None else total + x
            out[s, p] = total


def spill_kernel(depth_count, offsets_prev, *refs):
    before, *spills, out = refs
    slab, _, rows, cols = out.shape
    depth = lax.axis_index("depth")
    _, _, row_p, col_p = share(offsets_prev, rows, 1)
    mask = lax.broadcasted_iota(jnp.int32, (rows, spills[0].shape[-1]), 0) < row_p
    for s in range(slab):
        for p in range(2):
            x = spills[0][s, p]
            for q in range(1, depth_count):
                x = jnp.where(depth == q, spills[q][s, p], x)
            out[s, p] = before[s, p] + placed(x, row_p, col_p, mask, cols)


def add_kernel(count, *refs):
    a, b = refs[:2]
    refs[2 + count][...] = a[...] + b[...]


def add_then(a, b, later):
    vmem, anywhere = pl.BlockSpec(memory_space=pltpu.VMEM), pl.BlockSpec(memory_space=pl.ANY)
    out = pl.pallas_call(
        lambda *refs: add_kernel(len(later), *refs),
        name="add_then",
        out_shape=[jax.ShapeDtypeStruct(x.shape, x.dtype) for x in (a, *later)],
        in_specs=[vmem] * 2 + [anywhere] * len(later),
        out_specs=[vmem] + [anywhere] * len(later),
        input_output_aliases={2 + i: 1 + i for i in range(len(later))},
    )(a, b, *later)
    return out[0], out[1:]


def call(kernel, name, scalars, arrays, outs, scratch=(), work=10**9):
    vmem = pl.BlockSpec(memory_space=pltpu.VMEM)
    moved = sum(math.prod(x.shape) * x.dtype.itemsize for x in (*arrays, *outs))
    return pl.pallas_call(
        kernel,
        name=name,
        out_shape=outs,
        in_specs=[pl.BlockSpec(memory_space=pltpu.SMEM)] * len(scalars) + [vmem] * len(arrays),
        out_specs=[vmem] * len(outs),
        scratch_shapes=scratch,
        compiler_params=pltpu.CompilerParams(vmem_limit_bytes=VMEM_LIMIT),
        cost_estimate=pl.CostEstimate(flops=work, bytes_accessed=moved, transcendentals=0),
    )(*scalars, *arrays)


def sum_round(x, level):
    depth_count, scan_count = lax.axis_size("depth"), lax.axis_size("scan")
    levels = scan_count.bit_length() - 1
    route = []
    for d in range(depth_count):
        step = 1 << ((level + (d % 2) * (levels // 2)) % levels)
        route += [(d * scan_count + i, d * scan_count + (i ^ step)) for i in range(scan_count)]
    return lax.ppermute(x, ("depth", "scan"), route)


def body(objects, probe, row_offsets, col_offsets, intensity):
    slab = objects.shape[0]
    n = probe.shape[-1]
    depth_count, scan_count = lax.axis_size("depth"), lax.axis_size("scan")
    depth = lax.axis_index("depth")
    f32 = jnp.float32

    def across(x, source, target, shift):
        route = [(source * scan_count + i, target * scan_count + (i + shift) % scan_count) for i in range(scan_count)]
        return lax.ppermute(x, ("depth", "scan"), route)

    offsets = jnp.concatenate([row_offsets, col_offsets])
    offsets_prev = lax.ppermute(offsets, "scan", [(i, (i + 1) % scan_count) for i in range(scan_count)])
    window = jax.ShapeDtypeStruct((slab, 2, n, n), f32)
    plane = jax.ShapeDtypeStruct((n, n), f32)
    whole = jax.ShapeDtypeStruct(objects.shape, f32)
    tiles, window_b, near, passed, start = call(
        own_kernel,
        "own",
        [offsets],
        [objects, intensity, probe],
        [whole, window, plane, plane, jax.ShapeDtypeStruct(probe.shape, f32)],
    )
    far = across(passed, 0, 0, 1)
    window_a, halo, other = call(prev_kernel, "prev", [offsets_prev], [tiles, window_b], [window] * 3)
    halos = [across(halo, q, 1, -1) for q in range(depth_count)]

    others = []
    for j in range(1, depth_count):
        target = lax.rem(depth + j, depth_count)
        payload = other if depth_count == 2 else jnp.where(target == 0, window_a, window_b)
        route = [((t - j) % depth_count, t) for t in (0, 1)]
        others.append(lax.ppermute(payload, "depth", route))

    tables = jnp.asarray(constant_tables(n))
    count = slab * depth_count
    parts = call(
        lambda *refs: wave_kernel(depth_count, *refs),
        "wave",
        [offsets],
        [tables, start, near, far, window_a, window_b, *others, *halos],
        [window] * depth_count + [jax.ShapeDtypeStruct((2, n // depth_count, n), f32)] * depth_count,
        [pltpu.VMEM((count, 2, n, n), f32)] * 2,
        work=5 * 10**9,
    )
    grads, probe_parts = parts[:depth_count], parts[depth_count:]

    probe_grad = probe_parts[0]
    for j in range(1, depth_count):
        probe_grad = probe_grad + lax.ppermute(
            probe_parts[j], "depth", [(t, (t + j) % depth_count) for t in range(depth_count)]
        )
    rounds = scan_count.bit_length() - 1
    paired = scan_count == 1 << rounds and rounds > 2
    if paired:
        probe_grad, grads = add_then(probe_grad, sum_round(probe_grad, 0), grads)
        for level in range(1, rounds - 2):
            probe_grad = probe_grad + sum_round(probe_grad, level)
    else:
        probe_grad = lax.psum(probe_grad, "scan")

    spill = [across(grads[(q - 1) % depth_count], 1, q, 1) for q in range(depth_count)]
    back = [grads[0]]
    for j in range(1, depth_count):
        back.append(lax.ppermute(grads[j], "depth", [(t, (t + j) % depth_count) for t in (0, 1)]))
    (object_grad,) = call(
        lambda *refs: place_kernel(depth_count, *refs), "place", [offsets, offsets_prev], back, [whole], work=2 * 10**9
    )
    if paired:
        probe_grad, (object_grad,) = add_then(probe_grad, sum_round(probe_grad, rounds - 2), [object_grad])
        last = sum_round(probe_grad, rounds - 1)
    (object_grad,) = call(
        lambda *refs: spill_kernel(depth_count, *refs), "spill", [offsets_prev], [object_grad, *spill], [whole]
    )
    if paired:
        probe_grad, (object_grad,) = add_then(probe_grad, last, [object_grad])
    return object_grad, probe_grad


def solution(mesh):
    in_specs = (P("depth", None, "scan", None), P(), P("scan"), P("scan"), P("scan", None, None))
    out_specs = (P("depth", None, "scan", None), P(None, "depth", None))
    return jax.shard_map(body, mesh=mesh, in_specs=in_specs, out_specs=out_specs, check_vma=False)
```

```python
import math

import jax
import jax.numpy as jnp
import ml_dtypes
import numpy as np
from jax import lax
from jax.experimental import pallas as pl
from jax.experimental.pallas import tpu as pltpu
from jax.sharding import PartitionSpec as P

PROPAGATION = 0.5
VMEM_LIMIT = 48 * 1024 * 1024


def block_form(matrix):
    return np.block([[matrix.real, -matrix.imag], [matrix.imag, matrix.real]])


def constant_tables(width):
    grid = np.arange(width)
    frequency = np.where(grid < width // 2, grid, grid - width)
    dft = np.exp(-2j * np.pi * ((grid[:, None] * grid[None, :]) % width) / width) / math.sqrt(width)
    chirp = np.exp(-1j * PROPAGATION * np.pi * frequency.astype(np.float64) ** 2 / width)
    step = dft.conj() @ (chirp[:, None] * dft)
    step = 0.5 * (step + step.T)
    full = np.stack([block_form(m) for m in (step, step.conj(), dft, dft.conj())])
    high = full.astype(np.float32).astype(ml_dtypes.bfloat16)
    low = (full - high.astype(np.float64)).astype(np.float32).astype(ml_dtypes.bfloat16)
    return np.stack([high, low], axis=1)


def halves(x):
    high = x.astype(jnp.bfloat16)
    return high, (x - high.astype(jnp.float32)).astype(jnp.bfloat16)


def dot(a, b):
    return jnp.dot(a, b, preferred_element_type=jnp.float32)


def times_right(x, high, low):
    x_high, x_low = halves(x)
    return dot(x_high, high) + (dot(x_low, high) + dot(x_high, low))


def times_left(high, low, x):
    x_high, x_low = halves(x)
    return dot(high, x_high) + (dot(high, x_low) + dot(low, x_high))


def both_sides(re, im, tables, which):
    n = re.shape[0]
    y = times_right(jnp.concatenate([re, im], axis=1), tables[which ^ 1, 0], tables[which ^ 1, 1])
    y = jnp.concatenate([y[:, :n], y[:, n:]], axis=0)
    z = times_left(tables[which, 0], tables[which, 1], y)
    return z[:n], z[n:]


def share(offsets, tile_rows, chips_back):
    count = lax.axis_size("scan")
    base = lax.rem(lax.axis_index("scan") + count - chips_back, count) * tile_rows
    second = offsets[1] - base == tile_rows
    a = jnp.where(second, 1, 0)
    return a, offsets[2 + a], offsets[1 - a] - base, offsets[3 - a]


def cut(tile, row, col, width):
    rows, cols = tile.shape
    part = pltpu.roll(tile, lax.rem(cols - col, cols), 1)[:, :width]
    return pltpu.roll(part, lax.rem(rows - row, rows), 0)


def own_kernel(offsets, objects, tiles, window_b):
    slab, _, rows, _ = objects.shape
    _, _, row_b, col_b = share(offsets, rows, 0)
    for s in range(slab):
        for p in range(2):
            tile = objects[s, p]
            tiles[s, p] = tile
            window_b[s, p] = cut(tile, row_b, col_b, window_b.shape[-1])


def prev_kernel(offsets_prev, after, tiles, window_b, window_a, halo, other):
    slab, _, rows, _ = tiles.shape
    width = halo.shape[-1]
    _, col_a, row_p, col_p = share(offsets_prev, rows, 1)
    on_a = lax.axis_index("depth") == 0
    for s in range(slab):
        for p in range(2):
            halo[s, p] = cut(tiles[s, p], row_p, col_p, width)
            window = cut(tiles[s, p], 0, col_a, width)
            window_a[s, p] = window
            other[s, p] = jnp.where(on_a, window_b[s, p], window)


def load_kernel(offsets, offsets_prev, intensity, far, probe, measured, start):
    rows = probe.shape[-1]
    near_a, _, _, _ = share(offsets, rows, 0)
    far_a, _, _, _ = share(offsets_prev, rows, 1)
    measured[...] = jnp.where(lax.axis_index("depth") == 0, far[far_a], intensity[1 - near_a])
    start[...] = probe[...]


def wave_kernel(depth_count, offsets, tables, probe, measured, window_a, window_b, *rest):
    others, rest = rest[: depth_count - 1], rest[depth_count - 1 :]
    halos, rest = rest[:depth_count], rest[depth_count:]
    grads, probe_parts = rest[:depth_count], rest[depth_count : 2 * depth_count]
    layers, waves = rest[2 * depth_count :]
    slab = window_a.shape[0]
    n = probe.shape[-1]
    count = slab * depth_count
    depth = lax.axis_index("depth")
    on_a = depth == 0
    _, _, row_b, _ = share(offsets, n, 0)
    split = jnp.where(on_a, 0, row_b)
    inside = lax.broadcasted_iota(jnp.int32, (n, n), 0) < n - split
    for s in range(slab):
        for p in range(2):
            layers[depth * slab + s, p] = jnp.where(on_a, window_a[s, p], window_b[s, p])
    for j in range(1, depth_count):
        base = lax.rem(depth - j + depth_count, depth_count) * slab
        for s in range(slab):
            layers[base + s] = others[j - 1][s]
    for q in range(depth_count):
        for s in range(slab):
            for p in range(2):
                layers[q * slab + s, p] = jnp.where(inside, layers[q * slab + s, p], halos[q][s, p])

    def enter(s, re, im):
        waves[s, 0] = re
        waves[s, 1] = im
        o_re, o_im = layers[s, 0], layers[s, 1]
        return re * o_re - im * o_im, re * o_im + im * o_re

    def forward(s, wave):
        return both_sides(*enter(s, *wave), tables, 0)

    wave = lax.fori_loop(0, count - 1, forward, (probe[0], probe[1]), unroll=True if count <= 8 else 1)
    far_re, far_im = both_sides(*enter(count - 1, *wave), tables, 2)
    misfit = 2.0 * (far_re * far_re + far_im * far_im - measured[...])
    chi = both_sides(misfit * far_re, misfit * far_im, tables, 3)

    def leave(s, chi_re, chi_im):
        w_re, w_im = waves[s, 0], waves[s, 1]
        o_re, o_im = layers[s, 0], layers[s, 1]
        waves[s, 0] = w_re * chi_re + w_im * chi_im
        waves[s, 1] = w_re * chi_im - w_im * chi_re
        return o_re * chi_re + o_im * chi_im, o_re * chi_im - o_im * chi_re

    def backward(t, chi):
        return both_sides(*leave(count - 1 - t, *chi), tables, 1)

    chi = lax.fori_loop(0, count - 1, backward, chi, unroll=True if count <= 8 else 1)
    grad = leave(0, *chi)
    for j in range(depth_count):
        base = lax.rem(depth + j, depth_count) * slab
        for s in range(slab):
            grads[j][s] = waves[base + s]
    rows = n // depth_count
    waves[0, 0] = jnp.where(depth < 2, grad[0], 0.0)
    waves[0, 1] = jnp.where(depth < 2, grad[1], 0.0)
    for j in range(depth_count):
        start = pl.multiple_of(lax.rem(depth + j, depth_count) * rows, rows)
        for p in range(2):
            probe_parts[j][p] = waves[0, p, pl.ds(start, rows), :]


def turn_kernel(offsets, after, *refs):
    on_a = lax.axis_index("depth") == 0
    count = len(refs) // 2
    for x, out in zip(refs[:count], refs[count:]):
        slab, _, rows, _ = x.shape
        _, _, row_b, _ = share(offsets, rows, 0)
        shift = lax.rem(jnp.where(on_a, 0, row_b), rows)
        for s in range(slab):
            for p in range(2):
                out[s, p] = pltpu.roll(x[s, p], shift, 0)


def placed(x, col, mask, cols):
    blank = jnp.zeros((x.shape[0], cols - x.shape[1]), x.dtype)
    return pltpu.roll(jnp.concatenate([jnp.where(mask, x, 0.0), blank], axis=1), col, 1)


def place_kernel(depth_count, offsets, offsets_prev, *refs):
    *parts, out, token = refs
    slab, _, rows, cols = out.shape
    depth = lax.axis_index("depth")
    _, _, row_b, col_b = share(offsets, rows, 0)
    _, col_a, _, _ = share(offsets_prev, rows, 1)
    row_index = lax.broadcasted_iota(jnp.int32, (rows, parts[0].shape[-1]), 0)
    corners = []
    for j in range(depth_count):
        is_a = depth == j
        is_b = lax.rem(depth + depth_count - 1, depth_count) == j
        first = jnp.where(is_a, 0, row_b)
        last = jnp.where(is_a | is_b, rows, 0)
        corners.append((jnp.where(is_a, col_a, col_b), (row_index >= first) & (row_index < last)))
    for s in range(slab):
        for p in range(2):
            total = None
            for (col, mask), part in zip(corners, parts):
                x = placed(part[s, p], col, mask, cols)
                total = x if total is None else total + x
            out[s, p] = total
    token[...] = jnp.zeros_like(token)


def spill_kernel(depth_count, offsets_prev, *refs):
    before, *spills, out, token = refs
    slab, _, rows, cols = out.shape
    depth = lax.axis_index("depth")
    _, _, row_p, col_p = share(offsets_prev, rows, 1)
    mask = lax.broadcasted_iota(jnp.int32, (rows, spills[0].shape[-1]), 0) < row_p
    for s in range(slab):
        for p in range(2):
            x = spills[0][s, p]
            for q in range(1, depth_count):
                x = jnp.where(depth == q, spills[q][s, p], x)
            out[s, p] = before[s, p] + placed(x, col_p, mask, cols)
    token[...] = jnp.zeros_like(token)


def call(kernel, name, scalars, arrays, outs, scratch=(), work=10**9, after=()):
    vmem = pl.BlockSpec(memory_space=pltpu.VMEM)
    moved = sum(math.prod(x.shape) * x.dtype.itemsize for x in (*arrays, *outs))
    return pl.pallas_call(
        kernel,
        name=name,
        out_shape=outs,
        in_specs=[pl.BlockSpec(memory_space=pltpu.SMEM)] * len(scalars)
        + [pl.BlockSpec(memory_space=pl.ANY)] * len(after)
        + [vmem] * len(arrays),
        out_specs=[vmem] * len(outs),
        scratch_shapes=scratch,
        compiler_params=pltpu.CompilerParams(vmem_limit_bytes=VMEM_LIMIT),
        cost_estimate=pl.CostEstimate(flops=work, bytes_accessed=moved, transcendentals=0),
    )(*scalars, *after, *arrays)


def sum_round(x, level):
    depth_count, scan_count = lax.axis_size("depth"), lax.axis_size("scan")
    levels = scan_count.bit_length() - 1
    route = []
    for d in range(depth_count):
        step = 1 << ((level + (d % 2) * (levels // 2)) % levels)
        route += [(d * scan_count + i, d * scan_count + (i ^ step)) for i in range(scan_count)]
    return lax.ppermute(x, ("depth", "scan"), route)


def body(objects, probe, row_offsets, col_offsets, intensity):
    slab = objects.shape[0]
    n = probe.shape[-1]
    depth_count, scan_count = lax.axis_size("depth"), lax.axis_size("scan")
    depth = lax.axis_index("depth")
    f32 = jnp.float32

    def across(x, source, target, shift):
        route = [(source * scan_count + i, target * scan_count + (i + shift) % scan_count) for i in range(scan_count)]
        return lax.ppermute(x, ("depth", "scan"), route)

    offsets = jnp.concatenate([row_offsets, col_offsets])
    offsets_prev = lax.ppermute(offsets, "scan", [(i, (i + 1) % scan_count) for i in range(scan_count)])
    far = across(intensity, 0, 0, 1)
    window = jax.ShapeDtypeStruct((slab, 2, n, n), f32)
    whole = jax.ShapeDtypeStruct(objects.shape, f32)
    token = jax.ShapeDtypeStruct((8, n), f32)
    tiles, window_b = call(own_kernel, "own", [offsets], [objects], [whole, window])
    window_a, halo, other = call(prev_kernel, "prev", [offsets_prev], [tiles, window_b], [window] * 3, after=[far])
    halos = [across(halo, q, 1, -1) for q in range(depth_count)]
    measured, start = call(
        load_kernel,
        "load",
        [offsets, offsets_prev],
        [intensity, far, probe],
        [jax.ShapeDtypeStruct((n, n), f32), jax.ShapeDtypeStruct(probe.shape, f32)],
    )

    others = []
    for j in range(1, depth_count):
        target = lax.rem(depth + j, depth_count)
        payload = other if depth_count == 2 else jnp.where(target == 0, window_a, window_b)
        route = [((t - j) % depth_count, t) for t in (0, 1)]
        others.append(lax.ppermute(payload, "depth", route))

    tables = jnp.asarray(constant_tables(n))
    count = slab * depth_count
    parts = call(
        lambda *refs: wave_kernel(depth_count, *refs),
        "wave",
        [offsets],
        [tables, start, measured, window_a, window_b, *others, *halos],
        [window] * depth_count + [jax.ShapeDtypeStruct((2, n // depth_count, n), f32)] * depth_count,
        [pltpu.VMEM((count, 2, n, n), f32)] * 2,
        work=5 * 10**9,
    )
    grads, probe_parts = parts[:depth_count], parts[depth_count:]

    probe_grad = probe_parts[0]
    for j in range(1, depth_count):
        probe_grad = probe_grad + lax.ppermute(
            probe_parts[j], "depth", [(t, (t + j) % depth_count) for t in range(depth_count)]
        )
    rounds = scan_count.bit_length() - 1
    paired = scan_count == 1 << rounds and rounds > 2
    grads = call(turn_kernel, "turn", [offsets], grads, [window] * depth_count, after=[probe_grad])
    if paired:
        for level in range(rounds - 2):
            probe_grad = probe_grad + sum_round(probe_grad, level)
    else:
        probe_grad = lax.psum(probe_grad, "scan")

    spill = [across(grads[(q - 1) % depth_count], 1, q, 1) for q in range(depth_count)]
    back = [grads[0]]
    for j in range(1, depth_count):
        back.append(lax.ppermute(grads[j], "depth", [(t, (t + j) % depth_count) for t in (0, 1)]))
    object_grad, zero = call(
        lambda *refs: place_kernel(depth_count, *refs),
        "place",
        [offsets, offsets_prev],
        back,
        [whole, token],
        work=2 * 10**9,
    )
    if paired:
        probe_grad = probe_grad + sum_round(probe_grad, rounds - 2) + zero[0, 0]
        last = sum_round(probe_grad, rounds - 1)
    object_grad, zero = call(
        lambda *refs: spill_kernel(depth_count, *refs),
        "spill",
        [offsets_prev],
        [object_grad, *spill],
        [whole, token],
    )
    if paired:
        probe_grad = probe_grad + last + zero[0, 0]
    return object_grad, probe_grad


def solution(mesh):
    in_specs = (P("depth", None, "scan", None), P(), P("scan"), P("scan"), P("scan", None, None))
    out_specs = (P("depth", None, "scan", None), P(None, "depth", None))
    return jax.shard_map(body, mesh=mesh, in_specs=in_specs, out_specs=out_specs, check_vma=False)
```

```python
import math

import jax
import jax.numpy as jnp
import ml_dtypes
import numpy as np
from jax import lax
from jax.experimental import pallas as pl
from jax.experimental.pallas import tpu as pltpu
from jax.sharding import PartitionSpec as P

PROPAGATION = 0.5
VMEM_LIMIT = 48 * 1024 * 1024


def block_form(matrix):
    return np.block([[matrix.real, -matrix.imag], [matrix.imag, matrix.real]])


def constant_tables(width):
    grid = np.arange(width)
    frequency = np.where(grid < width // 2, grid, grid - width)
    dft = np.exp(-2j * np.pi * ((grid[:, None] * grid[None, :]) % width) / width) / math.sqrt(width)
    chirp = np.exp(-1j * PROPAGATION * np.pi * frequency.astype(np.float64) ** 2 / width)
    step = dft.conj() @ (chirp[:, None] * dft)
    step = 0.5 * (step + step.T)
    full = np.stack([block_form(m) for m in (step, step.conj(), dft, dft.conj())])
    high = full.astype(np.float32).astype(ml_dtypes.bfloat16)
    low = (full - high.astype(np.float64)).astype(np.float32).astype(ml_dtypes.bfloat16)
    return np.stack([high, low], axis=1)


def halves(x):
    high = x.astype(jnp.bfloat16)
    return high, (x - high.astype(jnp.float32)).astype(jnp.bfloat16)


def dot(a, b):
    return jnp.dot(a, b, preferred_element_type=jnp.float32)


def times_right(x, high, low):
    x_high, x_low = halves(x)
    return dot(x_high, high) + (dot(x_low, high) + dot(x_high, low))


def times_left(high, low, x):
    x_high, x_low = halves(x)
    return dot(high, x_high) + (dot(high, x_low) + dot(low, x_high))


def both_sides(re, im, tables, which):
    n = re.shape[0]
    y = times_right(jnp.concatenate([re, im], axis=1), tables[which ^ 1, 0], tables[which ^ 1, 1])
    y = jnp.concatenate([y[:, :n], y[:, n:]], axis=0)
    z = times_left(tables[which, 0], tables[which, 1], y)
    return z[:n], z[n:]


def share(offsets, tile_rows, chips_back):
    count = lax.axis_size("scan")
    base = lax.rem(lax.axis_index("scan") + count - chips_back, count) * tile_rows
    second = offsets[1] - base == tile_rows
    a = jnp.where(second, 1, 0)
    return a, offsets[2 + a], offsets[1 - a] - base, offsets[3 - a]


def cut(tile, row, col, width):
    rows, cols = tile.shape
    part = pltpu.roll(tile, lax.rem(cols - col, cols), 1)[:, :width]
    return pltpu.roll(part, lax.rem(rows - row, rows), 0)


def own_kernel(offsets, objects, tiles, window_b):
    slab, _, rows, _ = objects.shape
    _, _, row_b, col_b = share(offsets, rows, 0)
    for s in range(slab):
        for p in range(2):
            tile = objects[s, p]
            tiles[s, p] = tile
            window_b[s, p] = cut(tile, row_b, col_b, window_b.shape[-1])


def prev_kernel(offsets_prev, after, tiles, window_a, halo):
    slab, _, rows, _ = tiles.shape
    width = halo.shape[-1]
    _, col_a, row_p, col_p = share(offsets_prev, rows, 1)
    for s in range(slab):
        for p in range(2):
            halo[s, p] = cut(tiles[s, p], row_p, col_p, width)
            window_a[s, p] = cut(tiles[s, p], 0, col_a, width)


def join_kernel(offsets, after, window_b, halo, joined):
    slab, _, rows, cols = joined.shape
    _, _, row_b, _ = share(offsets, rows, 0)
    inside = lax.broadcasted_iota(jnp.int32, (rows, cols), 0) < rows - row_b
    for s in range(slab):
        for p in range(2):
            joined[s, p] = jnp.where(inside, window_b[s, p], halo[s, p])


def load_kernel(offsets, offsets_prev, intensity, far, probe, measured, start):
    rows = probe.shape[-1]
    near_a, _, _, _ = share(offsets, rows, 0)
    far_a, _, _, _ = share(offsets_prev, rows, 1)
    measured[...] = jnp.where(lax.axis_index("depth") == 0, far[far_a], intensity[1 - near_a])
    start[...] = probe[...]


def wave_kernel(depth_count, tables, probe, measured, window_a, window_b, *rest):
    others_a, others_b = rest[: depth_count - 1], rest[depth_count - 1 : 2 * depth_count - 2]
    rest = rest[2 * depth_count - 2 :]
    grads, (probe_grad, layers, waves) = rest[:depth_count], rest[depth_count:]
    slab = window_a.shape[0]
    n = probe.shape[-1]
    count = slab * depth_count
    depth = lax.axis_index("depth")
    on_a = depth == 0
    for j in range(depth_count):
        base = lax.rem(depth - j + depth_count, depth_count) * slab
        of_a, of_b = ((window_a, *others_a)[j], (window_b, *others_b)[j])
        for s in range(slab):
            for p in range(2):
                layers[base + s, p] = jnp.where(on_a, of_a[s, p], of_b[s, p])

    def enter(s, re, im):
        waves[s, 0] = re
        waves[s, 1] = im
        o_re, o_im = layers[s, 0], layers[s, 1]
        return re * o_re - im * o_im, re * o_im + im * o_re

    def forward(s, wave):
        return both_sides(*enter(s, *wave), tables, 0)

    wave = lax.fori_loop(0, count - 1, forward, (probe[0], probe[1]), unroll=True if count <= 8 else 1)
    far_re, far_im = both_sides(*enter(count - 1, *wave), tables, 2)
    misfit = 2.0 * (far_re * far_re + far_im * far_im - measured[...])
    chi = both_sides(misfit * far_re, misfit * far_im, tables, 3)

    def leave(s, chi_re, chi_im):
        w_re, w_im = waves[s, 0], waves[s, 1]
        o_re, o_im = layers[s, 0], layers[s, 1]
        waves[s, 0] = w_re * chi_re + w_im * chi_im
        waves[s, 1] = w_re * chi_im - w_im * chi_re
        return o_re * chi_re + o_im * chi_im, o_re * chi_im - o_im * chi_re

    def backward(t, chi):
        return both_sides(*leave(count - 1 - t, *chi), tables, 1)

    chi = lax.fori_loop(0, count - 1, backward, chi, unroll=True if count <= 8 else 1)
    grad = leave(0, *chi)
    for j in range(depth_count):
        base = lax.rem(depth + j, depth_count) * slab
        for s in range(slab):
            grads[j][s] = waves[base + s]
    rows = n // depth_count
    for k in range(depth_count):
        for p in range(2):
            probe_grad[k, p] = grad[p][k * rows : (k + 1) * rows]


def turn_kernel(offsets, after, *refs):
    on_a = lax.axis_index("depth") == 0
    count = len(refs) // 2
    for x, out in zip(refs[:count], refs[count:]):
        slab, _, rows, _ = x.shape
        _, _, row_b, _ = share(offsets, rows, 0)
        shift = lax.rem(jnp.where(on_a, 0, row_b), rows)
        for s in range(slab):
            for p in range(2):
                out[s, p] = pltpu.roll(x[s, p], shift, 0)


def placed(x, col, mask, cols):
    blank = jnp.zeros((x.shape[0], cols - x.shape[1]), x.dtype)
    return pltpu.roll(jnp.concatenate([jnp.where(mask, x, 0.0), blank], axis=1), col, 1)


def place_kernel(depth_count, offsets, offsets_prev, *refs):
    *parts, out = refs
    slab, _, rows, cols = out.shape
    depth = lax.axis_index("depth")
    _, _, row_b, col_b = share(offsets, rows, 0)
    _, col_a, _, _ = share(offsets_prev, rows, 1)
    row_index = lax.broadcasted_iota(jnp.int32, (rows, parts[0].shape[-1]), 0)
    corners = []
    for j in range(depth_count):
        is_a = depth == j
        is_b = lax.rem(depth + depth_count - 1, depth_count) == j
        first = jnp.where(is_a, 0, row_b)
        last = jnp.where(is_a | is_b, rows, 0)
        corners.append((jnp.where(is_a, col_a, col_b), (row_index >= first) & (row_index < last)))
    for s in range(slab):
        for p in range(2):
            total = None
            for (col, mask), part in zip(corners, parts):
                x = placed(part[s, p], col, mask, cols)
                total = x if total is None else total + x
            out[s, p] = total


def keep_kernel(after, blocks, *refs):
    *sent, out = refs
    depth = lax.axis_index("depth")
    x = blocks[0]
    for k, block in enumerate(sent):
        x = jnp.where(depth == k + 1, block[...], x)
    out[...] = x


def spill_kernel(depth_count, offsets_prev, before, *refs):
    *spills, out, token = refs
    slab, _, rows, cols = out.shape
    depth = lax.axis_index("depth")
    _, _, row_p, col_p = share(offsets_prev, rows, 1)
    mask = lax.broadcasted_iota(jnp.int32, (rows, spills[0].shape[-1]), 0) < row_p
    for s in range(slab):
        for p in range(2):
            x = spills[0][s, p]
            for q in range(1, depth_count):
                x = jnp.where(depth == q, spills[q][s, p], x)
            out[s, p] = before[s, p] + placed(x, col_p, mask, cols)
    token[...] = jnp.zeros_like(token)


def add_kernel(after, a, b, out):
    out[...] = a[...] + b[...]


def call(kernel, name, scalars, arrays, outs, scratch=(), work=10**9, after=()):
    vmem = pl.BlockSpec(memory_space=pltpu.VMEM)
    moved = sum(math.prod(x.shape) * x.dtype.itemsize for x in (*arrays, *outs))
    return pl.pallas_call(
        kernel,
        name=name,
        out_shape=outs,
        in_specs=[pl.BlockSpec(memory_space=pltpu.SMEM)] * len(scalars)
        + [pl.BlockSpec(memory_space=pl.ANY)] * len(after)
        + [vmem] * len(arrays),
        out_specs=[vmem] * len(outs),
        scratch_shapes=scratch,
        compiler_params=pltpu.CompilerParams(vmem_limit_bytes=VMEM_LIMIT),
        cost_estimate=pl.CostEstimate(flops=work, bytes_accessed=moved, transcendentals=0),
    )(*scalars, *after, *arrays)


def body(objects, probe, row_offsets, col_offsets, intensity):
    slab = objects.shape[0]
    n = probe.shape[-1]
    depth_count, scan_count = lax.axis_size("depth"), lax.axis_size("scan")
    f32 = jnp.float32

    def across(x, source, target, shift):
        route = [(source * scan_count + i, target * scan_count + (i + shift) % scan_count) for i in range(scan_count)]
        return lax.ppermute(x, ("depth", "scan"), route)

    offsets = jnp.concatenate([row_offsets, col_offsets])
    offsets_prev = lax.ppermute(offsets, "scan", [(i, (i + 1) % scan_count) for i in range(scan_count)])
    far = across(intensity, 0, 0, 1)
    window = jax.ShapeDtypeStruct((slab, 2, n, n), f32)
    whole = jax.ShapeDtypeStruct(objects.shape, f32)
    tiles, window_b = call(own_kernel, "own", [offsets], [objects], [whole, window])
    window_a, halo = call(prev_kernel, "prev", [offsets_prev], [tiles], [window] * 2, after=[far])
    halo = lax.ppermute(halo, "scan", [((i + 1) % scan_count, i) for i in range(scan_count)])

    def gathered(x, target):
        return [lax.ppermute(x, "depth", [((target - j) % depth_count, target)]) for j in range(1, depth_count)]

    others_a = gathered(window_a, 0)
    measured, start = call(
        load_kernel,
        "load",
        [offsets, offsets_prev],
        [intensity, far, probe],
        [jax.ShapeDtypeStruct((n, n), f32), jax.ShapeDtypeStruct(probe.shape, f32)],
    )

    (window_b,) = call(join_kernel, "join", [offsets], [window_b, halo], [window], after=[measured])
    others_b = gathered(window_b, 1)

    tables = jnp.asarray(constant_tables(n))
    count = slab * depth_count
    blocks = jax.ShapeDtypeStruct((depth_count, 2, n // depth_count, n), f32)
    *grads, probe_grad = call(
        lambda *refs: wave_kernel(depth_count, *refs),
        "wave",
        [],
        [tables, start, measured, window_a, window_b, *others_a, *others_b],
        [window] * depth_count + [blocks],
        [pltpu.VMEM((count, 2, n, n), f32)] * 2,
        work=5 * 10**9,
    )

    probe_grad = probe_grad + lax.ppermute(probe_grad, "depth", [(1, 0)])
    grads = call(turn_kernel, "turn", [offsets], grads, [window] * depth_count, after=[probe_grad])

    spill = [across(grads[(q - 1) % depth_count], 1, q, 1) for q in range(depth_count)]
    back = [grads[0]]
    for j in range(1, depth_count):
        back.append(lax.ppermute(grads[j], "depth", [(t, (t + j) % depth_count) for t in (0, 1)]))
    (object_grad,) = call(
        lambda *refs: place_kernel(depth_count, *refs),
        "place",
        [offsets, offsets_prev],
        back,
        [whole],
        work=2 * 10**9,
    )
    rounds = scan_count.bit_length() - 1
    if scan_count == 1 << rounds:
        order = [*range(rounds // 2, rounds), *reversed(range(rounds // 2))]
        for place, level in enumerate(order):
            last = lax.ppermute(probe_grad, ("depth", "scan"), [(i, i ^ (1 << level)) for i in range(scan_count)])
            if place == rounds - 2:
                (probe_grad,) = call(add_kernel, "add", [], [probe_grad, last], [blocks], after=[object_grad])
            else:
                probe_grad = probe_grad + last
    else:
        probe_grad = lax.psum(probe_grad, "scan")
    object_grad, token = call(
        lambda *refs: spill_kernel(depth_count, *refs),
        "spill",
        [offsets_prev],
        [object_grad, *spill],
        [whole, jax.ShapeDtypeStruct((8, n), f32)],
    )
    sent = [lax.ppermute(probe_grad[k], "depth", [(0, k)]) for k in range(1, depth_count)]
    (probe_grad,) = call(
        keep_kernel, "keep", [], [probe_grad, *sent], [jax.ShapeDtypeStruct(blocks.shape[1:], f32)], after=[token]
    )
    return object_grad, probe_grad


def solution(mesh):
    in_specs = (P("depth", None, "scan", None), P(), P("scan"), P("scan"), P("scan", None, None))
    out_specs = (P("depth", None, "scan", None), P(None, "depth", None))
    return jax.shard_map(body, mesh=mesh, in_specs=in_specs, out_specs=out_specs, check_vma=False)
```

```python
import math

import jax
import jax.numpy as jnp
import ml_dtypes
import numpy as np
from jax import lax
from jax.experimental import pallas as pl
from jax.experimental.pallas import tpu as pltpu
from jax.sharding import PartitionSpec as P

PROPAGATION = 0.5
VMEM_LIMIT = 48 * 1024 * 1024


def block_form(matrix):
    return np.block([[matrix.real, -matrix.imag], [matrix.imag, matrix.real]])


def constant_tables(width):
    grid = np.arange(width)
    frequency = np.where(grid < width // 2, grid, grid - width)
    dft = np.exp(-2j * np.pi * ((grid[:, None] * grid[None, :]) % width) / width) / math.sqrt(width)
    chirp = np.exp(-1j * PROPAGATION * np.pi * frequency.astype(np.float64) ** 2 / width)
    step = dft.conj() @ (chirp[:, None] * dft)
    step = 0.5 * (step + step.T)
    full = np.stack([block_form(m) for m in (step, step.conj(), dft, dft.conj())])
    high = full.astype(np.float32).astype(ml_dtypes.bfloat16)
    low = (full - high.astype(np.float64)).astype(np.float32).astype(ml_dtypes.bfloat16)
    return np.stack([high, low], axis=1)


def halves(x):
    high = x.astype(jnp.bfloat16)
    return high, (x - high.astype(jnp.float32)).astype(jnp.bfloat16)


def dot(a, b):
    return jnp.dot(a, b, preferred_element_type=jnp.float32)


def times_right(x, high, low):
    x_high, x_low = halves(x)
    return dot(x_high, high) + (dot(x_low, high) + dot(x_high, low))


def times_left(high, low, x):
    x_high, x_low = halves(x)
    return dot(high, x_high) + (dot(high, x_low) + dot(low, x_high))


def both_sides(re, im, tables, which):
    n = re.shape[0]
    y = times_right(jnp.concatenate([re, im], axis=1), tables[which ^ 1, 0], tables[which ^ 1, 1])
    y = jnp.concatenate([y[:, :n], y[:, n:]], axis=0)
    z = times_left(tables[which, 0], tables[which, 1], y)
    return z[:n], z[n:]


def share(offsets, tile_rows, chips_back):
    count = lax.axis_size("scan")
    base = lax.rem(lax.axis_index("scan") + count - chips_back, count) * tile_rows
    second = offsets[1] - base == tile_rows
    a = jnp.where(second, 1, 0)
    return a, offsets[2 + a], offsets[1 - a] - base, offsets[3 - a]


def cut(tile, row, col, width):
    rows, cols = tile.shape
    part = pltpu.roll(tile, lax.rem(cols - col, cols), 1)[:, :width]
    return pltpu.roll(part, lax.rem(rows - row, rows), 0)


def own_kernel(offsets, objects, tiles, window_b):
    slab, _, rows, _ = objects.shape
    _, _, row_b, col_b = share(offsets, rows, 0)
    for s in range(slab):
        for p in range(2):
            tile = objects[s, p]
            tiles[s, p] = tile
            window_b[s, p] = cut(tile, row_b, col_b, window_b.shape[-1])


def prev_kernel(offsets_prev, after, tiles, window_a, halo):
    slab, _, rows, _ = tiles.shape
    width = halo.shape[-1]
    _, col_a, row_p, col_p = share(offsets_prev, rows, 1)
    for s in range(slab):
        for p in range(2):
            halo[s, p] = cut(tiles[s, p], row_p, col_p, width)
            window_a[s, p] = cut(tiles[s, p], 0, col_a, width)


def join_kernel(offsets, after, window_b, halo, joined):
    slab, _, rows, cols = joined.shape
    _, _, row_b, _ = share(offsets, rows, 0)
    inside = lax.broadcasted_iota(jnp.int32, (rows, cols), 0) < rows - row_b
    for s in range(slab):
        for p in range(2):
            joined[s, p] = jnp.where(inside, window_b[s, p], halo[s, p])


def load_kernel(offsets, offsets_prev, intensity, far, probe, measured, start):
    rows = probe.shape[-1]
    near_a, _, _, _ = share(offsets, rows, 0)
    far_a, _, _, _ = share(offsets_prev, rows, 1)
    measured[...] = jnp.where(lax.axis_index("depth") == 0, far[far_a], intensity[1 - near_a])
    start[...] = probe[...]


def wave_kernel(depth_count, offsets, tables, probe, measured, window_a, window_b, *rest):
    others_a, others_b = rest[: depth_count - 1], rest[depth_count - 1 : 2 * depth_count - 2]
    rest = rest[2 * depth_count - 2 :]
    grads, probe_parts = rest[:depth_count], rest[depth_count : 2 * depth_count]
    layers, waves = rest[2 * depth_count :]
    slab = window_a.shape[0]
    n = probe.shape[-1]
    count = slab * depth_count
    depth = lax.axis_index("depth")
    on_a = depth == 0
    for j in range(depth_count):
        base = lax.rem(depth - j + depth_count, depth_count) * slab
        of_a, of_b = ((window_a, *others_a)[j], (window_b, *others_b)[j])
        for s in range(slab):
            for p in range(2):
                layers[base + s, p] = jnp.where(on_a, of_a[s, p], of_b[s, p])

    def enter(s, re, im):
        waves[s, 0] = re
        waves[s, 1] = im
        o_re, o_im = layers[s, 0], layers[s, 1]
        return re * o_re - im * o_im, re * o_im + im * o_re

    def forward(s, wave):
        return both_sides(*enter(s, *wave), tables, 0)

    wave = lax.fori_loop(0, count - 1, forward, (probe[0], probe[1]), unroll=True if count <= 8 else 1)
    far_re, far_im = both_sides(*enter(count - 1, *wave), tables, 2)
    misfit = 2.0 * (far_re * far_re + far_im * far_im - measured[...])
    chi = both_sides(misfit * far_re, misfit * far_im, tables, 3)

    def leave(s, chi_re, chi_im):
        w_re, w_im = waves[s, 0], waves[s, 1]
        o_re, o_im = layers[s, 0], layers[s, 1]
        waves[s, 0] = w_re * chi_re + w_im * chi_im
        waves[s, 1] = w_re * chi_im - w_im * chi_re
        return o_re * chi_re + o_im * chi_im, o_re * chi_im - o_im * chi_re

    def backward(t, chi):
        return both_sides(*leave(count - 1 - t, *chi), tables, 1)

    chi = lax.fori_loop(0, count - 1, backward, chi, unroll=True if count <= 8 else 1)
    grad = leave(0, *chi)
    _, _, row_b, _ = share(offsets, n, 0)
    turn = lax.rem(jnp.where(on_a, 0, row_b), n)
    for j in range(depth_count):
        base = lax.rem(depth + j, depth_count) * slab
        for s in range(slab):
            for p in range(2):
                grads[j][s, p] = pltpu.roll(waves[base + s, p], turn, 0)
    rows = n // depth_count
    waves[0, 0] = jnp.where(depth < 2, grad[0], 0.0)
    waves[0, 1] = jnp.where(depth < 2, grad[1], 0.0)
    for j in range(depth_count):
        start = pl.multiple_of(lax.rem(depth + j, depth_count) * rows, rows)
        for p in range(2):
            probe_parts[j][p] = waves[0, p, pl.ds(start, rows), :]


def placed(x, col, mask, cols):
    blank = jnp.zeros((x.shape[0], cols - x.shape[1]), x.dtype)
    return pltpu.roll(jnp.concatenate([jnp.where(mask, x, 0.0), blank], axis=1), col, 1)


def place_kernel(depth_count, offsets, offsets_prev, *refs):
    *parts, out = refs
    slab, _, rows, cols = out.shape
    depth = lax.axis_index("depth")
    _, _, row_b, col_b = share(offsets, rows, 0)
    _, col_a, _, _ = share(offsets_prev, rows, 1)
    row_index = lax.broadcasted_iota(jnp.int32, (rows, parts[0].shape[-1]), 0)
    corners = []
    for j in range(depth_count):
        is_a = depth == j
        is_b = lax.rem(depth + depth_count - 1, depth_count) == j
        first = jnp.where(is_a, 0, row_b)
        last = jnp.where(is_a | is_b, rows, 0)
        corners.append((jnp.where(is_a, col_a, col_b), (row_index >= first) & (row_index < last)))
    for s in range(slab):
        for p in range(2):
            total = None
            for (col, mask), part in zip(corners, parts):
                x = placed(part[s, p], col, mask, cols)
                total = x if total is None else total + x
            out[s, p] = total


def step_kernel(depth_count, later, slices, *refs):
    a, b, *parts = refs[later:-2] if slices else refs[later:-1]
    total = refs[-2] if slices else refs[-1]
    total[...] = a[...] + b[...]
    place = lax.rem(lax.axis_index("depth") + depth_count - 1, depth_count)
    for j, part in enumerate(parts):

        @pl.when(place == j)
        def _():
            for i, s in enumerate(slices):
                refs[-1][i] = part[s]


def spill_kernel(offsets_prev, before, *refs):
    *spills, out, token = refs
    slab, _, rows, cols = out.shape
    _, _, row_p, col_p = share(offsets_prev, rows, 1)
    mask = lax.broadcasted_iota(jnp.int32, (rows, spills[0].shape[-1]), 0) < row_p
    came = [(spill, i) for spill in spills for i in range(spill.shape[0])]
    for s in range(slab):
        for p in range(2):
            out[s, p] = before[s, p] + placed(came[s][0][came[s][1], p], col_p, mask, cols)
    token[...] = jnp.zeros_like(token)


def call(kernel, name, scalars, arrays, outs, scratch=(), work=10**9, after=()):
    vmem = pl.BlockSpec(memory_space=pltpu.VMEM)
    moved = sum(math.prod(x.shape) * x.dtype.itemsize for x in (*arrays, *outs))
    return pl.pallas_call(
        kernel,
        name=name,
        out_shape=outs,
        in_specs=[pl.BlockSpec(memory_space=pltpu.SMEM)] * len(scalars)
        + [pl.BlockSpec(memory_space=pl.ANY)] * len(after)
        + [vmem] * len(arrays),
        out_specs=[vmem] * len(outs),
        scratch_shapes=scratch,
        compiler_params=pltpu.CompilerParams(vmem_limit_bytes=VMEM_LIMIT),
        cost_estimate=pl.CostEstimate(flops=work, bytes_accessed=moved, transcendentals=0),
    )(*scalars, *after, *arrays)


def sum_round(x, level):
    depth_count, scan_count = lax.axis_size("depth"), lax.axis_size("scan")
    levels = scan_count.bit_length() - 1
    route = []
    for d in range(depth_count):
        step = 1 << ((level + (d % 2) * (levels // 2)) % levels)
        route += [(d * scan_count + i, d * scan_count + (i ^ step)) for i in range(scan_count)]
    return lax.ppermute(x, ("depth", "scan"), route)


def body(objects, probe, row_offsets, col_offsets, intensity):
    slab = objects.shape[0]
    n = probe.shape[-1]
    depth_count, scan_count = lax.axis_size("depth"), lax.axis_size("scan")
    f32 = jnp.float32

    def across(x, source, target, shift):
        route = [(source * scan_count + i, target * scan_count + (i + shift) % scan_count) for i in range(scan_count)]
        return lax.ppermute(x, ("depth", "scan"), route)

    offsets = jnp.concatenate([row_offsets, col_offsets])
    offsets_prev = lax.ppermute(offsets, "scan", [(i, (i + 1) % scan_count) for i in range(scan_count)])
    far = across(intensity, 0, 0, 1)
    window = jax.ShapeDtypeStruct((slab, 2, n, n), f32)
    whole = jax.ShapeDtypeStruct(objects.shape, f32)
    tiles, window_b = call(own_kernel, "own", [offsets], [objects], [whole, window])
    window_a, halo = call(prev_kernel, "prev", [offsets_prev], [tiles], [window] * 2, after=[far])
    halo = lax.ppermute(halo, "scan", [((i + 1) % scan_count, i) for i in range(scan_count)])

    def gathered(x, target):
        return [lax.ppermute(x, "depth", [((target - j) % depth_count, target)]) for j in range(1, depth_count)]

    others_a = gathered(window_a, 0)
    measured, start = call(
        load_kernel,
        "load",
        [offsets, offsets_prev],
        [intensity, far, probe],
        [jax.ShapeDtypeStruct((n, n), f32), jax.ShapeDtypeStruct(probe.shape, f32)],
    )

    (window_b,) = call(join_kernel, "join", [offsets], [window_b, halo], [window], after=[measured])
    others_b = gathered(window_b, 1)

    tables = jnp.asarray(constant_tables(n))
    count = slab * depth_count
    parts = call(
        lambda *refs: wave_kernel(depth_count, *refs),
        "wave",
        [offsets],
        [tables, start, measured, window_a, window_b, *others_a, *others_b],
        [window] * depth_count + [jax.ShapeDtypeStruct((2, n // depth_count, n), f32)] * depth_count,
        [pltpu.VMEM((count, 2, n, n), f32)] * 2,
        work=5 * 10**9,
    )
    grads, probe_parts = parts[:depth_count], parts[depth_count:]

    back, sums = [grads[0]], [probe_parts[0]]
    for j in range(1, depth_count):
        sums.append(lax.ppermute(probe_parts[j], "depth", [(t, (t + j) % depth_count) for t in range(depth_count)]))
        back.append(lax.ppermute(grads[j], "depth", [(t, (t + j) % depth_count) for t in (0, 1)]))

    half = jax.ShapeDtypeStruct(sums[0].shape, f32)
    ahead = [(i, (i + 1) % scan_count) for i in range(scan_count)]
    rounds = scan_count.bit_length() - 1
    paired = scan_count == 1 << rounds and rounds > 2
    spill = []

    def step(a, b, slices, after):
        outs = [half, jax.ShapeDtypeStruct((len(slices), 2, n, n), f32)] if slices else [half]
        return call(
            lambda *refs: step_kernel(depth_count, len(after), slices, *refs),
            "step",
            [],
            [a, b, *(back if slices else [])],
            outs,
            after=after,
        )

    (object_grad,) = call(
        lambda *refs: place_kernel(depth_count, *refs),
        "place",
        [offsets, offsets_prev],
        back,
        [whole],
        work=2 * 10**9,
    )
    turns = rounds - 1 if paired else 1
    share_of = [tuple(range(slab * k // turns, slab * (k + 1) // turns)) for k in range(turns)]
    total = sums[0]
    for x in sums[1:-1]:
        total = total + x
    other = sums[-1] if depth_count > 1 else jnp.zeros_like(total)
    for k, slices in enumerate(share_of):
        total, *payload = step(total, other, slices, spill[k - 2 : k - 1] if k >= 2 else [])
        other = sum_round(total, k) if paired else jnp.zeros_like(total)
        spill += [lax.ppermute(x, "scan", ahead) for x in payload]
    if paired:
        (total,) = step(total, other, (), [*spill[:-1][-1:], object_grad])
        other = sum_round(total, rounds - 1)
    object_grad, token = call(
        spill_kernel, "spill", [offsets_prev], [object_grad, *spill], [whole, jax.ShapeDtypeStruct((8, n), f32)]
    )
    if paired:
        (total,) = step(total, other, (), [token])
    else:
        total = lax.psum(total, "scan")
    return object_grad, total


def solution(mesh):
    in_specs = (P("depth", None, "scan", None), P(), P("scan"), P("scan"), P("scan", None, None))
    out_specs = (P("depth", None, "scan", None), P(None, "depth", None))
    return jax.shard_map(body, mesh=mesh, in_specs=in_specs, out_specs=out_specs, check_vma=False)
```

```python
import math

import jax
import jax.numpy as jnp
import ml_dtypes
import numpy as np
from jax import lax
from jax.experimental import pallas as pl
from jax.experimental.pallas import tpu as pltpu
from jax.sharding import PartitionSpec as P

PROPAGATION = 0.5
VMEM_LIMIT = 48 * 1024 * 1024


def block_form(matrix):
    return np.block([[matrix.real, -matrix.imag], [matrix.imag, matrix.real]])


def constant_tables(width):
    grid = np.arange(width)
    frequency = np.where(grid < width // 2, grid, grid - width)
    dft = np.exp(-2j * np.pi * ((grid[:, None] * grid[None, :]) % width) / width) / math.sqrt(width)
    chirp = np.exp(-1j * PROPAGATION * np.pi * frequency.astype(np.float64) ** 2 / width)
    step = dft.conj() @ (chirp[:, None] * dft)
    step = 0.5 * (step + step.T)
    full = np.stack([block_form(m) for m in (step, step.conj(), dft, dft.conj())])
    high = full.astype(np.float32).astype(ml_dtypes.bfloat16)
    low = (full - high.astype(np.float64)).astype(np.float32).astype(ml_dtypes.bfloat16)
    return np.stack([high, low], axis=1)


def halves(x):
    high = x.astype(jnp.bfloat16)
    return high, (x - high.astype(jnp.float32)).astype(jnp.bfloat16)


def dot(a, b):
    return jnp.dot(a, b, preferred_element_type=jnp.float32)


def times_right(x, high, low):
    x_high, x_low = halves(x)
    return dot(x_high, high) + (dot(x_low, high) + dot(x_high, low))


def times_left(high, low, x):
    x_high, x_low = halves(x)
    return dot(high, x_high) + (dot(high, x_low) + dot(low, x_high))


def both_sides(re, im, tables, which):
    n = re.shape[0]
    y = times_right(jnp.concatenate([re, im], axis=1), tables[which ^ 1, 0], tables[which ^ 1, 1])
    y = jnp.concatenate([y[:, :n], y[:, n:]], axis=0)
    z = times_left(tables[which, 0], tables[which, 1], y)
    return z[:n], z[n:]


def share(offsets, tile_rows, chips_back):
    count = lax.axis_size("scan")
    base = lax.rem(lax.axis_index("scan") + count - chips_back, count) * tile_rows
    second = offsets[1] - base == tile_rows
    a = jnp.where(second, 1, 0)
    return a, offsets[2 + a], offsets[1 - a] - base, offsets[3 - a]


def cut(tile, row, col, width):
    rows, cols = tile.shape
    part = pltpu.roll(tile, lax.rem(cols - col, cols), 1)[:, :width]
    return pltpu.roll(part, lax.rem(rows - row, rows), 0)


def own_kernel(offsets, objects, tiles, window_b):
    slab, _, rows, _ = objects.shape
    _, _, row_b, col_b = share(offsets, rows, 0)
    for s in range(slab):
        for p in range(2):
            tile = objects[s, p]
            tiles[s, p] = tile
            window_b[s, p] = cut(tile, row_b, col_b, window_b.shape[-1])


def prev_kernel(offsets_prev, tiles, window_a, halo):
    slab, _, rows, _ = tiles.shape
    width = halo.shape[-1]
    _, col_a, row_p, col_p = share(offsets_prev, rows, 1)
    for s in range(slab):
        for p in range(2):
            halo[s, p] = cut(tiles[s, p], row_p, col_p, width)
            window_a[s, p] = cut(tiles[s, p], 0, col_a, width)


def join_kernel(offsets, after, window_b, halo, joined):
    slab, _, rows, cols = joined.shape
    _, _, row_b, _ = share(offsets, rows, 0)
    inside = lax.broadcasted_iota(jnp.int32, (rows, cols), 0) < rows - row_b
    for s in range(slab):
        for p in range(2):
            joined[s, p] = jnp.where(inside, window_b[s, p], halo[s, p])


def load_kernel(offsets, after, intensity, probe, passed, near, start):
    a, _, _, _ = share(offsets, probe.shape[-1], 0)
    passed[...] = intensity[a]
    near[...] = intensity[1 - a]
    start[...] = probe[...]


def wave_kernel(depth_count, offsets, tables, probe, near, far, window_a, window_b, *rest):
    others_a, others_b = rest[: depth_count - 1], rest[depth_count - 1 : 2 * depth_count - 2]
    rest = rest[2 * depth_count - 2 :]
    grads, probe_parts = rest[:depth_count], rest[depth_count : 2 * depth_count]
    layers, waves = rest[2 * depth_count :]
    slab = window_a.shape[0]
    n = probe.shape[-1]
    count = slab * depth_count
    depth = lax.axis_index("depth")
    on_a = depth == 0
    for j in range(depth_count):
        base = lax.rem(depth - j + depth_count, depth_count) * slab
        of_a, of_b = ((window_a, *others_a)[j], (window_b, *others_b)[j])
        for s in range(slab):
            for p in range(2):
                layers[base + s, p] = jnp.where(on_a, of_a[s, p], of_b[s, p])

    def enter(s, re, im):
        waves[s, 0] = re
        waves[s, 1] = im
        o_re, o_im = layers[s, 0], layers[s, 1]
        return re * o_re - im * o_im, re * o_im + im * o_re

    def forward(s, wave):
        return both_sides(*enter(s, *wave), tables, 0)

    wave = lax.fori_loop(0, count - 1, forward, (probe[0], probe[1]), unroll=True if count <= 8 else 1)
    far_re, far_im = both_sides(*enter(count - 1, *wave), tables, 2)
    measured = jnp.where(on_a, far[...], near[...])
    misfit = 2.0 * (far_re * far_re + far_im * far_im - measured)
    chi = both_sides(misfit * far_re, misfit * far_im, tables, 3)

    def leave(s, chi_re, chi_im):
        w_re, w_im = waves[s, 0], waves[s, 1]
        o_re, o_im = layers[s, 0], layers[s, 1]
        waves[s, 0] = w_re * chi_re + w_im * chi_im
        waves[s, 1] = w_re * chi_im - w_im * chi_re
        return o_re * chi_re + o_im * chi_im, o_re * chi_im - o_im * chi_re

    def backward(t, chi):
        return both_sides(*leave(count - 1 - t, *chi), tables, 1)

    chi = lax.fori_loop(0, count - 1, backward, chi, unroll=True if count <= 8 else 1)
    grad = leave(0, *chi)
    _, _, row_b, _ = share(offsets, n, 0)
    turn = lax.rem(jnp.where(on_a, 0, row_b), n)
    for j in range(depth_count):
        base = lax.rem(depth + j, depth_count) * slab
        for s in range(slab):
            for p in range(2):
                grads[j][s, p] = pltpu.roll(waves[base + s, p], turn, 0)
    rows = n // depth_count
    waves[0, 0] = jnp.where(depth < 2, grad[0], 0.0)
    waves[0, 1] = jnp.where(depth < 2, grad[1], 0.0)
    for j in range(depth_count):
        start = pl.multiple_of(lax.rem(depth + j, depth_count) * rows, rows)
        for p in range(2):
            probe_parts[j][p] = waves[0, p, pl.ds(start, rows), :]


def placed(x, col, mask, cols):
    blank = jnp.zeros((x.shape[0], cols - x.shape[1]), x.dtype)
    return pltpu.roll(jnp.concatenate([jnp.where(mask, x, 0.0), blank], axis=1), col, 1)


def place_kernel(depth_count, offsets, offsets_prev, *refs):
    *parts, out = refs
    slab, _, rows, cols = out.shape
    depth = lax.axis_index("depth")
    _, _, row_b, col_b = share(offsets, rows, 0)
    _, col_a, _, _ = share(offsets_prev, rows, 1)
    row_index = lax.broadcasted_iota(jnp.int32, (rows, parts[0].shape[-1]), 0)
    corners = []
    for j in range(depth_count):
        is_a = depth == j
        is_b = lax.rem(depth + depth_count - 1, depth_count) == j
        first = jnp.where(is_a, 0, row_b)
        last = jnp.where(is_a | is_b, rows, 0)
        corners.append((jnp.where(is_a, col_a, col_b), (row_index >= first) & (row_index < last)))
    for s in range(slab):
        for p in range(2):
            total = None
            for (col, mask), part in zip(corners, parts):
                x = placed(part[s, p], col, mask, cols)
                total = x if total is None else total + x
            out[s, p] = total


def step_kernel(depth_count, later, slices, *refs):
    a, b, *parts = refs[later:-2] if slices else refs[later:-1]
    total = refs[-2] if slices else refs[-1]
    total[...] = a[...] + b[...]
    place = lax.rem(lax.axis_index("depth") + depth_count - 1, depth_count)
    for j, part in enumerate(parts):

        @pl.when(place == j)
        def _():
            for i, s in enumerate(slices):
                refs[-1][i] = part[s]


def spill_kernel(offsets_prev, before, *refs):
    *spills, out, token = refs
    slab, _, rows, cols = out.shape
    _, _, row_p, col_p = share(offsets_prev, rows, 1)
    mask = lax.broadcasted_iota(jnp.int32, (rows, spills[0].shape[-1]), 0) < row_p
    came = [(spill, i) for spill in spills for i in range(spill.shape[0])]
    for s in range(slab):
        for p in range(2):
            out[s, p] = before[s, p] + placed(came[s][0][came[s][1], p], col_p, mask, cols)
    token[...] = jnp.zeros_like(token)


def call(kernel, name, scalars, arrays, outs, scratch=(), work=10**9, after=()):
    vmem = pl.BlockSpec(memory_space=pltpu.VMEM)
    moved = sum(math.prod(x.shape) * x.dtype.itemsize for x in (*arrays, *outs))
    return pl.pallas_call(
        kernel,
        name=name,
        out_shape=outs,
        in_specs=[pl.BlockSpec(memory_space=pltpu.SMEM)] * len(scalars)
        + [pl.BlockSpec(memory_space=pl.ANY)] * len(after)
        + [vmem] * len(arrays),
        out_specs=[vmem] * len(outs),
        scratch_shapes=scratch,
        compiler_params=pltpu.CompilerParams(vmem_limit_bytes=VMEM_LIMIT),
        cost_estimate=pl.CostEstimate(flops=work, bytes_accessed=moved, transcendentals=0),
    )(*scalars, *after, *arrays)


def sum_round(x, level):
    depth_count, scan_count = lax.axis_size("depth"), lax.axis_size("scan")
    levels = scan_count.bit_length() - 1
    route = []
    for d in range(depth_count):
        step = 1 << ((level + (d % 2) * (levels // 2)) % levels)
        route += [(d * scan_count + i, d * scan_count + (i ^ step)) for i in range(scan_count)]
    return lax.ppermute(x, ("depth", "scan"), route)


def body(objects, probe, row_offsets, col_offsets, intensity):
    slab = objects.shape[0]
    n = probe.shape[-1]
    depth_count, scan_count = lax.axis_size("depth"), lax.axis_size("scan")
    f32 = jnp.float32

    def across(x, source, target, shift):
        route = [(source * scan_count + i, target * scan_count + (i + shift) % scan_count) for i in range(scan_count)]
        return lax.ppermute(x, ("depth", "scan"), route)

    offsets = jnp.concatenate([row_offsets, col_offsets])
    offsets_prev = lax.ppermute(offsets, "scan", [(i, (i + 1) % scan_count) for i in range(scan_count)])
    window = jax.ShapeDtypeStruct((slab, 2, n, n), f32)
    whole = jax.ShapeDtypeStruct(objects.shape, f32)
    tiles, window_b = call(own_kernel, "own", [offsets], [objects], [whole, window])
    window_a, halo = call(prev_kernel, "prev", [offsets_prev], [tiles], [window] * 2)
    halo = lax.ppermute(halo, "scan", [((i + 1) % scan_count, i) for i in range(scan_count)])

    def gathered(x, target):
        return [lax.ppermute(x, "depth", [((target - j) % depth_count, target)]) for j in range(1, depth_count)]

    others_a = gathered(window_a, 0)
    plane = jax.ShapeDtypeStruct((n, n), f32)
    passed, near, start = call(
        load_kernel,
        "load",
        [offsets],
        [intensity, probe],
        [plane, plane, jax.ShapeDtypeStruct(probe.shape, f32)],
        after=[window_a],
    )
    far = across(passed, 0, 0, 1)
    (window_b,) = call(join_kernel, "join", [offsets], [window_b, halo], [window], after=[far])
    others_b = gathered(window_b, 1)

    tables = jnp.asarray(constant_tables(n))
    count = slab * depth_count
    parts = call(
        lambda *refs: wave_kernel(depth_count, *refs),
        "wave",
        [offsets],
        [tables, start, near, far, window_a, window_b, *others_a, *others_b],
        [window] * depth_count + [jax.ShapeDtypeStruct((2, n // depth_count, n), f32)] * depth_count,
        [pltpu.VMEM((count, 2, n, n), f32)] * 2,
        work=5 * 10**9,
    )
    grads, probe_parts = parts[:depth_count], parts[depth_count:]

    back, sums = [grads[0]], [probe_parts[0]]
    for j in range(1, depth_count):
        sums.append(lax.ppermute(probe_parts[j], "depth", [(t, (t + j) % depth_count) for t in range(depth_count)]))
        back.append(lax.ppermute(grads[j], "depth", [(t, (t + j) % depth_count) for t in (0, 1)]))

    half = jax.ShapeDtypeStruct(sums[0].shape, f32)
    ahead = [(i, (i + 1) % scan_count) for i in range(scan_count)]
    rounds = scan_count.bit_length() - 1
    paired = scan_count == 1 << rounds and rounds > 2
    spill = []

    def step(a, b, slices, after):
        outs = [half, jax.ShapeDtypeStruct((len(slices), 2, n, n), f32)] if slices else [half]
        return call(
            lambda *refs: step_kernel(depth_count, len(after), slices, *refs),
            "step",
            [],
            [a, b, *(back if slices else [])],
            outs,
            after=after,
        )

    (object_grad,) = call(
        lambda *refs: place_kernel(depth_count, *refs),
        "place",
        [offsets, offsets_prev],
        back,
        [whole],
        work=2 * 10**9,
    )
    turns = rounds - 1 if paired else 1
    share_of = [tuple(range(slab * k // turns, slab * (k + 1) // turns)) for k in range(turns)]
    total = sums[0]
    for x in sums[1:-1]:
        total = total + x
    other = sums[-1] if depth_count > 1 else jnp.zeros_like(total)
    for k, slices in enumerate(share_of):
        total, *payload = step(total, other, slices, spill[k - 2 : k - 1] if k >= 2 else [])
        other = sum_round(total, k) if paired else jnp.zeros_like(total)
        spill += [lax.ppermute(x, "scan", ahead) for x in payload]
    if paired:
        (total,) = step(total, other, (), [*spill[:-1][-1:], object_grad])
        other = sum_round(total, rounds - 1)
    object_grad, token = call(
        spill_kernel, "spill", [offsets_prev], [object_grad, *spill], [whole, jax.ShapeDtypeStruct((8, n), f32)]
    )
    if paired:
        (total,) = step(total, other, (), [token])
    else:
        total = lax.psum(total, "scan")
    return object_grad, total


def solution(mesh):
    in_specs = (P("depth", None, "scan", None), P(), P("scan"), P("scan"), P("scan", None, None))
    out_specs = (P("depth", None, "scan", None), P(None, "depth", None))
    return jax.shard_map(body, mesh=mesh, in_specs=in_specs, out_specs=out_specs, check_vma=False)
```

```python
import math

import jax
import jax.numpy as jnp
import ml_dtypes
import numpy as np
from jax import lax
from jax.experimental import pallas as pl
from jax.experimental.pallas import tpu as pltpu
from jax.sharding import PartitionSpec as P

PROPAGATION = 0.5
VMEM_LIMIT = 48 * 1024 * 1024


def block_form(matrix):
    return np.block([[matrix.real, -matrix.imag], [matrix.imag, matrix.real]])


def constant_tables(width):
    grid = np.arange(width)
    frequency = np.where(grid < width // 2, grid, grid - width)
    dft = np.exp(-2j * np.pi * ((grid[:, None] * grid[None, :]) % width) / width) / math.sqrt(width)
    chirp = np.exp(-1j * PROPAGATION * np.pi * frequency.astype(np.float64) ** 2 / width)
    step = dft.conj() @ (chirp[:, None] * dft)
    step = 0.5 * (step + step.T)
    full = np.stack([block_form(m) for m in (step, step.conj(), dft, dft.conj())])
    high = full.astype(np.float32).astype(ml_dtypes.bfloat16)
    low = (full - high.astype(np.float64)).astype(np.float32).astype(ml_dtypes.bfloat16)
    return np.stack([high, low], axis=1)


def halves(x):
    high = x.astype(jnp.bfloat16)
    return high, (x - high.astype(jnp.float32)).astype(jnp.bfloat16)


def dot(a, b):
    return jnp.dot(a, b, preferred_element_type=jnp.float32)


def times_right(x, high, low):
    x_high, x_low = halves(x)
    return dot(jnp.concatenate([x_high, x_low, x_high], axis=1), jnp.concatenate([high, high, low], axis=0))


def times_left(high, low, x):
    x_high, x_low = halves(x)
    return dot(jnp.concatenate([high, high, low], axis=1), jnp.concatenate([x_high, x_low, x_high], axis=0))


def both_sides(re, im, tables, which):
    n = re.shape[0]
    y = times_right(jnp.concatenate([re, im], axis=1), tables[which ^ 1, 0], tables[which ^ 1, 1])
    y = jnp.concatenate([y[:, :n], y[:, n:]], axis=0)
    z = times_left(tables[which, 0], tables[which, 1], y)
    return z[:n], z[n:]


def share(offsets, tile_rows):
    a = jnp.where(offsets[1] >= offsets[0], 1, 0)
    return a, offsets[2 + a], offsets[1 - a] - offsets[a] + tile_rows, offsets[3 - a]


def cut(tile, row, col, width):
    rows, cols = tile.shape
    part = pltpu.roll(tile, lax.rem(cols - col, cols), 1)[:, :width]
    return pltpu.roll(part, lax.rem(rows - row, rows), 0)


def own_kernel(offsets, objects, tiles, window_b):
    slab, _, rows, _ = objects.shape
    _, _, row_b, col_b = share(offsets, rows)
    for s in range(slab):
        for p in range(2):
            tile = objects[s, p]
            tiles[s, p] = tile
            window_b[s, p] = cut(tile, row_b, col_b, window_b.shape[-1])


def prev_kernel(offsets_prev, after, tiles, window_a, halo):
    slab, _, rows, _ = tiles.shape
    width = halo.shape[-1]
    _, col_a, row_p, col_p = share(offsets_prev, rows)
    for s in range(slab):
        for p in range(2):
            halo[s, p] = cut(tiles[s, p], row_p, col_p, width)
            window_a[s, p] = cut(tiles[s, p], 0, col_a, width)


def join_kernel(offsets, after, window_b, halo, joined):
    slab, _, rows, cols = joined.shape
    _, _, row_b, _ = share(offsets, rows)
    inside = lax.broadcasted_iota(jnp.int32, (rows, cols), 0) < rows - row_b
    for s in range(slab):
        for p in range(2):
            joined[s, p] = jnp.where(inside, window_b[s, p], halo[s, p])


def load_kernel(offsets, offsets_prev, intensity, far, probe, measured, start):
    rows = probe.shape[-1]
    near_a, _, _, _ = share(offsets, rows)
    far_a, _, _, _ = share(offsets_prev, rows)
    measured[...] = jnp.where(lax.axis_index("depth") == 0, far[far_a], intensity[1 - near_a])
    start[...] = probe[...]


def wave_kernel(depth_count, offsets, tables, probe, measured, window_a, window_b, *rest):
    others_a, others_b = rest[: depth_count - 1], rest[depth_count - 1 : 2 * depth_count - 2]
    rest = rest[2 * depth_count - 2 :]
    grads, probe_parts = rest[:depth_count], rest[depth_count : 2 * depth_count]
    layers, waves = rest[2 * depth_count :]
    slab = window_a.shape[0]
    n = probe.shape[-1]
    count = slab * depth_count
    depth = lax.axis_index("depth")
    on_a = depth == 0
    for j in range(depth_count):
        base = lax.rem(depth - j + depth_count, depth_count) * slab
        of_a, of_b = ((window_a, *others_a)[j], (window_b, *others_b)[j])
        for s in range(slab):
            for p in range(2):
                layers[base + s, p] = jnp.where(on_a, of_a[s, p], of_b[s, p])

    def enter(s, re, im):
        waves[s, 0] = re
        waves[s, 1] = im
        o_re, o_im = layers[s, 0], layers[s, 1]
        return re * o_re - im * o_im, re * o_im + im * o_re

    def forward(s, wave):
        return both_sides(*enter(s, *wave), tables, 0)

    wave = lax.fori_loop(0, count - 1, forward, (probe[0], probe[1]), unroll=True if count <= 8 else 1)
    far_re, far_im = both_sides(*enter(count - 1, *wave), tables, 2)
    misfit = 2.0 * (far_re * far_re + far_im * far_im - measured[...])
    chi = both_sides(misfit * far_re, misfit * far_im, tables, 3)

    def leave(s, chi_re, chi_im):
        w_re, w_im = waves[s, 0], waves[s, 1]
        o_re, o_im = layers[s, 0], layers[s, 1]
        waves[s, 0] = w_re * chi_re + w_im * chi_im
        waves[s, 1] = w_re * chi_im - w_im * chi_re
        return o_re * chi_re + o_im * chi_im, o_re * chi_im - o_im * chi_re

    def backward(t, chi):
        return both_sides(*leave(count - 1 - t, *chi), tables, 1)

    chi = lax.fori_loop(0, count - 1, backward, chi, unroll=True if count <= 8 else 1)
    grad = leave(0, *chi)
    _, _, row_b, _ = share(offsets, n)
    turn = lax.rem(jnp.where(on_a, 0, row_b), n)
    for j in range(depth_count):
        base = lax.rem(depth + j, depth_count) * slab
        for s in range(slab):
            for p in range(2):
                grads[j][s, p] = pltpu.roll(waves[base + s, p], turn, 0)
    rows = n // depth_count
    waves[0, 0] = jnp.where(depth < 2, grad[0], 0.0)
    waves[0, 1] = jnp.where(depth < 2, grad[1], 0.0)
    for j in range(depth_count):
        start = pl.multiple_of(lax.rem(depth + j, depth_count) * rows, rows)
        for p in range(2):
            probe_parts[j][p] = waves[0, p, pl.ds(start, rows), :]


def placed(x, col, mask, cols):
    blank = jnp.zeros((x.shape[0], cols - x.shape[1]), x.dtype)
    return pltpu.roll(jnp.concatenate([jnp.where(mask, x, 0.0), blank], axis=1), col, 1)


def place_kernel(depth_count, offsets, offsets_prev, *refs):
    *parts, out = refs
    slab, _, rows, cols = out.shape
    depth = lax.axis_index("depth")
    _, _, row_b, col_b = share(offsets, rows)
    _, col_a, _, _ = share(offsets_prev, rows)
    row_index = lax.broadcasted_iota(jnp.int32, (rows, parts[0].shape[-1]), 0)
    corners = []
    for j in range(depth_count):
        is_a = depth == j
        is_b = lax.rem(depth + depth_count - 1, depth_count) == j
        first = jnp.where(is_a, 0, row_b)
        last = jnp.where(is_a | is_b, rows, 0)
        corners.append((jnp.where(is_a, col_a, col_b), (row_index >= first) & (row_index < last)))
    for s in range(slab):
        for p in range(2):
            total = None
            for (col, mask), part in zip(corners, parts):
                x = placed(part[s, p], col, mask, cols)
                total = x if total is None else total + x
            out[s, p] = total


def step_kernel(depth_count, later, slices, *refs):
    a, b, *parts = refs[later:-2] if slices else refs[later:-1]
    total = refs[-2] if slices else refs[-1]
    total[...] = a[...] + b[...]
    place = lax.rem(lax.axis_index("depth") + depth_count - 1, depth_count)
    for j, part in enumerate(parts):

        @pl.when(place == j)
        def _():
            for i, s in enumerate(slices):
                refs[-1][i] = part[s]


def spill_kernel(offsets_prev, before, *refs):
    *spills, out, token = refs
    slab, _, rows, cols = out.shape
    _, _, row_p, col_p = share(offsets_prev, rows)
    mask = lax.broadcasted_iota(jnp.int32, (rows, spills[0].shape[-1]), 0) < row_p
    came = [(spill, i) for spill in spills for i in range(spill.shape[0])]
    for s in range(slab):
        for p in range(2):
            out[s, p] = before[s, p] + placed(came[s][0][came[s][1], p], col_p, mask, cols)
    token[...] = jnp.zeros_like(token)


def call(kernel, name, scalars, arrays, outs, scratch=(), work=10**9, after=()):
    vmem = pl.BlockSpec(memory_space=pltpu.VMEM)
    moved = sum(math.prod(x.shape) * x.dtype.itemsize for x in (*arrays, *outs))
    return pl.pallas_call(
        kernel,
        name=name,
        out_shape=outs,
        in_specs=[pl.BlockSpec(memory_space=pltpu.SMEM)] * len(scalars)
        + [pl.BlockSpec(memory_space=pl.ANY)] * len(after)
        + [vmem] * len(arrays),
        out_specs=[vmem] * len(outs),
        scratch_shapes=scratch,
        compiler_params=pltpu.CompilerParams(vmem_limit_bytes=VMEM_LIMIT),
        cost_estimate=pl.CostEstimate(flops=work, bytes_accessed=moved, transcendentals=0),
    )(*scalars, *after, *arrays)


def sum_round(x, level):
    depth_count, scan_count = lax.axis_size("depth"), lax.axis_size("scan")
    levels = scan_count.bit_length() - 1
    route = []
    for d in range(depth_count):
        step = 1 << ((level + (d % 2) * (levels // 2)) % levels)
        route += [(d * scan_count + i, d * scan_count + (i ^ step)) for i in range(scan_count)]
    return lax.ppermute(x, ("depth", "scan"), route)


def body(objects, probe, row_offsets, col_offsets, intensity):
    slab = objects.shape[0]
    n = probe.shape[-1]
    depth_count, scan_count = lax.axis_size("depth"), lax.axis_size("scan")
    f32 = jnp.float32

    def across(x, source, target, shift):
        route = [(source * scan_count + i, target * scan_count + (i + shift) % scan_count) for i in range(scan_count)]
        return lax.ppermute(x, ("depth", "scan"), route)

    offsets = jnp.concatenate([row_offsets, col_offsets])
    offsets_prev = lax.ppermute(offsets, "scan", [(i, (i + 1) % scan_count) for i in range(scan_count)])
    far = across(intensity, 0, 0, 1)
    window = jax.ShapeDtypeStruct((slab, 2, n, n), f32)
    whole = jax.ShapeDtypeStruct(objects.shape, f32)
    tiles, window_b = call(own_kernel, "own", [offsets], [objects], [whole, window])
    window_a, halo = call(prev_kernel, "prev", [offsets_prev], [tiles], [window] * 2, after=[far])
    halo = lax.ppermute(halo, "scan", [((i + 1) % scan_count, i) for i in range(scan_count)])

    def gathered(x, target):
        return [lax.ppermute(x, "depth", [((target - j) % depth_count, target)]) for j in range(1, depth_count)]

    others_a = gathered(window_a, 0)
    measured, start = call(
        load_kernel,
        "load",
        [offsets, offsets_prev],
        [intensity, far, probe],
        [jax.ShapeDtypeStruct((n, n), f32), jax.ShapeDtypeStruct(probe.shape, f32)],
    )

    (window_b,) = call(join_kernel, "join", [offsets], [window_b, halo], [window], after=[measured])
    others_b = gathered(window_b, 1)

    tables = jnp.asarray(constant_tables(n))
    count = slab * depth_count
    parts = call(
        lambda *refs: wave_kernel(depth_count, *refs),
        "wave",
        [offsets],
        [tables, start, measured, window_a, window_b, *others_a, *others_b],
        [window] * depth_count + [jax.ShapeDtypeStruct((2, n // depth_count, n), f32)] * depth_count,
        [pltpu.VMEM((count, 2, n, n), f32)] * 2,
        work=5 * 10**9,
    )
    grads, probe_parts = parts[:depth_count], parts[depth_count:]

    back, sums = [grads[0]], [probe_parts[0]]
    for j in range(1, depth_count):
        sums.append(lax.ppermute(probe_parts[j], "depth", [(t, (t + j) % depth_count) for t in range(depth_count)]))
        back.append(lax.ppermute(grads[j], "depth", [(t, (t + j) % depth_count) for t in (0, 1)]))

    half = jax.ShapeDtypeStruct(sums[0].shape, f32)
    ahead = [(i, (i + 1) % scan_count) for i in range(scan_count)]
    rounds = scan_count.bit_length() - 1
    paired = scan_count == 1 << rounds and rounds > 2
    spill = []

    def step(a, b, slices, after):
        outs = [half, jax.ShapeDtypeStruct((len(slices), 2, n, n), f32)] if slices else [half]
        return call(
            lambda *refs: step_kernel(depth_count, len(after), slices, *refs),
            "step",
            [],
            [a, b, *(back if slices else [])],
            outs,
            after=after,
        )

    (object_grad,) = call(
        lambda *refs: place_kernel(depth_count, *refs),
        "place",
        [offsets, offsets_prev],
        back,
        [whole],
        work=2 * 10**9,
    )
    turns = rounds - 1 if paired else 1
    cuts = [0, slab // 3] + [slab] * (turns - 1) if turns > 1 else [0, slab]
    share_of = [tuple(range(cuts[k], cuts[k + 1])) for k in range(turns)]
    total = sums[0]
    for x in sums[1:-1]:
        total = total + x
    other = sums[-1] if depth_count > 1 else jnp.zeros_like(total)
    for k, slices in enumerate(share_of):
        total, *payload = step(total, other, slices, spill[:1] if k == 2 else [])
        other = sum_round(total, k) if paired else jnp.zeros_like(total)
        spill += [lax.ppermute(x, "scan", ahead) for x in payload]
    if paired:
        (total,) = step(total, other, (), [object_grad])
        other = sum_round(total, rounds - 1)
    object_grad, token = call(
        spill_kernel, "spill", [offsets_prev], [object_grad, *spill], [whole, jax.ShapeDtypeStruct((8, n), f32)]
    )
    if paired:
        (total,) = step(total, other, (), [token])
    else:
        total = lax.psum(total, "scan")
    return object_grad, total


def solution(mesh):
    in_specs = (P("depth", None, "scan", None), P(), P("scan"), P("scan"), P("scan", None, None))
    out_specs = (P("depth", None, "scan", None), P(None, "depth", None))
    return jax.shard_map(body, mesh=mesh, in_specs=in_specs, out_specs=out_specs, check_vma=False)
```

```python
import math

import jax
import jax.numpy as jnp
import ml_dtypes
import numpy as np
from jax import lax
from jax.experimental import pallas as pl
from jax.experimental.pallas import tpu as pltpu
from jax.sharding import PartitionSpec as P

PROPAGATION = 0.5
VMEM_LIMIT = 48 * 1024 * 1024


def block_form(matrix):
    return np.block([[matrix.real, -matrix.imag], [matrix.imag, matrix.real]])


def constant_tables(width):
    grid = np.arange(width)
    frequency = np.where(grid < width // 2, grid, grid - width)
    dft = np.exp(-2j * np.pi * ((grid[:, None] * grid[None, :]) % width) / width) / math.sqrt(width)
    chirp = np.exp(-1j * PROPAGATION * np.pi * frequency.astype(np.float64) ** 2 / width)
    step = dft.conj() @ (chirp[:, None] * dft)
    step = 0.5 * (step + step.T)
    full = np.stack([block_form(m) for m in (step, step.conj(), dft, dft.conj())])
    high = full.astype(np.float32).astype(ml_dtypes.bfloat16)
    low = (full - high.astype(np.float64)).astype(np.float32).astype(ml_dtypes.bfloat16)
    return np.stack([high, low], axis=1)


def halves(x):
    high = x.astype(jnp.bfloat16)
    return high, (x - high.astype(jnp.float32)).astype(jnp.bfloat16)


def dot(a, b):
    return jnp.dot(a, b, preferred_element_type=jnp.float32)


def times_right(x, high, low):
    x_high, x_low = halves(x)
    return dot(jnp.concatenate([x_high, x_low, x_high], axis=1), jnp.concatenate([high, high, low], axis=0))


def times_left(high, low, x):
    x_high, x_low = halves(x)
    y = dot(jnp.concatenate([high, high, low], axis=1), jnp.concatenate([x_high, x_low, x_high], axis=0))
    n = x.shape[0]
    return y[:n, :n] - y[n:, n:], y[:n, n:] + y[n:, :n]


def both_sides(re, im, tables, which):
    n = re.shape[0]
    y = times_right(jnp.concatenate([re, im], axis=1), tables[which ^ 1, 0], tables[which ^ 1, 1])
    return times_left(tables[which, 0, :, :n], tables[which, 1, :, :n], y)


def share(offsets, tile_rows):
    a = jnp.where(offsets[1] >= offsets[0], 1, 0)
    return a, offsets[2 + a], offsets[1 - a] - offsets[a] + tile_rows, offsets[3 - a]


def cut(tile, row, col, width):
    rows, cols = tile.shape
    part = pltpu.roll(tile, lax.rem(cols - col, cols), 1)[:, :width]
    return pltpu.roll(part, lax.rem(rows - row, rows), 0)


def own_kernel(offsets, objects, tiles, window_b):
    slab, _, rows, _ = objects.shape
    _, _, row_b, col_b = share(offsets, rows)
    for s in range(slab):
        for p in range(2):
            tile = objects[s, p]
            tiles[s, p] = tile
            window_b[s, p] = cut(tile, row_b, col_b, window_b.shape[-1])


def prev_kernel(offsets_prev, after, tiles, window_a, halo):
    slab, _, rows, _ = tiles.shape
    width = halo.shape[-1]
    _, col_a, row_p, col_p = share(offsets_prev, rows)
    for s in range(slab):
        for p in range(2):
            halo[s, p] = cut(tiles[s, p], row_p, col_p, width)
            window_a[s, p] = cut(tiles[s, p], 0, col_a, width)


def join_kernel(offsets, after, window_b, halo, joined):
    slab, _, rows, cols = joined.shape
    _, _, row_b, _ = share(offsets, rows)
    inside = lax.broadcasted_iota(jnp.int32, (rows, cols), 0) < rows - row_b
    for s in range(slab):
        for p in range(2):
            joined[s, p] = jnp.where(inside, window_b[s, p], halo[s, p])


def load_kernel(offsets, offsets_prev, intensity, far, probe, measured, start):
    rows = probe.shape[-1]
    near_a, _, _, _ = share(offsets, rows)
    far_a, _, _, _ = share(offsets_prev, rows)
    measured[...] = jnp.where(lax.axis_index("depth") == 0, far[far_a], intensity[1 - near_a])
    start[...] = probe[...]


def wave_kernel(depth_count, offsets, tables, probe, measured, window_a, window_b, *rest):
    others_a, others_b = rest[: depth_count - 1], rest[depth_count - 1 : 2 * depth_count - 2]
    rest = rest[2 * depth_count - 2 :]
    grads, probe_parts = rest[:depth_count], rest[depth_count : 2 * depth_count]
    layers, waves = rest[2 * depth_count :]
    slab = window_a.shape[0]
    n = probe.shape[-1]
    count = slab * depth_count
    depth = lax.axis_index("depth")
    on_a = depth == 0
    for j in range(depth_count):
        base = lax.rem(depth - j + depth_count, depth_count) * slab
        of_a, of_b = ((window_a, *others_a)[j], (window_b, *others_b)[j])
        for s in range(slab):
            for p in range(2):
                layers[base + s, p] = jnp.where(on_a, of_a[s, p], of_b[s, p])

    def enter(s, re, im):
        waves[s, 0] = re
        waves[s, 1] = im
        o_re, o_im = layers[s, 0], layers[s, 1]
        return re * o_re - im * o_im, re * o_im + im * o_re

    def forward(s, wave):
        return both_sides(*enter(s, *wave), tables, 0)

    wave = lax.fori_loop(0, count - 1, forward, (probe[0], probe[1]), unroll=True if count <= 8 else 1)
    far_re, far_im = both_sides(*enter(count - 1, *wave), tables, 2)
    misfit = 2.0 * (far_re * far_re + far_im * far_im - measured[...])
    chi = both_sides(misfit * far_re, misfit * far_im, tables, 3)

    def leave(s, chi_re, chi_im):
        w_re, w_im = waves[s, 0], waves[s, 1]
        o_re, o_im = layers[s, 0], layers[s, 1]
        waves[s, 0] = w_re * chi_re + w_im * chi_im
        waves[s, 1] = w_re * chi_im - w_im * chi_re
        return o_re * chi_re + o_im * chi_im, o_re * chi_im - o_im * chi_re

    def backward(t, chi):
        return both_sides(*leave(count - 1 - t, *chi), tables, 1)

    chi = lax.fori_loop(0, count - 1, backward, chi, unroll=True if count <= 8 else 1)
    grad = leave(0, *chi)
    _, _, row_b, _ = share(offsets, n)
    turn = lax.rem(jnp.where(on_a, 0, row_b), n)
    for j in range(depth_count):
        base = lax.rem(depth + j, depth_count) * slab
        for s in range(slab):
            for p in range(2):
                grads[j][s, p] = pltpu.roll(waves[base + s, p], turn, 0)
    rows = n // depth_count
    waves[0, 0] = jnp.where(depth < 2, grad[0], 0.0)
    waves[0, 1] = jnp.where(depth < 2, grad[1], 0.0)
    for j in range(depth_count):
        start = pl.multiple_of(lax.rem(depth + j, depth_count) * rows, rows)
        for p in range(2):
            probe_parts[j][p] = waves[0, p, pl.ds(start, rows), :]


def placed(x, col, mask, cols):
    blank = jnp.zeros((x.shape[0], cols - x.shape[1]), x.dtype)
    return pltpu.roll(jnp.concatenate([jnp.where(mask, x, 0.0), blank], axis=1), col, 1)


def place_kernel(depth_count, offsets, offsets_prev, *refs):
    *parts, out = refs
    slab, _, rows, cols = out.shape
    depth = lax.axis_index("depth")
    _, _, row_b, col_b = share(offsets, rows)
    _, col_a, _, _ = share(offsets_prev, rows)
    row_index = lax.broadcasted_iota(jnp.int32, (rows, parts[0].shape[-1]), 0)
    corners = []
    for j in range(depth_count):
        is_a = depth == j
        is_b = lax.rem(depth + depth_count - 1, depth_count) == j
        first = jnp.where(is_a, 0, row_b)
        last = jnp.where(is_a | is_b, rows, 0)
        corners.append((jnp.where(is_a, col_a, col_b), (row_index >= first) & (row_index < last)))
    for s in range(slab):
        for p in range(2):
            total = None
            for (col, mask), part in zip(corners, parts):
                x = placed(part[s, p], col, mask, cols)
                total = x if total is None else total + x
            out[s, p] = total


def step_kernel(depth_count, later, slices, *refs):
    a, b, *parts = refs[later:-2] if slices else refs[later:-1]
    total = refs[-2] if slices else refs[-1]
    total[...] = a[...] + b[...]
    place = lax.rem(lax.axis_index("depth") + depth_count - 1, depth_count)
    for j, part in enumerate(parts):

        @pl.when(place == j)
        def _():
            for i, s in enumerate(slices):
                refs[-1][i] = part[s]


def spill_kernel(offsets_prev, before, *refs):
    *spills, out, token = refs
    slab, _, rows, cols = out.shape
    _, _, row_p, col_p = share(offsets_prev, rows)
    mask = lax.broadcasted_iota(jnp.int32, (rows, spills[0].shape[-1]), 0) < row_p
    came = [(spill, i) for spill in spills for i in range(spill.shape[0])]
    for s in range(slab):
        for p in range(2):
            out[s, p] = before[s, p] + placed(came[s][0][came[s][1], p], col_p, mask, cols)
    token[...] = jnp.zeros_like(token)


def call(kernel, name, scalars, arrays, outs, scratch=(), work=10**9, after=()):
    vmem = pl.BlockSpec(memory_space=pltpu.VMEM)
    moved = sum(math.prod(x.shape) * x.dtype.itemsize for x in (*arrays, *outs))
    return pl.pallas_call(
        kernel,
        name=name,
        out_shape=outs,
        in_specs=[pl.BlockSpec(memory_space=pltpu.SMEM)] * len(scalars)
        + [pl.BlockSpec(memory_space=pl.ANY)] * len(after)
        + [vmem] * len(arrays),
        out_specs=[vmem] * len(outs),
        scratch_shapes=scratch,
        compiler_params=pltpu.CompilerParams(vmem_limit_bytes=VMEM_LIMIT),
        cost_estimate=pl.CostEstimate(flops=work, bytes_accessed=moved, transcendentals=0),
    )(*scalars, *after, *arrays)


def sum_round(x, level):
    depth_count, scan_count = lax.axis_size("depth"), lax.axis_size("scan")
    levels = scan_count.bit_length() - 1
    route = []
    for d in range(depth_count):
        step = 1 << ((level + (d % 2) * (levels // 2)) % levels)
        route += [(d * scan_count + i, d * scan_count + (i ^ step)) for i in range(scan_count)]
    return lax.ppermute(x, ("depth", "scan"), route)


def body(objects, probe, row_offsets, col_offsets, intensity):
    slab = objects.shape[0]
    n = probe.shape[-1]
    depth_count, scan_count = lax.axis_size("depth"), lax.axis_size("scan")
    f32 = jnp.float32

    def across(x, source, target, shift):
        route = [(source * scan_count + i, target * scan_count + (i + shift) % scan_count) for i in range(scan_count)]
        return lax.ppermute(x, ("depth", "scan"), route)

    offsets = jnp.concatenate([row_offsets, col_offsets])
    offsets_prev = lax.ppermute(offsets, "scan", [(i, (i + 1) % scan_count) for i in range(scan_count)])
    far = across(intensity, 1, 0, 1)
    window = jax.ShapeDtypeStruct((slab, 2, n, n), f32)
    whole = jax.ShapeDtypeStruct(objects.shape, f32)
    tiles, window_b = call(own_kernel, "own", [offsets], [objects], [whole, window])
    window_a, halo = call(prev_kernel, "prev", [offsets_prev], [tiles], [window] * 2, after=[far])
    halo = lax.ppermute(halo, "scan", [((i + 1) % scan_count, i) for i in range(scan_count)])

    def gathered(x, target):
        return [lax.ppermute(x, "depth", [((target - j) % depth_count, target)]) for j in range(1, depth_count)]

    others_a = gathered(window_a, 0)
    measured, start = call(
        load_kernel,
        "load",
        [offsets, offsets_prev],
        [intensity, far, probe],
        [jax.ShapeDtypeStruct((n, n), f32), jax.ShapeDtypeStruct(probe.shape, f32)],
    )

    (window_b,) = call(join_kernel, "join", [offsets], [window_b, halo], [window], after=[measured])
    others_b = gathered(window_b, 1)

    tables = jnp.asarray(constant_tables(n))
    count = slab * depth_count
    parts = call(
        lambda *refs: wave_kernel(depth_count, *refs),
        "wave",
        [offsets],
        [tables, start, measured, window_a, window_b, *others_a, *others_b],
        [window] * depth_count + [jax.ShapeDtypeStruct((2, n // depth_count, n), f32)] * depth_count,
        [pltpu.VMEM((count, 2, n, n), f32)] * 2,
        work=5 * 10**9,
    )
    grads, probe_parts = parts[:depth_count], parts[depth_count:]

    back, sums = [grads[0]], [probe_parts[0]]
    for j in range(1, depth_count):
        sums.append(lax.ppermute(probe_parts[j], "depth", [(t, (t + j) % depth_count) for t in range(depth_count)]))
        back.append(lax.ppermute(grads[j], "depth", [(t, (t + j) % depth_count) for t in (0, 1)]))

    half = jax.ShapeDtypeStruct(sums[0].shape, f32)
    ahead = [(i, (i + 1) % scan_count) for i in range(scan_count)]
    rounds = scan_count.bit_length() - 1
    paired = scan_count == 1 << rounds and rounds > 2
    spill = []

    def step(a, b, slices, after):
        outs = [half, jax.ShapeDtypeStruct((len(slices), 2, n, n), f32)] if slices else [half]
        return call(
            lambda *refs: step_kernel(depth_count, len(after), slices, *refs),
            "step",
            [],
            [a, b, *(back if slices else [])],
            outs,
            after=after,
        )

    (object_grad,) = call(
        lambda *refs: place_kernel(depth_count, *refs),
        "place",
        [offsets, offsets_prev],
        back,
        [whole],
        work=2 * 10**9,
    )
    turns = rounds - 1 if paired else 1
    cuts = [0, slab // 3] + [slab] * (turns - 1) if turns > 1 else [0, slab]
    share_of = [tuple(range(cuts[k], cuts[k + 1])) for k in range(turns)]
    total = sums[0]
    for x in sums[1:-1]:
        total = total + x
    other = sums[-1] if depth_count > 1 else jnp.zeros_like(total)
    for k, slices in enumerate(share_of):
        total, *payload = step(total, other, slices, spill[:1] if k == 2 else [])
        other = sum_round(total, k) if paired else jnp.zeros_like(total)
        spill += [lax.ppermute(x, "scan", ahead) for x in payload]
    if paired:
        (total,) = step(total, other, (), [object_grad])
        other = sum_round(total, rounds - 1)
    object_grad, token = call(
        spill_kernel, "spill", [offsets_prev], [object_grad, *spill], [whole, jax.ShapeDtypeStruct((8, n), f32)]
    )
    if paired:
        (total,) = step(total, other, (), [token])
    else:
        total = lax.psum(total, "scan")
    return object_grad, total


def solution(mesh):
    in_specs = (P("depth", None, "scan", None), P(), P("scan"), P("scan"), P("scan", None, None))
    out_specs = (P("depth", None, "scan", None), P(None, "depth", None))
    return jax.shard_map(body, mesh=mesh, in_specs=in_specs, out_specs=out_specs, check_vma=False)
```

```python
import math

import jax
import jax.numpy as jnp
import ml_dtypes
import numpy as np
from jax import lax
from jax.experimental import pallas as pl
from jax.experimental.pallas import tpu as pltpu
from jax.sharding import PartitionSpec as P

PROPAGATION = 0.5
VMEM_LIMIT = 48 * 1024 * 1024


def block_form(matrix):
    return np.block([[matrix.real, -matrix.imag], [matrix.imag, matrix.real]])


def constant_tables(width):
    grid = np.arange(width)
    frequency = np.where(grid < width // 2, grid, grid - width)
    dft = np.exp(-2j * np.pi * ((grid[:, None] * grid[None, :]) % width) / width) / math.sqrt(width)
    chirp = np.exp(-1j * PROPAGATION * np.pi * frequency.astype(np.float64) ** 2 / width)
    step = dft.conj() @ (chirp[:, None] * dft)
    step = 0.5 * (step + step.T)
    full = np.stack([block_form(m) for m in (step, step.conj(), dft, dft.conj())])
    high = full.astype(np.float32).astype(ml_dtypes.bfloat16)
    low = (full - high.astype(np.float64)).astype(np.float32).astype(ml_dtypes.bfloat16)
    return np.stack([high, low], axis=1)


def halves(x):
    high = x.astype(jnp.bfloat16)
    return high, (x - high.astype(jnp.float32)).astype(jnp.bfloat16)


def dot(a, b):
    return jnp.dot(a, b, preferred_element_type=jnp.float32)


def times_right(x, high, low):
    x_high, x_low = halves(x)
    return dot(jnp.concatenate([x_high, x_low, x_high], axis=1), jnp.concatenate([high, high, low], axis=0))


def times_left(high, low, x):
    x_high, x_low = halves(x)
    y = dot(jnp.concatenate([high, high, low], axis=1), jnp.concatenate([x_high, x_low, x_high], axis=0))
    n = x.shape[0]
    return y[:n, :n] - y[n:, n:], y[:n, n:] + y[n:, :n]


def both_sides(re, im, tables, which):
    n = re.shape[0]
    y = times_right(jnp.concatenate([re, im], axis=1), tables[which ^ 1, 0], tables[which ^ 1, 1])
    return times_left(tables[which, 0, :, :n], tables[which, 1, :, :n], y)


def share(offsets, tile_rows):
    a = jnp.where(offsets[1] >= offsets[0], 1, 0)
    return a, offsets[2 + a], offsets[1 - a] - offsets[a] + tile_rows, offsets[3 - a]


def cut(tile, row, col, width):
    rows, cols = tile.shape
    part = pltpu.roll(tile, lax.rem(cols - col, cols), 1)[:, :width]
    return pltpu.roll(part, lax.rem(rows - row, rows), 0)


def own_kernel(offsets, objects, tiles, window_b):
    slab, _, rows, _ = objects.shape
    _, _, row_b, col_b = share(offsets, rows)
    for s in range(slab):
        for p in range(2):
            tile = objects[s, p]
            tiles[s, p] = tile
            window_b[s, p] = cut(tile, row_b, col_b, window_b.shape[-1])


def halo_kernel(offsets_prev, tiles, halo):
    slab, _, rows, _ = tiles.shape
    _, _, row_p, col_p = share(offsets_prev, rows)
    for s in range(slab):
        for p in range(2):
            halo[s, p] = cut(tiles[s, p], row_p, col_p, halo.shape[-1])


def ahead_kernel(offsets_prev, after, tiles, window_a):
    slab, _, rows, _ = tiles.shape
    _, col_a, _, _ = share(offsets_prev, rows)
    for s in range(slab):
        for p in range(2):
            window_a[s, p] = cut(tiles[s, p], 0, col_a, window_a.shape[-1])


def hold_kernel(count, *refs):
    refs[count + 1][...] = refs[count][...]


def joined(inside, window_b, halo, s, p):
    return jnp.where(inside, window_b[s, p], halo[s, p])


def rows_here(offsets, rows, cols):
    _, _, row_b, _ = share(offsets, rows)
    return lax.broadcasted_iota(jnp.int32, (rows, cols), 0) < rows - row_b


def join_kernel(offsets, window_b, halo, out):
    slab, _, rows, cols = out.shape
    inside = rows_here(offsets, rows, cols)
    for s in range(slab):
        for p in range(2):
            out[s, p] = joined(inside, window_b, halo, s, p)


def load_kernel(offsets, offsets_prev, intensity, far, probe, measured, start):
    rows = probe.shape[-1]
    near_a, _, _, _ = share(offsets, rows)
    far_a, _, _, _ = share(offsets_prev, rows)
    measured[...] = jnp.where(lax.axis_index("depth") == 0, far[far_a], intensity[1 - near_a])
    start[...] = probe[...]


def enter(s, re, im, layers, waves):
    waves[s, 0] = re
    waves[s, 1] = im
    o_re, o_im = layers[s, 0], layers[s, 1]
    return re * o_re - im * o_im, re * o_im + im * o_re


def leave(s, chi_re, chi_im, layers, waves):
    w_re, w_im = waves[s, 0], waves[s, 1]
    o_re, o_im = layers[s, 0], layers[s, 1]
    waves[s, 0] = w_re * chi_re + w_im * chi_im
    waves[s, 1] = w_re * chi_im - w_im * chi_re
    return o_re * chi_re + o_im * chi_im, o_re * chi_im - o_im * chi_re


def steps(count, body, start):
    return lax.fori_loop(0, count, body, start, unroll=True if count <= 8 else 1)


def first_kernel(after, tables, probe, window_a, window_b, layers, waves, state):
    on_a = lax.axis_index("depth") == 0
    slab = layers.shape[0]
    for s in range(slab):
        for p in range(2):
            layers[s, p] = jnp.where(on_a, window_a[s, p], window_b[s, p])

    def forward(s, wave):
        return both_sides(*enter(s, *wave, layers, waves), tables, 0)

    state[0], state[1] = steps(slab, forward, (probe[0], probe[1]))


def wave_kernel(depth_count, offsets, tables, state, measured, layers_0, waves_0, window_b, halo, *rest):
    others_a, others_b = rest[: depth_count - 1], rest[depth_count - 1 : 2 * depth_count - 3]
    rest = rest[2 * depth_count - 3 :]
    grads, probe_parts = rest[:depth_count], rest[depth_count : 2 * depth_count]
    layers, waves = rest[2 * depth_count :]
    slab, n = window_b.shape[0], state.shape[-1]
    count = slab * depth_count
    depth = lax.axis_index("depth")
    on_a = depth == 0
    inside = rows_here(offsets, n, n)
    for s in range(slab):
        layers[s] = layers_0[s]
        waves[s] = waves_0[s]
    for q in range(1, depth_count):
        for s in range(slab):
            for p in range(2):
                of_b = joined(inside, window_b, halo, s, p) if q == 1 else others_b[depth_count - 1 - q][s, p]
                layers[q * slab + s, p] = jnp.where(on_a, others_a[depth_count - 1 - q][s, p], of_b)

    def forward(t, wave):
        return both_sides(*enter(slab + t, *wave, layers, waves), tables, 0)

    wave = steps(count - 1 - slab, forward, (state[0], state[1]))
    far_re, far_im = both_sides(*enter(count - 1, *wave, layers, waves), tables, 2)
    misfit = 2.0 * (far_re * far_re + far_im * far_im - measured[...])
    chi = both_sides(misfit * far_re, misfit * far_im, tables, 3)

    def backward(t, chi):
        return both_sides(*leave(count - 1 - t, *chi, layers, waves), tables, 1)

    grad = leave(0, *steps(count - 1, backward, chi), layers, waves)
    _, _, row_b, _ = share(offsets, n)
    turn = lax.rem(jnp.where(on_a, 0, row_b), n)
    for j in range(depth_count):
        base = lax.rem(depth + j, depth_count) * slab
        for s in range(slab):
            for p in range(2):
                grads[j][s, p] = pltpu.roll(waves[base + s, p], turn, 0)
    rows = n // depth_count
    waves[0, 0] = jnp.where(depth < 2, grad[0], 0.0)
    waves[0, 1] = jnp.where(depth < 2, grad[1], 0.0)
    for j in range(depth_count):
        start = pl.multiple_of(lax.rem(depth + j, depth_count) * rows, rows)
        for p in range(2):
            probe_parts[j][p] = waves[0, p, pl.ds(start, rows), :]


def placed(x, col, mask, cols):
    blank = jnp.zeros((x.shape[0], cols - x.shape[1]), x.dtype)
    return pltpu.roll(jnp.concatenate([jnp.where(mask, x, 0.0), blank], axis=1), col, 1)


def place_kernel(depth_count, offsets, offsets_prev, *refs):
    *parts, out = refs
    slab, _, rows, cols = out.shape
    depth = lax.axis_index("depth")
    _, _, row_b, col_b = share(offsets, rows)
    _, col_a, _, _ = share(offsets_prev, rows)
    row_index = lax.broadcasted_iota(jnp.int32, (rows, parts[0].shape[-1]), 0)
    corners = []
    for j in range(depth_count):
        is_a = depth == j
        is_b = lax.rem(depth + depth_count - 1, depth_count) == j
        first = jnp.where(is_a, 0, row_b)
        last = jnp.where(is_a | is_b, rows, 0)
        corners.append((jnp.where(is_a, col_a, col_b), (row_index >= first) & (row_index < last)))
    for s in range(slab):
        for p in range(2):
            total = None
            for (col, mask), part in zip(corners, parts):
                x = placed(part[s, p], col, mask, cols)
                total = x if total is None else total + x
            out[s, p] = total


def step_kernel(depth_count, later, slices, *refs):
    a, b, *parts = refs[later:-2] if slices else refs[later:-1]
    total = refs[-2] if slices else refs[-1]
    total[...] = a[...] + b[...]
    place = lax.rem(lax.axis_index("depth") + depth_count - 1, depth_count)
    for j, part in enumerate(parts):

        @pl.when(place == j)
        def _():
            for i, s in enumerate(slices):
                refs[-1][i] = part[s]


def spill_kernel(offsets_prev, before, *refs):
    *spills, out, token = refs
    slab, _, rows, cols = out.shape
    _, _, row_p, col_p = share(offsets_prev, rows)
    mask = lax.broadcasted_iota(jnp.int32, (rows, spills[0].shape[-1]), 0) < row_p
    came = [(spill, i) for spill in spills for i in range(spill.shape[0])]
    for s in range(slab):
        for p in range(2):
            out[s, p] = before[s, p] + placed(came[s][0][came[s][1], p], col_p, mask, cols)
    token[...] = jnp.zeros_like(token)


def call(kernel, name, scalars, arrays, outs, scratch=(), work=10**9, after=()):
    vmem = pl.BlockSpec(memory_space=pltpu.VMEM)
    moved = sum(math.prod(x.shape) * x.dtype.itemsize for x in (*arrays, *outs))
    return pl.pallas_call(
        kernel,
        name=name,
        out_shape=outs,
        in_specs=[pl.BlockSpec(memory_space=pltpu.SMEM)] * len(scalars)
        + [pl.BlockSpec(memory_space=pl.ANY)] * len(after)
        + [vmem] * len(arrays),
        out_specs=[vmem] * len(outs),
        scratch_shapes=scratch,
        compiler_params=pltpu.CompilerParams(vmem_limit_bytes=VMEM_LIMIT),
        cost_estimate=pl.CostEstimate(flops=work, bytes_accessed=moved, transcendentals=0),
    )(*scalars, *after, *arrays)


def sum_round(x, level):
    depth_count, scan_count = lax.axis_size("depth"), lax.axis_size("scan")
    levels = scan_count.bit_length() - 1
    route = []
    for d in range(depth_count):
        step = 1 << ((level + (d % 2) * (levels // 2)) % levels)
        route += [(d * scan_count + i, d * scan_count + (i ^ step)) for i in range(scan_count)]
    return lax.ppermute(x, ("depth", "scan"), route)


def body(objects, probe, row_offsets, col_offsets, intensity):
    slab = objects.shape[0]
    n = probe.shape[-1]
    depth_count, scan_count = lax.axis_size("depth"), lax.axis_size("scan")
    f32 = jnp.float32

    def across(x, source, target, shift):
        route = [(source * scan_count + i, target * scan_count + (i + shift) % scan_count) for i in range(scan_count)]
        return lax.ppermute(x, ("depth", "scan"), route)

    offsets = jnp.concatenate([row_offsets, col_offsets])
    offsets_prev = lax.ppermute(offsets, "scan", [(i, (i + 1) % scan_count) for i in range(scan_count)])
    far = across(intensity, 0, 0, 1)
    window = jax.ShapeDtypeStruct((slab, 2, n, n), f32)
    whole = jax.ShapeDtypeStruct(objects.shape, f32)
    tiles, window_b = call(own_kernel, "own", [offsets], [objects], [whole, window])
    (halo,) = call(halo_kernel, "halo", [offsets_prev], [tiles], [window])
    (window_a,) = call(ahead_kernel, "ahead", [offsets_prev], [tiles], [window], after=[halo])

    others_a = [lax.ppermute(window_a, "depth", [(-j % depth_count, 0)]) for j in range(1, depth_count)]
    halo_0 = across(halo, 0, 0, -1)
    waits = [*others_a, far]
    (halo,) = call(lambda *refs: hold_kernel(len(waits), *refs), "hold", [], [halo], [window], after=waits)
    route = [
        (d * scan_count + (i + 1) % scan_count, d * scan_count + i) for d in range(1, depth_count) for i in range(scan_count)
    ]
    halo = lax.ppermute(halo, ("depth", "scan"), route)
    measured, start = call(
        load_kernel,
        "load",
        [offsets, offsets_prev],
        [intensity, far, probe],
        [jax.ShapeDtypeStruct((n, n), f32), jax.ShapeDtypeStruct(probe.shape, f32)],
    )
    (first_b,) = call(join_kernel, "join", [offsets], [window_b, halo_0], [window])
    first_b = lax.ppermute(first_b, "depth", [(0, 1)])
    tables = jnp.asarray(constant_tables(n))
    layers, waves, state = call(
        first_kernel,
        "first",
        [],
        [tables, start, window_a, first_b],
        [window, window, jax.ShapeDtypeStruct((2, n, n), f32)],
        work=2 * 10**9,
        after=[measured],
    )
    others_b = []
    if depth_count > 2:
        (third_b,) = call(join_kernel, "join", [offsets], [window_b, halo], [window])
        others_b = [lax.ppermute(third_b, "depth", [((1 - j) % depth_count, 1)]) for j in range(2, depth_count)]
    count = slab * depth_count
    parts = call(
        lambda *refs: wave_kernel(depth_count, *refs),
        "wave",
        [offsets],
        [tables, state, measured, layers, waves, window_b, halo, *others_a, *others_b],
        [window] * depth_count + [jax.ShapeDtypeStruct((2, n // depth_count, n), f32)] * depth_count,
        [pltpu.VMEM((count, 2, n, n), f32)] * 2,
        work=5 * 10**9,
    )
    grads, probe_parts = parts[:depth_count], parts[depth_count:]

    back, sums = [grads[0]], [probe_parts[0]]
    for j in range(1, depth_count):
        sums.append(lax.ppermute(probe_parts[j], "depth", [(t, (t + j) % depth_count) for t in range(depth_count)]))
        back.append(lax.ppermute(grads[j], "depth", [(t, (t + j) % depth_count) for t in (0, 1)]))

    half = jax.ShapeDtypeStruct(sums[0].shape, f32)
    ahead = [(i, (i + 1) % scan_count) for i in range(scan_count)]
    rounds = scan_count.bit_length() - 1
    paired = scan_count == 1 << rounds and rounds > 2
    spill = []

    def step(a, b, slices, after):
        outs = [half, jax.ShapeDtypeStruct((len(slices), 2, n, n), f32)] if slices else [half]
        return call(
            lambda *refs: step_kernel(depth_count, len(after), slices, *refs),
            "step",
            [],
            [a, b, *(back if slices else [])],
            outs,
            after=after,
        )

    (object_grad,) = call(
        lambda *refs: place_kernel(depth_count, *refs),
        "place",
        [offsets, offsets_prev],
        back,
        [whole],
        work=2 * 10**9,
    )
    turns = rounds - 1 if paired else 1
    cuts = [0, slab // 3] + [slab] * (turns - 1) if turns > 1 else [0, slab]
    share_of = [tuple(range(cuts[k], cuts[k + 1])) for k in range(turns)]
    total = sums[0]
    for x in sums[1:-1]:
        total = total + x
    other = sums[-1] if depth_count > 1 else jnp.zeros_like(total)
    for k, slices in enumerate(share_of):
        total, *payload = step(total, other, slices, spill[:1] if k == 2 else [])
        other = sum_round(total, k) if paired else jnp.zeros_like(total)
        spill += [lax.ppermute(x, "scan", ahead) for x in payload]
    if paired:
        (total,) = step(total, other, (), [object_grad])
        other = sum_round(total, rounds - 1)
    object_grad, token = call(
        spill_kernel, "spill", [offsets_prev], [object_grad, *spill], [whole, jax.ShapeDtypeStruct((8, n), f32)]
    )
    if paired:
        (total,) = step(total, other, (), [token])
    else:
        total = lax.psum(total, "scan")
    return object_grad, total


def solution(mesh):
    in_specs = (P("depth", None, "scan", None), P(), P("scan"), P("scan"), P("scan", None, None))
    out_specs = (P("depth", None, "scan", None), P(None, "depth", None))
    return jax.shard_map(body, mesh=mesh, in_specs=in_specs, out_specs=out_specs, check_vma=False)
```

```python
import math

import jax
import jax.numpy as jnp
import ml_dtypes
import numpy as np
from jax import lax
from jax.experimental import pallas as pl
from jax.experimental.pallas import tpu as pltpu
from jax.sharding import PartitionSpec as P

PROPAGATION = 0.5
VMEM_LIMIT = 48 * 1024 * 1024


def block_form(matrix):
    return np.block([[matrix.real, -matrix.imag], [matrix.imag, matrix.real]])


def constant_tables(width):
    grid = np.arange(width)
    frequency = np.where(grid < width // 2, grid, grid - width)
    dft = np.exp(-2j * np.pi * ((grid[:, None] * grid[None, :]) % width) / width) / math.sqrt(width)
    chirp = np.exp(-1j * PROPAGATION * np.pi * frequency.astype(np.float64) ** 2 / width)
    step = dft.conj() @ (chirp[:, None] * dft)
    step = 0.5 * (step + step.T)
    full = np.stack([block_form(m) for m in (step, step.conj(), dft, dft.conj())])
    high = full.astype(np.float32).astype(ml_dtypes.bfloat16)
    low = (full - high.astype(np.float64)).astype(np.float32).astype(ml_dtypes.bfloat16)
    return np.stack([high, low], axis=1)


def halves(x):
    high = x.astype(jnp.bfloat16)
    return high, (x - high.astype(jnp.float32)).astype(jnp.bfloat16)


def dot(a, b):
    return jnp.dot(a, b, preferred_element_type=jnp.float32)


def times_right(x, high, low):
    x_high, x_low = halves(x)
    return dot(jnp.concatenate([x_high, x_low, x_high], axis=1), jnp.concatenate([high, high, low], axis=0))


def times_left(high, low, x):
    x_high, x_low = halves(x)
    y = dot(jnp.concatenate([high, high, low], axis=1), jnp.concatenate([x_high, x_low, x_high], axis=0))
    n = x.shape[0]
    return y[:n, :n] - y[n:, n:], y[:n, n:] + y[n:, :n]


def both_sides(re, im, tables, which):
    n = re.shape[0]
    y = times_right(jnp.concatenate([re, im], axis=1), tables[which ^ 1, 0], tables[which ^ 1, 1])
    return times_left(tables[which, 0, :, :n], tables[which, 1, :, :n], y)


def share(offsets, tile_rows):
    a = jnp.where(offsets[1] >= offsets[0], 1, 0)
    return a, offsets[2 + a], offsets[1 - a] - offsets[a] + tile_rows, offsets[3 - a]


def cut(tile, row, col, width):
    rows, cols = tile.shape
    part = pltpu.roll(tile, lax.rem(cols - col, cols), 1)[:, :width]
    return pltpu.roll(part, lax.rem(rows - row, rows), 0)


def own_kernel(offsets, objects, tiles, window_b):
    slab, _, rows, _ = objects.shape
    _, _, row_b, col_b = share(offsets, rows)
    for s in range(slab):
        for p in range(2):
            tile = objects[s, p]
            tiles[s, p] = tile
            window_b[s, p] = cut(tile, row_b, col_b, window_b.shape[-1])


def prev_kernel(offsets_prev, after, tiles, window_a, halo):
    slab, _, rows, _ = tiles.shape
    width = halo.shape[-1]
    _, col_a, row_p, col_p = share(offsets_prev, rows)
    for s in range(slab):
        for p in range(2):
            halo[s, p] = cut(tiles[s, p], row_p, col_p, width)
            window_a[s, p] = cut(tiles[s, p], 0, col_a, width)


def rows_here(offsets, rows, cols):
    _, _, row_b, _ = share(offsets, rows)
    return lax.broadcasted_iota(jnp.int32, (rows, cols), 0) < rows - row_b


def join_kernel(offsets, after, window_b, halo, joined):
    slab, _, rows, cols = joined.shape
    inside = rows_here(offsets, rows, cols)
    for s in range(slab):
        for p in range(2):
            joined[s, p] = jnp.where(inside, window_b[s, p], halo[s, p])


def load_kernel(offsets, offsets_prev, intensity, far, probe, measured, start):
    rows = probe.shape[-1]
    near_a, _, _, _ = share(offsets, rows)
    far_a, _, _, _ = share(offsets_prev, rows)
    measured[...] = jnp.where(lax.axis_index("depth") == 1, far[far_a], intensity[1 - near_a])
    start[...] = probe[...]


def wave_kernel(depth_count, offsets, tables, probe, measured, window_a, window_b, halo, *rest):
    others_a, others_b = rest[: depth_count - 1], rest[depth_count - 1 : 2 * depth_count - 2]
    rest = rest[2 * depth_count - 2 :]
    grads, probe_parts = rest[:depth_count], rest[depth_count : 2 * depth_count]
    layers, waves = rest[2 * depth_count :]
    slab = window_a.shape[0]
    n = probe.shape[-1]
    count = slab * depth_count
    depth = lax.axis_index("depth")
    on_a = depth == 1
    inside = rows_here(offsets, n, n)
    for q in range(depth_count):
        of_a = (window_a, *others_a)[(1 - q) % depth_count]
        of_b = others_b[depth_count - 1 - q] if q else None
        for s in range(slab):
            for p in range(2):
                b_layer = of_b[s, p] if q else jnp.where(inside, window_b[s, p], halo[s, p])
                layers[q * slab + s, p] = jnp.where(on_a, of_a[s, p], b_layer)

    def enter(s, re, im):
        waves[s, 0] = re
        waves[s, 1] = im
        o_re, o_im = layers[s, 0], layers[s, 1]
        return re * o_re - im * o_im, re * o_im + im * o_re

    def forward(s, wave):
        return both_sides(*enter(s, *wave), tables, 0)

    wave = lax.fori_loop(0, count - 1, forward, (probe[0], probe[1]), unroll=True if count <= 8 else 1)
    far_re, far_im = both_sides(*enter(count - 1, *wave), tables, 2)
    misfit = 2.0 * (far_re * far_re + far_im * far_im - measured[...])
    chi = both_sides(misfit * far_re, misfit * far_im, tables, 3)

    def leave(s, chi_re, chi_im):
        w_re, w_im = waves[s, 0], waves[s, 1]
        o_re, o_im = layers[s, 0], layers[s, 1]
        waves[s, 0] = w_re * chi_re + w_im * chi_im
        waves[s, 1] = w_re * chi_im - w_im * chi_re
        return o_re * chi_re + o_im * chi_im, o_re * chi_im - o_im * chi_re

    def backward(t, chi):
        return both_sides(*leave(count - 1 - t, *chi), tables, 1)

    chi = lax.fori_loop(0, count - 1, backward, chi, unroll=True if count <= 8 else 1)
    grad = leave(0, *chi)
    _, _, row_b, _ = share(offsets, n)
    turn = lax.rem(jnp.where(on_a, 0, row_b), n)
    for j in range(depth_count):
        base = lax.rem(depth + j, depth_count) * slab
        for s in range(slab):
            for p in range(2):
                grads[j][s, p] = pltpu.roll(waves[base + s, p], turn, 0)
    rows = n // depth_count
    waves[0, 0] = jnp.where(depth < 2, grad[0], 0.0)
    waves[0, 1] = jnp.where(depth < 2, grad[1], 0.0)
    for j in range(depth_count):
        start = pl.multiple_of(lax.rem(depth + j, depth_count) * rows, rows)
        for p in range(2):
            probe_parts[j][p] = waves[0, p, pl.ds(start, rows), :]


def placed(x, col, mask, cols):
    blank = jnp.zeros((x.shape[0], cols - x.shape[1]), x.dtype)
    return pltpu.roll(jnp.concatenate([jnp.where(mask, x, 0.0), blank], axis=1), col, 1)


def place_kernel(depth_count, offsets, offsets_prev, *refs):
    *parts, out = refs
    slab, _, rows, cols = out.shape
    depth = lax.axis_index("depth")
    _, _, row_b, col_b = share(offsets, rows)
    _, col_a, _, _ = share(offsets_prev, rows)
    row_index = lax.broadcasted_iota(jnp.int32, (rows, parts[0].shape[-1]), 0)
    corners = []
    for j in range(depth_count):
        is_b = depth == j
        is_a = lax.rem(depth + depth_count - 1, depth_count) == j
        first = jnp.where(is_a, 0, row_b)
        last = jnp.where(is_a | is_b, rows, 0)
        corners.append((jnp.where(is_a, col_a, col_b), (row_index >= first) & (row_index < last)))
    for s in range(slab):
        for p in range(2):
            total = None
            for (col, mask), part in zip(corners, parts):
                x = placed(part[s, p], col, mask, cols)
                total = x if total is None else total + x
            out[s, p] = total


def step_kernel(depth_count, later, slices, *refs):
    a, b, *parts = refs[later:-2] if slices else refs[later:-1]
    total = refs[-2] if slices else refs[-1]
    total[...] = a[...] + b[...]
    place = lax.axis_index("depth")
    for j, part in enumerate(parts):

        @pl.when(place == j)
        def _():
            for i, s in enumerate(slices):
                refs[-1][i] = part[s]


def spill_kernel(offsets_prev, before, *refs):
    *spills, out, token = refs
    slab, _, rows, cols = out.shape
    _, _, row_p, col_p = share(offsets_prev, rows)
    mask = lax.broadcasted_iota(jnp.int32, (rows, spills[0].shape[-1]), 0) < row_p
    came = [(spill, i) for spill in spills for i in range(spill.shape[0])]
    for s in range(slab):
        for p in range(2):
            out[s, p] = before[s, p] + placed(came[s][0][came[s][1], p], col_p, mask, cols)
    token[...] = jnp.zeros_like(token)


def call(kernel, name, scalars, arrays, outs, scratch=(), work=10**9, after=()):
    vmem = pl.BlockSpec(memory_space=pltpu.VMEM)
    moved = sum(math.prod(x.shape) * x.dtype.itemsize for x in (*arrays, *outs))
    return pl.pallas_call(
        kernel,
        name=name,
        out_shape=outs,
        in_specs=[pl.BlockSpec(memory_space=pltpu.SMEM)] * len(scalars)
        + [pl.BlockSpec(memory_space=pl.ANY)] * len(after)
        + [vmem] * len(arrays),
        out_specs=[vmem] * len(outs),
        scratch_shapes=scratch,
        compiler_params=pltpu.CompilerParams(vmem_limit_bytes=VMEM_LIMIT),
        cost_estimate=pl.CostEstimate(flops=work, bytes_accessed=moved, transcendentals=0),
    )(*scalars, *after, *arrays)


def sum_round(x, level):
    depth_count, scan_count = lax.axis_size("depth"), lax.axis_size("scan")
    levels = scan_count.bit_length() - 1
    route = []
    for d in range(depth_count):
        step = 1 << ((level + (d % 2) * (levels // 2)) % levels)
        route += [(d * scan_count + i, d * scan_count + (i ^ step)) for i in range(scan_count)]
    return lax.ppermute(x, ("depth", "scan"), route)


def body(objects, probe, row_offsets, col_offsets, intensity):
    slab = objects.shape[0]
    n = probe.shape[-1]
    depth_count, scan_count = lax.axis_size("depth"), lax.axis_size("scan")
    f32 = jnp.float32

    def across(x, source, target, shift):
        route = [(source * scan_count + i, target * scan_count + (i + shift) % scan_count) for i in range(scan_count)]
        return lax.ppermute(x, ("depth", "scan"), route)

    offsets = jnp.concatenate([row_offsets, col_offsets])
    offsets_prev = lax.ppermute(offsets, "scan", [(i, (i + 1) % scan_count) for i in range(scan_count)])
    far = across(intensity, 0, 1, 1)
    window = jax.ShapeDtypeStruct((slab, 2, n, n), f32)
    whole = jax.ShapeDtypeStruct(objects.shape, f32)
    tiles, window_b = call(own_kernel, "own", [offsets], [objects], [whole, window])
    window_a, halo = call(prev_kernel, "prev", [offsets_prev], [tiles], [window] * 2, after=[far])
    halo_0 = across(halo, 0, 0, -1)
    route = [
        (d * scan_count + (i + 1) % scan_count, d * scan_count + i) for d in range(1, depth_count) for i in range(scan_count)
    ]
    halo = lax.ppermute(halo, ("depth", "scan"), route)

    def gathered(x, target):
        return [lax.ppermute(x, "depth", [((target - j) % depth_count, target)]) for j in range(1, depth_count)]

    others_a = gathered(window_a, 1)
    measured, start = call(
        load_kernel,
        "load",
        [offsets, offsets_prev],
        [intensity, far, probe],
        [jax.ShapeDtypeStruct((n, n), f32), jax.ShapeDtypeStruct(probe.shape, f32)],
    )

    (joined,) = call(join_kernel, "join", [offsets], [window_b, halo], [window], after=[measured])
    others_b = gathered(joined, 0)

    tables = jnp.asarray(constant_tables(n))
    count = slab * depth_count
    parts = call(
        lambda *refs: wave_kernel(depth_count, *refs),
        "wave",
        [offsets],
        [tables, start, measured, window_a, window_b, halo_0, *others_a, *others_b],
        [window] * depth_count + [jax.ShapeDtypeStruct((2, n // depth_count, n), f32)] * depth_count,
        [pltpu.VMEM((count, 2, n, n), f32)] * 2,
        work=5 * 10**9,
    )
    grads, probe_parts = parts[:depth_count], parts[depth_count:]

    back, sums = [grads[0]], [probe_parts[0]]
    for j in range(1, depth_count):
        sums.append(lax.ppermute(probe_parts[j], "depth", [(t, (t + j) % depth_count) for t in range(depth_count)]))
        back.append(lax.ppermute(grads[j], "depth", [(t, (t + j) % depth_count) for t in (0, 1)]))

    half = jax.ShapeDtypeStruct(sums[0].shape, f32)
    ahead = [(i, (i + 1) % scan_count) for i in range(scan_count)]
    rounds = scan_count.bit_length() - 1
    paired = scan_count == 1 << rounds and rounds > 2
    spill = []

    def step(a, b, slices, after):
        outs = [half, jax.ShapeDtypeStruct((len(slices), 2, n, n), f32)] if slices else [half]
        return call(
            lambda *refs: step_kernel(depth_count, len(after), slices, *refs),
            "step",
            [],
            [a, b, *(back if slices else [])],
            outs,
            after=after,
        )

    (object_grad,) = call(
        lambda *refs: place_kernel(depth_count, *refs),
        "place",
        [offsets, offsets_prev],
        back,
        [whole],
        work=2 * 10**9,
    )
    turns = rounds - 1 if paired else 1
    cuts = [0, slab // 3] + [slab] * (turns - 1) if turns > 1 else [0, slab]
    share_of = [tuple(range(cuts[k], cuts[k + 1])) for k in range(turns)]
    total = sums[0]
    for x in sums[1:-1]:
        total = total + x
    other = sums[-1] if depth_count > 1 else jnp.zeros_like(total)
    for k, slices in enumerate(share_of):
        total, *payload = step(total, other, slices, spill[:1] if k == 2 else [])
        other = sum_round(total, k) if paired else jnp.zeros_like(total)
        spill += [lax.ppermute(x, "scan", ahead) for x in payload]
    if paired:
        (total,) = step(total, other, (), [object_grad])
        other = sum_round(total, rounds - 1)
    object_grad, token = call(
        spill_kernel, "spill", [offsets_prev], [object_grad, *spill], [whole, jax.ShapeDtypeStruct((8, n), f32)]
    )
    if paired:
        (total,) = step(total, other, (), [token])
    else:
        total = lax.psum(total, "scan")
    return object_grad, total


def solution(mesh):
    in_specs = (P("depth", None, "scan", None), P(), P("scan"), P("scan"), P("scan", None, None))
    out_specs = (P("depth", None, "scan", None), P(None, "depth", None))
    return jax.shard_map(body, mesh=mesh, in_specs=in_specs, out_specs=out_specs, check_vma=False)
```

```python
import math

import jax
import jax.numpy as jnp
import ml_dtypes
import numpy as np
from jax import lax
from jax.experimental import pallas as pl
from jax.experimental.pallas import tpu as pltpu
from jax.sharding import PartitionSpec as P

PROPAGATION = 0.5
VMEM_LIMIT = 48 * 1024 * 1024


def block_form(matrix):
    return np.block([[matrix.real, -matrix.imag], [matrix.imag, matrix.real]])


def constant_tables(width):
    grid = np.arange(width)
    frequency = np.where(grid < width // 2, grid, grid - width)
    dft = np.exp(-2j * np.pi * ((grid[:, None] * grid[None, :]) % width) / width) / math.sqrt(width)
    chirp = np.exp(-1j * PROPAGATION * np.pi * frequency.astype(np.float64) ** 2 / width)
    step = dft.conj() @ (chirp[:, None] * dft)
    step = 0.5 * (step + step.T)
    full = np.stack([block_form(m) for m in (step, step.conj(), dft, dft.conj())])
    high = full.astype(np.float32).astype(ml_dtypes.bfloat16)
    low = (full - high.astype(np.float64)).astype(np.float32).astype(ml_dtypes.bfloat16)
    return np.stack([high, low], axis=1)


def halves(x):
    high = x.astype(jnp.bfloat16)
    return high, (x - high.astype(jnp.float32)).astype(jnp.bfloat16)


def dot(a, b):
    return jnp.dot(a, b, preferred_element_type=jnp.float32)


def times_right(x, high, low):
    x_high, x_low = halves(x)
    return dot(jnp.concatenate([x_high, x_low, x_high], axis=1), jnp.concatenate([high, high, low], axis=0))


def times_left(high, low, x):
    x_high, x_low = halves(x)
    y = dot(jnp.concatenate([high, high, low], axis=1), jnp.concatenate([x_high, x_low, x_high], axis=0))
    n = x.shape[0]
    return y[:n, :n] - y[n:, n:], y[:n, n:] + y[n:, :n]


def both_sides(re, im, tables, which):
    n = re.shape[0]
    y = times_right(jnp.concatenate([re, im], axis=1), tables[which ^ 1, 0], tables[which ^ 1, 1])
    return times_left(tables[which, 0, :, :n], tables[which, 1, :, :n], y)


def share(offsets, tile_rows):
    a = jnp.where(offsets[1] >= offsets[0], 1, 0)
    return a, offsets[2 + a], offsets[1 - a] - offsets[a] + tile_rows, offsets[3 - a]


def cut(tile, row, col, width):
    rows, cols = tile.shape
    part = pltpu.roll(tile, lax.rem(cols - col, cols), 1)[:, :width]
    return pltpu.roll(part, lax.rem(rows - row, rows), 0)


def own_kernel(offsets, objects, tiles, window_b):
    slab, _, rows, _ = objects.shape
    _, _, row_b, col_b = share(offsets, rows)
    for s in range(slab):
        for p in range(2):
            tile = objects[s, p]
            tiles[s, p] = tile
            window_b[s, p] = cut(tile, row_b, col_b, window_b.shape[-1])


def prev_kernel(offsets_prev, after, tiles, window_a, halo):
    slab, _, rows, _ = tiles.shape
    width = halo.shape[-1]
    _, col_a, row_p, col_p = share(offsets_prev, rows)
    for s in range(slab):
        for p in range(2):
            halo[s, p] = cut(tiles[s, p], row_p, col_p, width)
            window_a[s, p] = cut(tiles[s, p], 0, col_a, width)


def hold_kernel(after, x, out):
    out[...] = x[...]


def load_kernel(offsets, offsets_prev, intensity, far, probe, measured, start):
    rows = probe.shape[-1]
    near_a, _, _, _ = share(offsets, rows)
    far_a, _, _, _ = share(offsets_prev, rows)
    measured[...] = jnp.where(lax.axis_index("depth") == 0, far[far_a], intensity[1 - near_a])
    start[...] = probe[...]


def wave_kernel(depth_count, offsets, tables, probe, measured, window_a, window_b, halo, *rest):
    others_a, others_b, halos = (rest[(depth_count - 1) * k : (depth_count - 1) * (k + 1)] for k in range(3))
    rest = rest[3 * depth_count - 3 :]
    grads, probe_parts = rest[:depth_count], rest[depth_count : 2 * depth_count]
    layers, waves = rest[2 * depth_count :]
    slab = window_a.shape[0]
    n = probe.shape[-1]
    count = slab * depth_count
    depth = lax.axis_index("depth")
    on_a = depth == 0
    _, _, row_b, _ = share(offsets, n)
    inside = lax.broadcasted_iota(jnp.int32, (n, n), 0) < n - row_b
    for q in range(depth_count):
        of_a = (window_a, *others_a)[-q % depth_count]
        of_b, below = (window_b, *others_b)[(1 - q) % depth_count], (halo, *halos)[(1 - q) % depth_count]
        for s in range(slab):
            for p in range(2):
                b_layer = jnp.where(inside, of_b[s, p], below[s, p])
                layers[q * slab + s, p] = jnp.where(on_a, of_a[s, p], b_layer)

    def enter(s, re, im):
        waves[s, 0] = re
        waves[s, 1] = im
        o_re, o_im = layers[s, 0], layers[s, 1]
        return re * o_re - im * o_im, re * o_im + im * o_re

    def forward(s, wave):
        return both_sides(*enter(s, *wave), tables, 0)

    wave = lax.fori_loop(0, count - 1, forward, (probe[0], probe[1]), unroll=True if count <= 8 else 1)
    far_re, far_im = both_sides(*enter(count - 1, *wave), tables, 2)
    misfit = 2.0 * (far_re * far_re + far_im * far_im - measured[...])
    chi = both_sides(misfit * far_re, misfit * far_im, tables, 3)

    def leave(s, chi_re, chi_im):
        w_re, w_im = waves[s, 0], waves[s, 1]
        o_re, o_im = layers[s, 0], layers[s, 1]
        waves[s, 0] = w_re * chi_re + w_im * chi_im
        waves[s, 1] = w_re * chi_im - w_im * chi_re
        return o_re * chi_re + o_im * chi_im, o_re * chi_im - o_im * chi_re

    def backward(t, chi):
        return both_sides(*leave(count - 1 - t, *chi), tables, 1)

    chi = lax.fori_loop(0, count - 1, backward, chi, unroll=True if count <= 8 else 1)
    grad = leave(0, *chi)
    turn = lax.rem(jnp.where(on_a, 0, row_b), n)
    for j in range(depth_count):
        base = lax.rem(depth + j, depth_count) * slab
        for s in range(slab):
            for p in range(2):
                grads[j][s, p] = pltpu.roll(waves[base + s, p], turn, 0)
    rows = n // depth_count
    waves[0, 0] = jnp.where(depth < 2, grad[0], 0.0)
    waves[0, 1] = jnp.where(depth < 2, grad[1], 0.0)
    for j in range(depth_count):
        start = pl.multiple_of(lax.rem(depth + j, depth_count) * rows, rows)
        for p in range(2):
            probe_parts[j][p] = waves[0, p, pl.ds(start, rows), :]


def placed(x, col, mask, cols):
    blank = jnp.zeros((x.shape[0], cols - x.shape[1]), x.dtype)
    return pltpu.roll(jnp.concatenate([jnp.where(mask, x, 0.0), blank], axis=1), col, 1)


def place_kernel(depth_count, offsets, offsets_prev, *refs):
    *parts, out = refs
    slab, _, rows, cols = out.shape
    depth = lax.axis_index("depth")
    _, _, row_b, col_b = share(offsets, rows)
    _, col_a, _, _ = share(offsets_prev, rows)
    row_index = lax.broadcasted_iota(jnp.int32, (rows, parts[0].shape[-1]), 0)
    corners = []
    for j in range(depth_count):
        is_a = depth == j
        is_b = lax.rem(depth + depth_count - 1, depth_count) == j
        first = jnp.where(is_a, 0, row_b)
        last = jnp.where(is_a | is_b, rows, 0)
        corners.append((jnp.where(is_a, col_a, col_b), (row_index >= first) & (row_index < last)))
    for s in range(slab):
        for p in range(2):
            total = None
            for (col, mask), part in zip(corners, parts):
                x = placed(part[s, p], col, mask, cols)
                total = x if total is None else total + x
            out[s, p] = total


def step_kernel(depth_count, later, slices, *refs):
    a, b, *parts = refs[later:-2] if slices else refs[later:-1]
    total = refs[-2] if slices else refs[-1]
    total[...] = a[...] + b[...]
    place = lax.rem(lax.axis_index("depth") + depth_count - 1, depth_count)
    for j, part in enumerate(parts):

        @pl.when(place == j)
        def _():
            for i, s in enumerate(slices):
                refs[-1][i] = part[s]


def spill_kernel(offsets_prev, before, *refs):
    *spills, out, token = refs
    slab, _, rows, cols = out.shape
    _, _, row_p, col_p = share(offsets_prev, rows)
    mask = lax.broadcasted_iota(jnp.int32, (rows, spills[0].shape[-1]), 0) < row_p
    came = [(spill, i) for spill in spills for i in range(spill.shape[0])]
    for s in range(slab):
        for p in range(2):
            out[s, p] = before[s, p] + placed(came[s][0][came[s][1], p], col_p, mask, cols)
    token[...] = jnp.zeros_like(token)


def call(kernel, name, scalars, arrays, outs, scratch=(), work=10**9, after=()):
    vmem = pl.BlockSpec(memory_space=pltpu.VMEM)
    moved = sum(math.prod(x.shape) * x.dtype.itemsize for x in (*arrays, *outs))
    return pl.pallas_call(
        kernel,
        name=name,
        out_shape=outs,
        in_specs=[pl.BlockSpec(memory_space=pltpu.SMEM)] * len(scalars)
        + [pl.BlockSpec(memory_space=pl.ANY)] * len(after)
        + [vmem] * len(arrays),
        out_specs=[vmem] * len(outs),
        scratch_shapes=scratch,
        compiler_params=pltpu.CompilerParams(vmem_limit_bytes=VMEM_LIMIT),
        cost_estimate=pl.CostEstimate(flops=work, bytes_accessed=moved, transcendentals=0),
    )(*scalars, *after, *arrays)


def sum_round(x, level):
    depth_count, scan_count = lax.axis_size("depth"), lax.axis_size("scan")
    levels = scan_count.bit_length() - 1
    route = []
    for d in range(depth_count):
        step = 1 << ((level + (d % 2) * (levels // 2)) % levels)
        route += [(d * scan_count + i, d * scan_count + (i ^ step)) for i in range(scan_count)]
    return lax.ppermute(x, ("depth", "scan"), route)


def body(objects, probe, row_offsets, col_offsets, intensity):
    slab = objects.shape[0]
    n = probe.shape[-1]
    depth_count, scan_count = lax.axis_size("depth"), lax.axis_size("scan")
    f32 = jnp.float32

    def across(x, source, target, shift):
        route = [(source * scan_count + i, target * scan_count + (i + shift) % scan_count) for i in range(scan_count)]
        return lax.ppermute(x, ("depth", "scan"), route)

    offsets = jnp.concatenate([row_offsets, col_offsets])
    offsets_prev = lax.ppermute(offsets, "scan", [(i, (i + 1) % scan_count) for i in range(scan_count)])
    far = across(intensity, 0, 0, 1)
    window = jax.ShapeDtypeStruct((slab, 2, n, n), f32)
    whole = jax.ShapeDtypeStruct(objects.shape, f32)
    tiles, window_b = call(own_kernel, "own", [offsets], [objects], [whole, window])
    window_a, halo = call(prev_kernel, "prev", [offsets_prev], [tiles], [window] * 2, after=[far])
    halo = lax.ppermute(halo, "scan", [((i + 1) % scan_count, i) for i in range(scan_count)])

    def gathered(x, target):
        return [lax.ppermute(x, "depth", [((target - j) % depth_count, target)]) for j in range(1, depth_count)]

    others_a = gathered(window_a, 0)
    measured, start = call(
        load_kernel,
        "load",
        [offsets, offsets_prev],
        [intensity, far, probe],
        [jax.ShapeDtypeStruct((n, n), f32), jax.ShapeDtypeStruct(probe.shape, f32)],
    )

    (halo,) = call(hold_kernel, "hold", [], [halo], [window], after=[measured])
    others_b, halos = gathered(window_b, 1), gathered(halo, 1)

    tables = jnp.asarray(constant_tables(n))
    count = slab * depth_count
    parts = call(
        lambda *refs: wave_kernel(depth_count, *refs),
        "wave",
        [offsets],
        [tables, start, measured, window_a, window_b, halo, *others_a, *others_b, *halos],
        [window] * depth_count + [jax.ShapeDtypeStruct((2, n // depth_count, n), f32)] * depth_count,
        [pltpu.VMEM((count, 2, n, n), f32)] * 2,
        work=5 * 10**9,
    )
    grads, probe_parts = parts[:depth_count], parts[depth_count:]

    back, sums = [grads[0]], [probe_parts[0]]
    for j in range(1, depth_count):
        sums.append(lax.ppermute(probe_parts[j], "depth", [(t, (t + j) % depth_count) for t in range(depth_count)]))
        back.append(lax.ppermute(grads[j], "depth", [(t, (t + j) % depth_count) for t in (0, 1)]))

    half = jax.ShapeDtypeStruct(sums[0].shape, f32)
    ahead = [(i, (i + 1) % scan_count) for i in range(scan_count)]
    rounds = scan_count.bit_length() - 1
    paired = scan_count == 1 << rounds and rounds > 2
    spill = []

    def step(a, b, slices, after):
        outs = [half, jax.ShapeDtypeStruct((len(slices), 2, n, n), f32)] if slices else [half]
        return call(
            lambda *refs: step_kernel(depth_count, len(after), slices, *refs),
            "step",
            [],
            [a, b, *(back if slices else [])],
            outs,
            after=after,
        )

    (object_grad,) = call(
        lambda *refs: place_kernel(depth_count, *refs),
        "place",
        [offsets, offsets_prev],
        back,
        [whole],
        work=2 * 10**9,
    )
    turns = rounds - 1 if paired else 1
    cuts = [0, slab // 3] + [slab] * (turns - 1) if turns > 1 else [0, slab]
    share_of = [tuple(range(cuts[k], cuts[k + 1])) for k in range(turns)]
    total = sums[0]
    for x in sums[1:-1]:
        total = total + x
    other = sums[-1] if depth_count > 1 else jnp.zeros_like(total)
    for k, slices in enumerate(share_of):
        total, *payload = step(total, other, slices, spill[:1] if k == 2 else [])
        other = sum_round(total, k) if paired else jnp.zeros_like(total)
        spill += [lax.ppermute(x, "scan", ahead) for x in payload]
    if paired:
        (total,) = step(total, other, (), [object_grad])
        other = sum_round(total, rounds - 1)
    object_grad, token = call(
        spill_kernel, "spill", [offsets_prev], [object_grad, *spill], [whole, jax.ShapeDtypeStruct((8, n), f32)]
    )
    if paired:
        (total,) = step(total, other, (), [token])
    else:
        total = lax.psum(total, "scan")
    return object_grad, total


def solution(mesh):
    in_specs = (P("depth", None, "scan", None), P(), P("scan"), P("scan"), P("scan", None, None))
    out_specs = (P("depth", None, "scan", None), P(None, "depth", None))
    return jax.shard_map(body, mesh=mesh, in_specs=in_specs, out_specs=out_specs, check_vma=False)
```

```python
import math

import jax
import jax.numpy as jnp
import ml_dtypes
import numpy as np
from jax import lax
from jax.experimental import pallas as pl
from jax.experimental.pallas import tpu as pltpu
from jax.sharding import PartitionSpec as P

PROPAGATION = 0.5
VMEM_LIMIT = 48 * 1024 * 1024


def block_form(matrix):
    return np.block([[matrix.real, -matrix.imag], [matrix.imag, matrix.real]])


def constant_tables(width):
    grid = np.arange(width)
    frequency = np.where(grid < width // 2, grid, grid - width)
    dft = np.exp(-2j * np.pi * ((grid[:, None] * grid[None, :]) % width) / width) / math.sqrt(width)
    chirp = np.exp(-1j * PROPAGATION * np.pi * frequency.astype(np.float64) ** 2 / width)
    step = dft.conj() @ (chirp[:, None] * dft)
    step = 0.5 * (step + step.T)
    full = np.stack([block_form(m) for m in (step, step.conj(), dft, dft.conj())])
    high = full.astype(np.float32).astype(ml_dtypes.bfloat16)
    low = (full - high.astype(np.float64)).astype(np.float32).astype(ml_dtypes.bfloat16)
    return np.stack([high, low], axis=1)


def halves(x):
    high = x.astype(jnp.bfloat16)
    return high, (x - high.astype(jnp.float32)).astype(jnp.bfloat16)


def dot(a, b):
    return jnp.dot(a, b, preferred_element_type=jnp.float32)


def times_right(x, high, low):
    x_high, x_low = halves(x)
    return dot(jnp.concatenate([x_high, x_low, x_high], axis=1), jnp.concatenate([high, high, low], axis=0))


def times_left(high, low, x):
    x_high, x_low = halves(x)
    y = dot(jnp.concatenate([high, high, low], axis=1), jnp.concatenate([x_high, x_low, x_high], axis=0))
    n = x.shape[0]
    return y[:n, :n] - y[n:, n:], y[:n, n:] + y[n:, :n]


def both_sides(re, im, tables, which):
    n = re.shape[0]
    y = times_right(jnp.concatenate([re, im], axis=1), tables[which ^ 1, 0], tables[which ^ 1, 1])
    return times_left(tables[which, 0, :, :n], tables[which, 1, :, :n], y)


def share(offsets, tile_rows):
    a = jnp.where(offsets[1] >= offsets[0], 1, 0)
    return a, offsets[2 + a], offsets[1 - a] - offsets[a] + tile_rows, offsets[3 - a]


def cut(tile, row, col, width):
    rows, cols = tile.shape
    part = pltpu.roll(tile, lax.rem(cols - col, cols), 1)[:, :width]
    return pltpu.roll(part, lax.rem(rows - row, rows), 0)


def own_kernel(offsets, objects, tiles, window_b):
    slab, _, rows, _ = objects.shape
    _, _, row_b, col_b = share(offsets, rows)
    for s in range(slab):
        for p in range(2):
            tile = objects[s, p]
            tiles[s, p] = tile
            window_b[s, p] = cut(tile, row_b, col_b, window_b.shape[-1])


def prev_kernel(offsets_prev, tiles, far, packed, halo):
    slab, _, rows, _ = tiles.shape
    width = halo.shape[-1]
    a, col_a, row_p, col_p = share(offsets_prev, rows)
    packed[2 * slab] = far[a]
    for s in range(slab):
        for p in range(2):
            halo[s, p] = cut(tiles[s, p], row_p, col_p, width)
            packed[2 * s + p] = cut(tiles[s, p], 0, col_a, width)


def rows_here(offsets, rows, cols):
    _, _, row_b, _ = share(offsets, rows)
    return lax.broadcasted_iota(jnp.int32, (rows, cols), 0) < rows - row_b


def join_kernel(offsets, after, window_b, halo, joined):
    slab, _, rows, cols = joined.shape
    inside = rows_here(offsets, rows, cols)
    for s in range(slab):
        for p in range(2):
            joined[s, p] = jnp.where(inside, window_b[s, p], halo[s, p])


def load_kernel(offsets, after, intensity, probe, near, start):
    a, _, _, _ = share(offsets, probe.shape[-1])
    near[...] = intensity[1 - a]
    start[...] = probe[...]


def wave_kernel(depth_count, offsets, tables, probe, near, packed, window_b, halo, *rest):
    others_a, others_b = rest[: depth_count - 1], rest[depth_count - 1 : 2 * depth_count - 2]
    rest = rest[2 * depth_count - 2 :]
    grads, probe_parts = rest[:depth_count], rest[depth_count : 2 * depth_count]
    layers, waves = rest[2 * depth_count :]
    slab = window_b.shape[0]
    n = probe.shape[-1]
    count = slab * depth_count
    depth = lax.axis_index("depth")
    on_a = depth == 1
    _, _, row_b, _ = share(offsets, n)
    inside = rows_here(offsets, n, n)
    for q in range(depth_count):
        of_a = (packed, *others_a)[(1 - q) % depth_count]
        of_b = (window_b, *others_b)[-q % depth_count]
        for s in range(slab):
            for p in range(2):
                b_layer = of_b[s, p] if q else jnp.where(inside, of_b[s, p], halo[s, p])
                layers[q * slab + s, p] = jnp.where(on_a, of_a[2 * s + p], b_layer)

    def enter(s, re, im):
        waves[s, 0] = re
        waves[s, 1] = im
        o_re, o_im = layers[s, 0], layers[s, 1]
        return re * o_re - im * o_im, re * o_im + im * o_re

    def forward(s, wave):
        return both_sides(*enter(s, *wave), tables, 0)

    wave = lax.fori_loop(0, count - 1, forward, (probe[0], probe[1]), unroll=True if count <= 8 else 1)
    far_re, far_im = both_sides(*enter(count - 1, *wave), tables, 2)
    measured = jnp.where(on_a, others_a[0][2 * slab], near[...])
    misfit = 2.0 * (far_re * far_re + far_im * far_im - measured)
    chi = both_sides(misfit * far_re, misfit * far_im, tables, 3)

    def leave(s, chi_re, chi_im):
        w_re, w_im = waves[s, 0], waves[s, 1]
        o_re, o_im = layers[s, 0], layers[s, 1]
        waves[s, 0] = w_re * chi_re + w_im * chi_im
        waves[s, 1] = w_re * chi_im - w_im * chi_re
        return o_re * chi_re + o_im * chi_im, o_re * chi_im - o_im * chi_re

    def backward(t, chi):
        return both_sides(*leave(count - 1 - t, *chi), tables, 1)

    chi = lax.fori_loop(0, count - 1, backward, chi, unroll=True if count <= 8 else 1)
    grad = leave(0, *chi)
    turn = lax.rem(jnp.where(on_a, 0, row_b), n)
    for j in range(depth_count):
        base = lax.rem(depth + j, depth_count) * slab
        for s in range(slab):
            for p in range(2):
                grads[j][s, p] = pltpu.roll(waves[base + s, p], turn, 0)
    rows = n // depth_count
    waves[0, 0] = jnp.where(depth < 2, grad[0], 0.0)
    waves[0, 1] = jnp.where(depth < 2, grad[1], 0.0)
    for j in range(depth_count):
        start = pl.multiple_of(lax.rem(depth + j, depth_count) * rows, rows)
        for p in range(2):
            probe_parts[j][p] = waves[0, p, pl.ds(start, rows), :]


def placed(x, col, mask, cols):
    blank = jnp.zeros((x.shape[0], cols - x.shape[1]), x.dtype)
    return pltpu.roll(jnp.concatenate([jnp.where(mask, x, 0.0), blank], axis=1), col, 1)


def place_kernel(depth_count, offsets, offsets_prev, *refs):
    *parts, out = refs
    slab, _, rows, cols = out.shape
    depth = lax.axis_index("depth")
    _, _, row_b, col_b = share(offsets, rows)
    _, col_a, _, _ = share(offsets_prev, rows)
    row_index = lax.broadcasted_iota(jnp.int32, (rows, parts[0].shape[-1]), 0)
    corners = []
    for j in range(depth_count):
        is_b = depth == j
        is_a = lax.rem(depth + depth_count - 1, depth_count) == j
        first = jnp.where(is_a, 0, row_b)
        last = jnp.where(is_a | is_b, rows, 0)
        corners.append((jnp.where(is_a, col_a, col_b), (row_index >= first) & (row_index < last)))
    for s in range(slab):
        for p in range(2):
            total = None
            for (col, mask), part in zip(corners, parts):
                x = placed(part[s, p], col, mask, cols)
                total = x if total is None else total + x
            out[s, p] = total


def step_kernel(depth_count, later, slices, *refs):
    a, b, *parts = refs[later:-2] if slices else refs[later:-1]
    total = refs[-2] if slices else refs[-1]
    total[...] = a[...] + b[...]
    place = lax.axis_index("depth")
    for j, part in enumerate(parts):

        @pl.when(place == j)
        def _():
            for i, s in enumerate(slices):
                refs[-1][i] = part[s]


def spill_kernel(offsets_prev, before, *refs):
    *spills, out, token = refs
    slab, _, rows, cols = out.shape
    _, _, row_p, col_p = share(offsets_prev, rows)
    mask = lax.broadcasted_iota(jnp.int32, (rows, spills[0].shape[-1]), 0) < row_p
    came = [(spill, i) for spill in spills for i in range(spill.shape[0])]
    for s in range(slab):
        for p in range(2):
            out[s, p] = before[s, p] + placed(came[s][0][came[s][1], p], col_p, mask, cols)
    token[...] = jnp.zeros_like(token)


def call(kernel, name, scalars, arrays, outs, scratch=(), work=10**9, after=()):
    vmem = pl.BlockSpec(memory_space=pltpu.VMEM)
    moved = sum(math.prod(x.shape) * x.dtype.itemsize for x in (*arrays, *outs))
    return pl.pallas_call(
        kernel,
        name=name,
        out_shape=outs,
        in_specs=[pl.BlockSpec(memory_space=pltpu.SMEM)] * len(scalars)
        + [pl.BlockSpec(memory_space=pl.ANY)] * len(after)
        + [vmem] * len(arrays),
        out_specs=[vmem] * len(outs),
        scratch_shapes=scratch,
        compiler_params=pltpu.CompilerParams(vmem_limit_bytes=VMEM_LIMIT),
        cost_estimate=pl.CostEstimate(flops=work, bytes_accessed=moved, transcendentals=0),
    )(*scalars, *after, *arrays)


def sum_round(x, level):
    depth_count, scan_count = lax.axis_size("depth"), lax.axis_size("scan")
    levels = scan_count.bit_length() - 1
    route = []
    for d in range(depth_count):
        step = 1 << ((level + (d % 2) * (levels // 2)) % levels)
        route += [(d * scan_count + i, d * scan_count + (i ^ step)) for i in range(scan_count)]
    return lax.ppermute(x, ("depth", "scan"), route)


def body(objects, probe, row_offsets, col_offsets, intensity):
    slab = objects.shape[0]
    n = probe.shape[-1]
    depth_count, scan_count = lax.axis_size("depth"), lax.axis_size("scan")
    f32 = jnp.float32

    def across(x, source, target, shift):
        route = [(source * scan_count + i, target * scan_count + (i + shift) % scan_count) for i in range(scan_count)]
        return lax.ppermute(x, ("depth", "scan"), route)

    offsets = jnp.concatenate([row_offsets, col_offsets])
    offsets_prev = lax.ppermute(offsets, "scan", [(i, (i + 1) % scan_count) for i in range(scan_count)])
    far = across(intensity, 0, 0, 1)
    window = jax.ShapeDtypeStruct((slab, 2, n, n), f32)
    whole = jax.ShapeDtypeStruct(objects.shape, f32)
    tiles, window_b = call(own_kernel, "own", [offsets], [objects], [whole, window])
    packed, halo = call(
        prev_kernel, "prev", [offsets_prev], [tiles, far], [jax.ShapeDtypeStruct((2 * slab + 1, n, n), f32), window]
    )
    halo_0 = across(halo, 0, 0, -1)
    route = [
        (d * scan_count + (i + 1) % scan_count, d * scan_count + i) for d in range(1, depth_count) for i in range(scan_count)
    ]
    halo = lax.ppermute(halo, ("depth", "scan"), route)

    def gathered(x, target):
        return [lax.ppermute(x, "depth", [((target - j) % depth_count, target)]) for j in range(1, depth_count)]

    others_a = gathered(packed, 1)
    near, start = call(
        load_kernel,
        "load",
        [offsets],
        [intensity, probe],
        [jax.ShapeDtypeStruct((n, n), f32), jax.ShapeDtypeStruct(probe.shape, f32)],
        after=others_a[:1],
    )
    (joined,) = call(join_kernel, "join", [offsets], [window_b, halo], [window], after=[near])
    others_b = gathered(joined, 0)

    tables = jnp.asarray(constant_tables(n))
    count = slab * depth_count
    parts = call(
        lambda *refs: wave_kernel(depth_count, *refs),
        "wave",
        [offsets],
        [tables, start, near, packed, window_b, halo_0, *others_a, *others_b],
        [window] * depth_count + [jax.ShapeDtypeStruct((2, n // depth_count, n), f32)] * depth_count,
        [pltpu.VMEM((count, 2, n, n), f32)] * 2,
        work=5 * 10**9,
    )
    grads, probe_parts = parts[:depth_count], parts[depth_count:]

    back, sums = [grads[0]], [probe_parts[0]]
    for j in range(1, depth_count):
        sums.append(lax.ppermute(probe_parts[j], "depth", [(t, (t + j) % depth_count) for t in range(depth_count)]))
        back.append(lax.ppermute(grads[j], "depth", [(t, (t + j) % depth_count) for t in (0, 1)]))

    half = jax.ShapeDtypeStruct(sums[0].shape, f32)
    ahead = [(i, (i + 1) % scan_count) for i in range(scan_count)]
    rounds = scan_count.bit_length() - 1
    paired = scan_count == 1 << rounds and rounds > 2
    spill = []

    def step(a, b, slices, after):
        outs = [half, jax.ShapeDtypeStruct((len(slices), 2, n, n), f32)] if slices else [half]
        return call(
            lambda *refs: step_kernel(depth_count, len(after), slices, *refs),
            "step",
            [],
            [a, b, *(back if slices else [])],
            outs,
            after=after,
        )

    (object_grad,) = call(
        lambda *refs: place_kernel(depth_count, *refs),
        "place",
        [offsets, offsets_prev],
        back,
        [whole],
        work=2 * 10**9,
    )
    turns = rounds - 1 if paired else 1
    cuts = [0, slab // 3] + [slab] * (turns - 1) if turns > 1 else [0, slab]
    share_of = [tuple(range(cuts[k], cuts[k + 1])) for k in range(turns)]
    total = sums[0]
    for x in sums[1:-1]:
        total = total + x
    other = sums[-1] if depth_count > 1 else jnp.zeros_like(total)
    for k, slices in enumerate(share_of):
        total, *payload = step(total, other, slices, spill[:1] if k == 2 else [])
        other = sum_round(total, k) if paired else jnp.zeros_like(total)
        spill += [lax.ppermute(x, "scan", ahead) for x in payload]
    if paired:
        (total,) = step(total, other, (), [object_grad])
        other = sum_round(total, rounds - 1)
    object_grad, token = call(
        spill_kernel, "spill", [offsets_prev], [object_grad, *spill], [whole, jax.ShapeDtypeStruct((8, n), f32)]
    )
    if paired:
        (total,) = step(total, other, (), [token])
    else:
        total = lax.psum(total, "scan")
    return object_grad, total


def solution(mesh):
    in_specs = (P("depth", None, "scan", None), P(), P("scan"), P("scan"), P("scan", None, None))
    out_specs = (P("depth", None, "scan", None), P(None, "depth", None))
    return jax.shard_map(body, mesh=mesh, in_specs=in_specs, out_specs=out_specs, check_vma=False)
```

```python
import math

import jax
import jax.numpy as jnp
import ml_dtypes
import numpy as np
from jax import lax
from jax.experimental import pallas as pl
from jax.experimental.pallas import tpu as pltpu
from jax.sharding import PartitionSpec as P

PROPAGATION = 0.5
VMEM_LIMIT = 48 * 1024 * 1024


def block_form(matrix):
    return np.block([[matrix.real, -matrix.imag], [matrix.imag, matrix.real]])


def constant_tables(width):
    grid = np.arange(width)
    frequency = np.where(grid < width // 2, grid, grid - width)
    dft = np.exp(-2j * np.pi * ((grid[:, None] * grid[None, :]) % width) / width) / math.sqrt(width)
    chirp = np.exp(-1j * PROPAGATION * np.pi * frequency.astype(np.float64) ** 2 / width)
    step = dft.conj() @ (chirp[:, None] * dft)
    step = 0.5 * (step + step.T)
    full = np.stack([block_form(m) for m in (step, step.conj(), dft, dft.conj())])
    high = full.astype(np.float32).astype(ml_dtypes.bfloat16)
    low = (full - high.astype(np.float64)).astype(np.float32).astype(ml_dtypes.bfloat16)
    return np.stack([high, low], axis=1)


def halves(x):
    high = x.astype(jnp.bfloat16)
    return high, (x - high.astype(jnp.float32)).astype(jnp.bfloat16)


def dot(a, b):
    return jnp.dot(a, b, preferred_element_type=jnp.float32)


def times_right(x, high, low):
    x_high, x_low = halves(x)
    return dot(jnp.concatenate([x_high, x_low, x_high], axis=1), jnp.concatenate([high, high, low], axis=0))


def times_left(high, low, x):
    x_high, x_low = halves(x)
    y = dot(jnp.concatenate([high, high, low], axis=1), jnp.concatenate([x_high, x_low, x_high], axis=0))
    n = x.shape[0]
    return y[:n, :n] - y[n:, n:], y[:n, n:] + y[n:, :n]


def both_sides(re, im, tables, which):
    n = re.shape[0]
    y = times_right(jnp.concatenate([re, im], axis=1), tables[which ^ 1, 0], tables[which ^ 1, 1])
    return times_left(tables[which, 0, :, :n], tables[which, 1, :, :n], y)


def share(offsets, tile_rows):
    a = jnp.where(offsets[1] >= offsets[0], 1, 0)
    return a, offsets[2 + a], offsets[1 - a] - offsets[a] + tile_rows, offsets[3 - a]


def cut(tile, row, col, width):
    rows, cols = tile.shape
    part = pltpu.roll(tile, lax.rem(cols - col, cols), 1)[:, :width]
    return pltpu.roll(part, lax.rem(rows - row, rows), 0)


def own_kernel(offsets, objects, tiles, window_b):
    slab, _, rows, _ = objects.shape
    _, _, row_b, col_b = share(offsets, rows)
    for s in range(slab):
        for p in range(2):
            tile = objects[s, p]
            tiles[s, p] = tile
            window_b[s, p] = cut(tile, row_b, col_b, window_b.shape[-1])


def prev_kernel(offsets_prev, after, tiles, window_a, halo):
    slab, _, rows, _ = tiles.shape
    width = halo.shape[-1]
    _, col_a, row_p, col_p = share(offsets_prev, rows)
    for s in range(slab):
        for p in range(2):
            halo[s, p] = cut(tiles[s, p], row_p, col_p, width)
            window_a[s, p] = cut(tiles[s, p], 0, col_a, width)


def hold_kernel(after, x, out):
    out[...] = x[...]


def load_kernel(offsets, offsets_prev, intensity, far, probe, measured, start):
    rows = probe.shape[-1]
    near_a, _, _, _ = share(offsets, rows)
    far_a, _, _, _ = share(offsets_prev, rows)
    measured[...] = jnp.where(lax.axis_index("depth") == 0, far[far_a], intensity[1 - near_a])
    start[...] = probe[...]


def wave_kernel(depth_count, offsets, tables, probe, measured, window_a, window_b, halo, *rest):
    others_a, others_b, halos = (rest[(depth_count - 1) * k : (depth_count - 1) * (k + 1)] for k in range(3))
    rest = rest[3 * depth_count - 3 :]
    grads, probe_parts = rest[:depth_count], rest[depth_count : 2 * depth_count]
    layers, waves = rest[2 * depth_count :]
    slab = window_a.shape[0]
    n = probe.shape[-1]
    count = slab * depth_count
    depth = lax.axis_index("depth")
    on_a = depth == 0
    _, _, row_b, _ = share(offsets, n)
    inside = lax.broadcasted_iota(jnp.int32, (n, n), 0) < n - row_b
    for q in range(depth_count):
        of_a = (window_a, *others_a)[-q % depth_count]
        of_b, below = (window_b, *others_b)[(1 - q) % depth_count], (halo, *halos)[(1 - q) % depth_count]
        for s in range(slab):
            for p in range(2):
                b_layer = jnp.where(inside, of_b[s, p], below[s, p])
                layers[q * slab + s, p] = jnp.where(on_a, of_a[s, p], b_layer)

    def enter(s, re, im):
        waves[s, 0] = re
        waves[s, 1] = im
        o_re, o_im = layers[s, 0], layers[s, 1]
        return re * o_re - im * o_im, re * o_im + im * o_re

    def forward(s, wave):
        return both_sides(*enter(s, *wave), tables, 0)

    wave = lax.fori_loop(0, count - 1, forward, (probe[0], probe[1]), unroll=True if count <= 8 else 1)
    far_re, far_im = both_sides(*enter(count - 1, *wave), tables, 2)
    misfit = 2.0 * (far_re * far_re + far_im * far_im - measured[...])
    chi = both_sides(misfit * far_re, misfit * far_im, tables, 3)

    def leave(s, chi_re, chi_im):
        w_re, w_im = waves[s, 0], waves[s, 1]
        o_re, o_im = layers[s, 0], layers[s, 1]
        waves[s, 0] = w_re * chi_re + w_im * chi_im
        waves[s, 1] = w_re * chi_im - w_im * chi_re
        return o_re * chi_re + o_im * chi_im, o_re * chi_im - o_im * chi_re

    def backward(t, chi):
        return both_sides(*leave(count - 1 - t, *chi), tables, 1)

    chi = lax.fori_loop(0, count - 1, backward, chi, unroll=True if count <= 8 else 1)
    grad = leave(0, *chi)
    turn = lax.rem(jnp.where(on_a, 0, row_b), n)
    for j in range(depth_count):
        base = lax.rem(depth + j, depth_count) * slab
        for s in range(slab):
            for p in range(2):
                grads[j][s, p] = pltpu.roll(waves[base + s, p], turn, 0)
    rows = n // depth_count
    waves[0, 0] = jnp.where(depth < 2, grad[0], 0.0)
    waves[0, 1] = jnp.where(depth < 2, grad[1], 0.0)
    for j in range(depth_count):
        start = pl.multiple_of(lax.rem(depth + j, depth_count) * rows, rows)
        for p in range(2):
            probe_parts[j][p] = waves[0, p, pl.ds(start, rows), :]


def placed(x, col, mask, cols):
    blank = jnp.zeros((x.shape[0], cols - x.shape[1]), x.dtype)
    return pltpu.roll(jnp.concatenate([jnp.where(mask, x, 0.0), blank], axis=1), col, 1)


def place_kernel(depth_count, offsets, offsets_prev, *refs):
    *parts, out = refs
    slab, _, rows, cols = out.shape
    depth = lax.axis_index("depth")
    _, _, row_b, col_b = share(offsets, rows)
    _, col_a, _, _ = share(offsets_prev, rows)
    row_index = lax.broadcasted_iota(jnp.int32, (rows, parts[0].shape[-1]), 0)
    corners = []
    for j in range(depth_count):
        is_a = depth == j
        is_b = lax.rem(depth + depth_count - 1, depth_count) == j
        first = jnp.where(is_a, 0, row_b)
        last = jnp.where(is_a | is_b, rows, 0)
        corners.append((jnp.where(is_a, col_a, col_b), (row_index >= first) & (row_index < last)))
    for s in range(slab):
        for p in range(2):
            total = None
            for (col, mask), part in zip(corners, parts):
                x = placed(part[s, p], col, mask, cols)
                total = x if total is None else total + x
            out[s, p] = total


def step_kernel(depth_count, later, slices, *refs):
    a, b, *parts = refs[later:-2] if slices else refs[later:-1]
    total = refs[-2] if slices else refs[-1]
    total[...] = a[...] + b[...]
    place = lax.rem(lax.axis_index("depth") + depth_count - 1, depth_count)
    for j, part in enumerate(parts):

        @pl.when(place == j)
        def _():
            for i, s in enumerate(slices):
                refs[-1][i] = part[s]


def spill_kernel(offsets_prev, before, *refs):
    *spills, out, token = refs
    slab, _, rows, cols = out.shape
    _, _, row_p, col_p = share(offsets_prev, rows)
    mask = lax.broadcasted_iota(jnp.int32, (rows, spills[0].shape[-1]), 0) < row_p
    came = [(spill, i) for spill in spills for i in range(spill.shape[0])]
    for s in range(slab):
        for p in range(2):
            out[s, p] = before[s, p] + placed(came[s][0][came[s][1], p], col_p, mask, cols)
    token[...] = jnp.zeros_like(token)


def call(kernel, name, scalars, arrays, outs, scratch=(), work=10**9, after=()):
    vmem = pl.BlockSpec(memory_space=pltpu.VMEM)
    moved = sum(math.prod(x.shape) * x.dtype.itemsize for x in (*arrays, *outs))
    return pl.pallas_call(
        kernel,
        name=name,
        out_shape=outs,
        in_specs=[pl.BlockSpec(memory_space=pltpu.SMEM)] * len(scalars)
        + [pl.BlockSpec(memory_space=pl.ANY)] * len(after)
        + [vmem] * len(arrays),
        out_specs=[vmem] * len(outs),
        scratch_shapes=scratch,
        compiler_params=pltpu.CompilerParams(vmem_limit_bytes=VMEM_LIMIT),
        cost_estimate=pl.CostEstimate(flops=work, bytes_accessed=moved, transcendentals=0),
    )(*scalars, *after, *arrays)


def sum_round(x, level):
    depth_count, scan_count = lax.axis_size("depth"), lax.axis_size("scan")
    levels = scan_count.bit_length() - 1
    route = []
    for d in range(depth_count):
        step = 1 << (1 + (level - 1 + d % 2) % (levels - 1) if level else 0)
        route += [(d * scan_count + i, d * scan_count + (i ^ step)) for i in range(scan_count)]
    return lax.ppermute(x, ("depth", "scan"), route)


def body(objects, probe, row_offsets, col_offsets, intensity):
    slab = objects.shape[0]
    n = probe.shape[-1]
    depth_count, scan_count = lax.axis_size("depth"), lax.axis_size("scan")
    f32 = jnp.float32

    def across(x, source, target, shift):
        route = [(source * scan_count + i, target * scan_count + (i + shift) % scan_count) for i in range(scan_count)]
        return lax.ppermute(x, ("depth", "scan"), route)

    offsets = jnp.concatenate([row_offsets, col_offsets])
    offsets_prev = lax.ppermute(offsets, "scan", [(i, (i + 1) % scan_count) for i in range(scan_count)])
    far = across(intensity, 0, 0, 1)
    window = jax.ShapeDtypeStruct((slab, 2, n, n), f32)
    whole = jax.ShapeDtypeStruct(objects.shape, f32)
    tiles, window_b = call(own_kernel, "own", [offsets], [objects], [whole, window])
    window_a, halo = call(prev_kernel, "prev", [offsets_prev], [tiles], [window] * 2, after=[far])
    halo = lax.ppermute(halo, "scan", [((i + 1) % scan_count, i) for i in range(scan_count)])

    def gathered(x, target):
        return [lax.ppermute(x, "depth", [((target - j) % depth_count, target)]) for j in range(1, depth_count)]

    others_a = gathered(window_a, 0)
    measured, start = call(
        load_kernel,
        "load",
        [offsets, offsets_prev],
        [intensity, far, probe],
        [jax.ShapeDtypeStruct((n, n), f32), jax.ShapeDtypeStruct(probe.shape, f32)],
    )

    (halo,) = call(hold_kernel, "hold", [], [halo], [window], after=[measured])
    others_b, halos = gathered(window_b, 1), gathered(halo, 1)

    tables = jnp.asarray(constant_tables(n))
    count = slab * depth_count
    parts = call(
        lambda *refs: wave_kernel(depth_count, *refs),
        "wave",
        [offsets],
        [tables, start, measured, window_a, window_b, halo, *others_a, *others_b, *halos],
        [window] * depth_count + [jax.ShapeDtypeStruct((2, n // depth_count, n), f32)] * depth_count,
        [pltpu.VMEM((count, 2, n, n), f32)] * 2,
        work=5 * 10**9,
    )
    grads, probe_parts = parts[:depth_count], parts[depth_count:]

    back, sums = [grads[0]], [probe_parts[0]]
    for j in range(1, depth_count):
        sums.append(lax.ppermute(probe_parts[j], "depth", [(t, (t + j) % depth_count) for t in range(depth_count)]))
        back.append(lax.ppermute(grads[j], "depth", [(t, (t + j) % depth_count) for t in (0, 1)]))

    half = jax.ShapeDtypeStruct(sums[0].shape, f32)
    ahead = [(i, (i + 1) % scan_count) for i in range(scan_count)]
    rounds = scan_count.bit_length() - 1
    paired = scan_count == 1 << rounds and rounds > 2
    spill = []

    def step(a, b, slices, after):
        outs = [half, jax.ShapeDtypeStruct((len(slices), 2, n, n), f32)] if slices else [half]
        return call(
            lambda *refs: step_kernel(depth_count, len(after), slices, *refs),
            "step",
            [],
            [a, b, *(back if slices else [])],
            outs,
            after=after,
        )

    (object_grad,) = call(
        lambda *refs: place_kernel(depth_count, *refs),
        "place",
        [offsets, offsets_prev],
        back,
        [whole],
        work=2 * 10**9,
    )
    turns = rounds - 1 if paired else 1
    cuts = [0, slab // 3] + [slab] * (turns - 1) if turns > 1 else [0, slab]
    share_of = [tuple(range(cuts[k], cuts[k + 1])) for k in range(turns)]
    total = sums[0]
    for x in sums[1:-1]:
        total = total + x
    other = sums[-1] if depth_count > 1 else jnp.zeros_like(total)
    for k, slices in enumerate(share_of):
        total, *payload = step(total, other, slices, spill[:1] if k == 2 else [])
        other = sum_round(total, k) if paired else jnp.zeros_like(total)
        spill += [lax.ppermute(x, "scan", ahead) for x in payload]
    if paired:
        (total,) = step(total, other, (), [object_grad])
        other = sum_round(total, rounds - 1)
    object_grad, token = call(
        spill_kernel, "spill", [offsets_prev], [object_grad, *spill], [whole, jax.ShapeDtypeStruct((8, n), f32)]
    )
    if paired:
        (total,) = step(total, other, (), [token])
    else:
        total = lax.psum(total, "scan")
    return object_grad, total


def solution(mesh):
    in_specs = (P("depth", None, "scan", None), P(), P("scan"), P("scan"), P("scan", None, None))
    out_specs = (P("depth", None, "scan", None), P(None, "depth", None))
    return jax.shard_map(body, mesh=mesh, in_specs=in_specs, out_specs=out_specs, check_vma=False)
```

```python
import math

import jax
import jax.numpy as jnp
import ml_dtypes
import numpy as np
from jax import lax
from jax.experimental import pallas as pl
from jax.experimental.pallas import tpu as pltpu
from jax.sharding import PartitionSpec as P

PROPAGATION = 0.5
VMEM_LIMIT = 48 * 1024 * 1024


def block_form(matrix):
    return np.block([[matrix.real, -matrix.imag], [matrix.imag, matrix.real]])


def constant_tables(width):
    grid = np.arange(width)
    frequency = np.where(grid < width // 2, grid, grid - width)
    dft = np.exp(-2j * np.pi * ((grid[:, None] * grid[None, :]) % width) / width) / math.sqrt(width)
    chirp = np.exp(-1j * PROPAGATION * np.pi * frequency.astype(np.float64) ** 2 / width)
    step = dft.conj() @ (chirp[:, None] * dft)
    step = 0.5 * (step + step.T)
    full = np.stack([block_form(m) for m in (step, step.conj(), dft, dft.conj())])
    high = full.astype(np.float32).astype(ml_dtypes.bfloat16)
    low = (full - high.astype(np.float64)).astype(np.float32).astype(ml_dtypes.bfloat16)
    return np.stack([high, low], axis=1)


def halves(x):
    high = x.astype(jnp.bfloat16)
    return high, (x - high.astype(jnp.float32)).astype(jnp.bfloat16)


def dot(a, b):
    return jnp.dot(a, b, preferred_element_type=jnp.float32)


def times_right(x, high, low):
    x_high, x_low = halves(x)
    return dot(jnp.concatenate([x_high, x_low, x_high], axis=1), jnp.concatenate([high, high, low], axis=0))


def times_left(high, low, x):
    x_high, x_low = halves(x)
    y = dot(jnp.concatenate([high, high, low], axis=1), jnp.concatenate([x_high, x_low, x_high], axis=0))
    n = x.shape[0]
    return y[:n, :n] - y[n:, n:], y[:n, n:] + y[n:, :n]


def both_sides(re, im, tables, which):
    n = re.shape[0]
    y = times_right(jnp.concatenate([re, im], axis=1), tables[which ^ 1, 0], tables[which ^ 1, 1])
    return times_left(tables[which, 0, :, :n], tables[which, 1, :, :n], y)


def share(offsets, tile_rows):
    a = jnp.where(offsets[1] >= offsets[0], 1, 0)
    return a, offsets[2 + a], offsets[1 - a] - offsets[a] + tile_rows, offsets[3 - a]


def cut(tile, row, col, width):
    rows, cols = tile.shape
    part = pltpu.roll(tile, lax.rem(cols - col, cols), 1)[:, :width]
    return pltpu.roll(part, lax.rem(rows - row, rows), 0)


def own_kernel(offsets, objects, tiles, window_b):
    slab, _, rows, _ = objects.shape
    _, _, row_b, col_b = share(offsets, rows)
    for s in range(slab):
        for p in range(2):
            tile = objects[s, p]
            tiles[s, p] = tile
            window_b[s, p] = cut(tile, row_b, col_b, window_b.shape[-1])


def prev_kernel(offsets_prev, after, tiles, window_a, halo):
    slab, _, rows, _ = tiles.shape
    width = halo.shape[-1]
    _, col_a, row_p, col_p = share(offsets_prev, rows)
    for s in range(slab):
        for p in range(2):
            halo[s, p] = cut(tiles[s, p], row_p, col_p, width)
            window_a[s, p] = cut(tiles[s, p], 0, col_a, width)


def hold_kernel(after, x, out):
    out[...] = x[...]


def load_kernel(offsets, offsets_prev, intensity, far, probe, measured, start):
    rows = probe.shape[-1]
    near_a, _, _, _ = share(offsets, rows)
    far_a, _, _, _ = share(offsets_prev, rows)
    measured[...] = jnp.where(lax.axis_index("depth") == 0, far[far_a], intensity[1 - near_a])
    start[...] = probe[...]


def wave_kernel(depth_count, offsets, tables, probe, measured, window_a, window_b, halo, *rest):
    others_a, others_b, halos = (rest[(depth_count - 1) * k : (depth_count - 1) * (k + 1)] for k in range(3))
    rest = rest[3 * depth_count - 3 :]
    grads, probe_parts = rest[:depth_count], rest[depth_count : 2 * depth_count]
    layers, waves = rest[2 * depth_count :]
    slab = window_a.shape[0]
    n = probe.shape[-1]
    count = slab * depth_count
    depth = lax.axis_index("depth")
    on_a = depth == 0
    _, _, row_b, _ = share(offsets, n)
    inside = lax.broadcasted_iota(jnp.int32, (n, n), 0) < n - row_b
    for q in range(depth_count):
        of_a = (window_a, *others_a)[-q % depth_count]
        of_b, below = (window_b, *others_b)[(1 - q) % depth_count], (halo, *halos)[(1 - q) % depth_count]
        for s in range(slab):
            for p in range(2):
                b_layer = jnp.where(inside, of_b[s, p], below[s, p])
                layers[q * slab + s, p] = jnp.where(on_a, of_a[s, p], b_layer)

    def enter(s, re, im):
        waves[s, 0] = re
        waves[s, 1] = im
        o_re, o_im = layers[s, 0], layers[s, 1]
        return re * o_re - im * o_im, re * o_im + im * o_re

    def forward(s, wave):
        return both_sides(*enter(s, *wave), tables, 0)

    wave = lax.fori_loop(0, count - 1, forward, (probe[0], probe[1]), unroll=True if count <= 8 else 1)
    far_re, far_im = both_sides(*enter(count - 1, *wave), tables, 2)
    misfit = 2.0 * (far_re * far_re + far_im * far_im - measured[...])
    chi = both_sides(misfit * far_re, misfit * far_im, tables, 3)

    def leave(s, chi_re, chi_im):
        w_re, w_im = waves[s, 0], waves[s, 1]
        o_re, o_im = layers[s, 0], layers[s, 1]
        waves[s, 0] = w_re * chi_re + w_im * chi_im
        waves[s, 1] = w_re * chi_im - w_im * chi_re
        return o_re * chi_re + o_im * chi_im, o_re * chi_im - o_im * chi_re

    def backward(t, chi):
        return both_sides(*leave(count - 1 - t, *chi), tables, 1)

    chi = lax.fori_loop(0, count - 1, backward, chi, unroll=True if count <= 8 else 1)
    grad = leave(0, *chi)
    turn = lax.rem(jnp.where(on_a, 0, row_b), n)
    for j in range(depth_count):
        base = lax.rem(depth + j, depth_count) * slab
        for s in range(slab):
            for p in range(2):
                grads[j][s, p] = pltpu.roll(waves[base + s, p], turn, 0)
    rows = n // depth_count
    waves[0, 0] = jnp.where(depth < 2, grad[0], 0.0)
    waves[0, 1] = jnp.where(depth < 2, grad[1], 0.0)
    for j in range(depth_count):
        start = pl.multiple_of(lax.rem(depth + j, depth_count) * rows, rows)
        for p in range(2):
            probe_parts[j][p] = waves[0, p, pl.ds(start, rows), :]


def placed(x, col, mask, cols):
    blank = jnp.zeros((x.shape[0], cols - x.shape[1]), x.dtype)
    return pltpu.roll(jnp.concatenate([jnp.where(mask, x, 0.0), blank], axis=1), col, 1)


def place_kernel(depth_count, offsets, offsets_prev, *refs):
    *parts, out = refs
    slab, _, rows, cols = out.shape
    depth = lax.axis_index("depth")
    _, _, row_b, col_b = share(offsets, rows)
    _, col_a, _, _ = share(offsets_prev, rows)
    row_index = lax.broadcasted_iota(jnp.int32, (rows, parts[0].shape[-1]), 0)
    corners = []
    for j in range(depth_count):
        is_a = depth == j
        is_b = lax.rem(depth + depth_count - 1, depth_count) == j
        first = jnp.where(is_a, 0, row_b)
        last = jnp.where(is_a | is_b, rows, 0)
        corners.append((jnp.where(is_a, col_a, col_b), (row_index >= first) & (row_index < last)))
    for s in range(slab):
        for p in range(2):
            total = None
            for (col, mask), part in zip(corners, parts):
                x = placed(part[s, p], col, mask, cols)
                total = x if total is None else total + x
            out[s, p] = total


def step_kernel(depth_count, later, slices, *refs):
    a, b, *parts = refs[later:-2] if slices else refs[later:-1]
    total = refs[-2] if slices else refs[-1]
    total[...] = a[...] + b[...]
    place = lax.rem(lax.axis_index("depth") + depth_count - 1, depth_count)
    for j, part in enumerate(parts):

        @pl.when(place == j)
        def _():
            for i, s in enumerate(slices):
                refs[-1][i] = part[s]


def spill_kernel(offsets_prev, before, *refs):
    *spills, out, token = refs
    slab, _, rows, cols = out.shape
    _, _, row_p, col_p = share(offsets_prev, rows)
    mask = lax.broadcasted_iota(jnp.int32, (rows, spills[0].shape[-1]), 0) < row_p
    came = [(spill, i) for spill in spills for i in range(spill.shape[0])]
    for s in range(slab):
        for p in range(2):
            out[s, p] = before[s, p] + placed(came[s][0][came[s][1], p], col_p, mask, cols)
    token[...] = jnp.zeros_like(token)


def call(kernel, name, scalars, arrays, outs, scratch=(), work=10**9, after=()):
    vmem = pl.BlockSpec(memory_space=pltpu.VMEM)
    moved = sum(math.prod(x.shape) * x.dtype.itemsize for x in (*arrays, *outs))
    return pl.pallas_call(
        kernel,
        name=name,
        out_shape=outs,
        in_specs=[pl.BlockSpec(memory_space=pltpu.SMEM)] * len(scalars)
        + [pl.BlockSpec(memory_space=pl.ANY)] * len(after)
        + [vmem] * len(arrays),
        out_specs=[vmem] * len(outs),
        scratch_shapes=scratch,
        compiler_params=pltpu.CompilerParams(vmem_limit_bytes=VMEM_LIMIT),
        cost_estimate=pl.CostEstimate(flops=work, bytes_accessed=moved, transcendentals=0),
    )(*scalars, *after, *arrays)


def sum_round(x, level):
    depth_count, scan_count = lax.axis_size("depth"), lax.axis_size("scan")
    levels = scan_count.bit_length() - 1
    route = []
    for d in range(depth_count):
        middle = level + 1 if d % 2 else levels - level
        step = 1 << (0 if level == 0 else 1 if level == levels - 1 else middle)
        route += [(d * scan_count + i, d * scan_count + (i ^ step)) for i in range(scan_count)]
    return lax.ppermute(x, ("depth", "scan"), route)


def body(objects, probe, row_offsets, col_offsets, intensity):
    slab = objects.shape[0]
    n = probe.shape[-1]
    depth_count, scan_count = lax.axis_size("depth"), lax.axis_size("scan")
    f32 = jnp.float32

    def across(x, source, target, shift):
        route = [(source * scan_count + i, target * scan_count + (i + shift) % scan_count) for i in range(scan_count)]
        return lax.ppermute(x, ("depth", "scan"), route)

    offsets = jnp.concatenate([row_offsets, col_offsets])
    offsets_prev = lax.ppermute(offsets, "scan", [(i, (i + 1) % scan_count) for i in range(scan_count)])
    far = across(intensity, 0, 0, 1)
    window = jax.ShapeDtypeStruct((slab, 2, n, n), f32)
    whole = jax.ShapeDtypeStruct(objects.shape, f32)
    tiles, window_b = call(own_kernel, "own", [offsets], [objects], [whole, window])
    window_a, halo = call(prev_kernel, "prev", [offsets_prev], [tiles], [window] * 2, after=[far])
    halo = lax.ppermute(halo, "scan", [((i + 1) % scan_count, i) for i in range(scan_count)])

    def gathered(x, target):
        return [lax.ppermute(x, "depth", [((target - j) % depth_count, target)]) for j in range(1, depth_count)]

    others_a = gathered(window_a, 0)
    measured, start = call(
        load_kernel,
        "load",
        [offsets, offsets_prev],
        [intensity, far, probe],
        [jax.ShapeDtypeStruct((n, n), f32), jax.ShapeDtypeStruct(probe.shape, f32)],
    )

    (halo,) = call(hold_kernel, "hold", [], [halo], [window], after=[measured])
    others_b, halos = gathered(window_b, 1), gathered(halo, 1)

    tables = jnp.asarray(constant_tables(n))
    count = slab * depth_count
    parts = call(
        lambda *refs: wave_kernel(depth_count, *refs),
        "wave",
        [offsets],
        [tables, start, measured, window_a, window_b, halo, *others_a, *others_b, *halos],
        [window] * depth_count + [jax.ShapeDtypeStruct((2, n // depth_count, n), f32)] * depth_count,
        [pltpu.VMEM((count, 2, n, n), f32)] * 2,
        work=5 * 10**9,
    )
    grads, probe_parts = parts[:depth_count], parts[depth_count:]

    back, sums = [grads[0]], [probe_parts[0]]
    for j in range(1, depth_count):
        sums.append(lax.ppermute(probe_parts[j], "depth", [(t, (t + j) % depth_count) for t in range(depth_count)]))
        back.append(lax.ppermute(grads[j], "depth", [(t, (t + j) % depth_count) for t in (0, 1)]))

    half = jax.ShapeDtypeStruct(sums[0].shape, f32)
    ahead = [(i, (i + 1) % scan_count) for i in range(scan_count)]
    rounds = scan_count.bit_length() - 1
    paired = scan_count == 1 << rounds and rounds > 2
    spill = []

    def step(a, b, slices, after):
        outs = [half, jax.ShapeDtypeStruct((len(slices), 2, n, n), f32)] if slices else [half]
        return call(
            lambda *refs: step_kernel(depth_count, len(after), slices, *refs),
            "step",
            [],
            [a, b, *(back if slices else [])],
            outs,
            after=after,
        )

    (object_grad,) = call(
        lambda *refs: place_kernel(depth_count, *refs),
        "place",
        [offsets, offsets_prev],
        back,
        [whole],
        work=2 * 10**9,
    )
    turns = rounds - 1 if paired else 1
    cuts = [0, slab // 3] + [slab] * (turns - 1) if turns > 1 else [0, slab]
    share_of = [tuple(range(cuts[k], cuts[k + 1])) for k in range(turns)]
    total = sums[0]
    for x in sums[1:-1]:
        total = total + x
    other = sums[-1] if depth_count > 1 else jnp.zeros_like(total)
    for k, slices in enumerate(share_of):
        total, *payload = step(total, other, slices, spill[:1] if k == 2 else [])
        other = sum_round(total, k) if paired else jnp.zeros_like(total)
        spill += [lax.ppermute(x, "scan", ahead) for x in payload]
    if paired:
        (total,) = step(total, other, (), [object_grad])
        other = sum_round(total, rounds - 1)
    object_grad, token = call(
        spill_kernel, "spill", [offsets_prev], [object_grad, *spill], [whole, jax.ShapeDtypeStruct((8, n), f32)]
    )
    if paired:
        (total,) = step(total, other, (), [token])
    else:
        total = lax.psum(total, "scan")
    return object_grad, total


def solution(mesh):
    in_specs = (P("depth", None, "scan", None), P(), P("scan"), P("scan"), P("scan", None, None))
    out_specs = (P("depth", None, "scan", None), P(None, "depth", None))
    return jax.shard_map(body, mesh=mesh, in_specs=in_specs, out_specs=out_specs, check_vma=False)
```

```python
import math

import jax
import jax.numpy as jnp
import ml_dtypes
import numpy as np
from jax import lax
from jax.experimental import pallas as pl
from jax.experimental.pallas import tpu as pltpu
from jax.sharding import PartitionSpec as P

PROPAGATION = 0.5
VMEM_LIMIT = 48 * 1024 * 1024


def block_form(matrix):
    return np.block([[matrix.real, -matrix.imag], [matrix.imag, matrix.real]])


def constant_tables(width):
    grid = np.arange(width)
    frequency = np.where(grid < width // 2, grid, grid - width)
    dft = np.exp(-2j * np.pi * ((grid[:, None] * grid[None, :]) % width) / width) / math.sqrt(width)
    chirp = np.exp(-1j * PROPAGATION * np.pi * frequency.astype(np.float64) ** 2 / width)
    step = dft.conj() @ (chirp[:, None] * dft)
    step = 0.5 * (step + step.T)
    full = np.stack([block_form(m) for m in (step, step.conj(), dft, dft.conj())])
    high = full.astype(np.float32).astype(ml_dtypes.bfloat16)
    low = (full - high.astype(np.float64)).astype(np.float32).astype(ml_dtypes.bfloat16)
    return np.stack([high, low], axis=1)


def halves(x):
    high = x.astype(jnp.bfloat16)
    return high, (x - high.astype(jnp.float32)).astype(jnp.bfloat16)


def dot(a, b):
    return jnp.dot(a, b, preferred_element_type=jnp.float32)


def times_right(x, high, low):
    x_high, x_low = halves(x)
    return dot(jnp.concatenate([x_high, x_low, x_high], axis=1), jnp.concatenate([high, high, low], axis=0))


def times_left(high, low, x):
    x_high, x_low = halves(x)
    y = dot(jnp.concatenate([high, high, low], axis=1), jnp.concatenate([x_high, x_low, x_high], axis=0))
    n = x.shape[0]
    return y[:n, :n] - y[n:, n:], y[:n, n:] + y[n:, :n]


def both_sides(re, im, tables, which):
    n = re.shape[0]
    y = times_right(jnp.concatenate([re, im], axis=1), tables[which ^ 1, 0], tables[which ^ 1, 1])
    return times_left(tables[which, 0, :, :n], tables[which, 1, :, :n], y)


def share(offsets, tile_rows):
    a = jnp.where(offsets[1] >= offsets[0], 1, 0)
    return a, offsets[2 + a], offsets[1 - a] - offsets[a] + tile_rows, offsets[3 - a]


def cut(tile, row, col, width):
    rows, cols = tile.shape
    part = pltpu.roll(tile, lax.rem(cols - col, cols), 1)[:, :width]
    return pltpu.roll(part, lax.rem(rows - row, rows), 0)


def own_kernel(offsets, objects, tiles, window_b):
    slab, _, rows, _ = objects.shape
    _, _, row_b, col_b = share(offsets, rows)
    for s in range(slab):
        for p in range(2):
            tile = objects[s, p]
            tiles[s, p] = tile
            window_b[s, p] = cut(tile, row_b, col_b, window_b.shape[-1])


def prev_kernel(offsets_prev, after, tiles, window_a, halo):
    slab, _, rows, _ = tiles.shape
    width = halo.shape[-1]
    _, col_a, row_p, col_p = share(offsets_prev, rows)
    for s in range(slab):
        for p in range(2):
            halo[s, p] = cut(tiles[s, p], row_p, col_p, width)
            window_a[s, p] = cut(tiles[s, p], 0, col_a, width)


def hold_kernel(after, x, out):
    out[...] = x[...]


def load_kernel(offsets, offsets_prev, intensity, far, probe, measured, start):
    rows = probe.shape[-1]
    near_a, _, _, _ = share(offsets, rows)
    far_a, _, _, _ = share(offsets_prev, rows)
    measured[...] = jnp.where(lax.axis_index("depth") == 0, far[far_a], intensity[1 - near_a])
    start[...] = probe[...]


def wave_kernel(depth_count, offsets, tables, probe, measured, window_a, window_b, halo, *rest):
    others_a, others_b, halos = (rest[(depth_count - 1) * k : (depth_count - 1) * (k + 1)] for k in range(3))
    rest = rest[3 * depth_count - 3 :]
    grads, probe_parts = rest[:depth_count], rest[depth_count : 2 * depth_count]
    layers, waves = rest[2 * depth_count :]
    slab = window_a.shape[0]
    n = probe.shape[-1]
    count = slab * depth_count
    depth = lax.axis_index("depth")
    on_a = depth == 0
    _, _, row_b, _ = share(offsets, n)
    inside = lax.broadcasted_iota(jnp.int32, (n, n), 0) < n - row_b
    for q in range(depth_count):
        of_a = (window_a, *others_a)[-q % depth_count]
        of_b, below = (window_b, *others_b)[(1 - q) % depth_count], (halo, *halos)[(1 - q) % depth_count]
        for s in range(slab):
            for p in range(2):
                b_layer = jnp.where(inside, of_b[s, p], below[s, p])
                layers[q * slab + s, p] = jnp.where(on_a, of_a[s, p], b_layer)

    def enter(s, re, im):
        waves[s, 0] = re
        waves[s, 1] = im
        o_re, o_im = layers[s, 0], layers[s, 1]
        return re * o_re - im * o_im, re * o_im + im * o_re

    def forward(s, wave):
        return both_sides(*enter(s, *wave), tables, 0)

    wave = lax.fori_loop(0, count - 1, forward, (probe[0], probe[1]), unroll=True if count <= 8 else 1)
    far_re, far_im = both_sides(*enter(count - 1, *wave), tables, 2)
    misfit = 2.0 * (far_re * far_re + far_im * far_im - measured[...])
    chi = both_sides(misfit * far_re, misfit * far_im, tables, 3)

    def leave(s, chi_re, chi_im):
        w_re, w_im = waves[s, 0], waves[s, 1]
        o_re, o_im = layers[s, 0], layers[s, 1]
        waves[s, 0] = w_re * chi_re + w_im * chi_im
        waves[s, 1] = w_re * chi_im - w_im * chi_re
        return o_re * chi_re + o_im * chi_im, o_re * chi_im - o_im * chi_re

    def backward(t, chi):
        return both_sides(*leave(count - 1 - t, *chi), tables, 1)

    chi = lax.fori_loop(0, count - 1, backward, chi, unroll=True if count <= 8 else 1)
    grad = leave(0, *chi)
    turn = lax.rem(jnp.where(on_a, 0, row_b), n)
    for j in range(depth_count):
        base = lax.rem(depth + j, depth_count) * slab
        for s in range(slab):
            for p in range(2):
                grads[j][s, p] = pltpu.roll(waves[base + s, p], turn, 0)
    rows = n // depth_count
    waves[0, 0] = jnp.where(depth < 2, grad[0], 0.0)
    waves[0, 1] = jnp.where(depth < 2, grad[1], 0.0)
    for j in range(depth_count):
        start = pl.multiple_of(lax.rem(depth + j, depth_count) * rows, rows)
        for p in range(2):
            probe_parts[j][p] = waves[0, p, pl.ds(start, rows), :]


def placed(x, col, mask, cols):
    blank = jnp.zeros((x.shape[0], cols - x.shape[1]), x.dtype)
    return pltpu.roll(jnp.concatenate([jnp.where(mask, x, 0.0), blank], axis=1), col, 1)


def place_kernel(depth_count, offsets, offsets_prev, *refs):
    *parts, out = refs
    slab, _, rows, cols = out.shape
    depth = lax.axis_index("depth")
    _, _, row_b, col_b = share(offsets, rows)
    _, col_a, _, _ = share(offsets_prev, rows)
    row_index = lax.broadcasted_iota(jnp.int32, (rows, parts[0].shape[-1]), 0)
    corners = []
    for j in range(depth_count):
        is_a = depth == j
        is_b = lax.rem(depth + depth_count - 1, depth_count) == j
        first = jnp.where(is_a, 0, row_b)
        last = jnp.where(is_a | is_b, rows, 0)
        corners.append((jnp.where(is_a, col_a, col_b), (row_index >= first) & (row_index < last)))
    for s in range(slab):
        for p in range(2):
            total = None
            for (col, mask), part in zip(corners, parts):
                x = placed(part[s, p], col, mask, cols)
                total = x if total is None else total + x
            out[s, p] = total


def step_kernel(depth_count, later, slices, *refs):
    a, b, *parts = refs[later:-2] if slices else refs[later:-1]
    total = refs[-2] if slices else refs[-1]
    total[...] = a[...] + b[...]
    place = lax.rem(lax.axis_index("depth") + depth_count - 1, depth_count)
    for j, part in enumerate(parts):

        @pl.when(place == j)
        def _():
            for i, s in enumerate(slices):
                refs[-1][i] = part[s]


def spill_kernel(offsets_prev, before, *refs):
    *spills, out, token = refs
    slab, _, rows, cols = out.shape
    _, _, row_p, col_p = share(offsets_prev, rows)
    mask = lax.broadcasted_iota(jnp.int32, (rows, spills[0].shape[-1]), 0) < row_p
    came = [(spill, i) for spill in spills for i in range(spill.shape[0])]
    for s in range(slab):
        for p in range(2):
            out[s, p] = before[s, p] + placed(came[s][0][came[s][1], p], col_p, mask, cols)
    token[...] = jnp.zeros_like(token)


def call(kernel, name, scalars, arrays, outs, scratch=(), work=10**9, after=()):
    vmem = pl.BlockSpec(memory_space=pltpu.VMEM)
    moved = sum(math.prod(x.shape) * x.dtype.itemsize for x in (*arrays, *outs))
    return pl.pallas_call(
        kernel,
        name=name,
        out_shape=outs,
        in_specs=[pl.BlockSpec(memory_space=pltpu.SMEM)] * len(scalars)
        + [pl.BlockSpec(memory_space=pl.ANY)] * len(after)
        + [vmem] * len(arrays),
        out_specs=[vmem] * len(outs),
        scratch_shapes=scratch,
        compiler_params=pltpu.CompilerParams(vmem_limit_bytes=VMEM_LIMIT),
        cost_estimate=pl.CostEstimate(flops=work, bytes_accessed=moved, transcendentals=0),
    )(*scalars, *after, *arrays)


def sum_round(x, level):
    depth_count, scan_count = lax.axis_size("depth"), lax.axis_size("scan")
    levels = scan_count.bit_length() - 1
    route = []
    for d in range(depth_count):
        step = 1 << ((level + (d % 2) * (levels // 2)) % levels)
        route += [(d * scan_count + i, d * scan_count + (i ^ step)) for i in range(scan_count)]
    return lax.ppermute(x, ("depth", "scan"), route)


def body(objects, probe, row_offsets, col_offsets, intensity):
    slab = objects.shape[0]
    n = probe.shape[-1]
    depth_count, scan_count = lax.axis_size("depth"), lax.axis_size("scan")
    f32 = jnp.float32

    offsets = jnp.concatenate([row_offsets, col_offsets])
    offsets_prev = lax.ppermute(offsets, "scan", [(i, (i + 1) % scan_count) for i in range(scan_count)])
    far = lax.ppermute(intensity, "scan", [(i, (i + 1) % scan_count) for i in range(scan_count)])
    window = jax.ShapeDtypeStruct((slab, 2, n, n), f32)
    whole = jax.ShapeDtypeStruct(objects.shape, f32)
    tiles, window_b = call(own_kernel, "own", [offsets], [objects], [whole, window])
    window_a, halo = call(prev_kernel, "prev", [offsets_prev], [tiles], [window] * 2, after=[far])
    halo = lax.ppermute(halo, "scan", [((i + 1) % scan_count, i) for i in range(scan_count)])

    def gathered(x, target):
        return [lax.ppermute(x, "depth", [((target - j) % depth_count, target)]) for j in range(1, depth_count)]

    others_a = gathered(window_a, 0)
    measured, start = call(
        load_kernel,
        "load",
        [offsets, offsets_prev],
        [intensity, far, probe],
        [jax.ShapeDtypeStruct((n, n), f32), jax.ShapeDtypeStruct(probe.shape, f32)],
    )

    (halo,) = call(hold_kernel, "hold", [], [halo], [window], after=[measured])
    others_b, halos = gathered(window_b, 1), gathered(halo, 1)

    tables = jnp.asarray(constant_tables(n))
    count = slab * depth_count
    parts = call(
        lambda *refs: wave_kernel(depth_count, *refs),
        "wave",
        [offsets],
        [tables, start, measured, window_a, window_b, halo, *others_a, *others_b, *halos],
        [window] * depth_count + [jax.ShapeDtypeStruct((2, n // depth_count, n), f32)] * depth_count,
        [pltpu.VMEM((count, 2, n, n), f32)] * 2,
        work=5 * 10**9,
    )
    grads, probe_parts = parts[:depth_count], parts[depth_count:]

    back, sums = [grads[0]], [probe_parts[0]]
    for j in range(1, depth_count):
        sums.append(lax.ppermute(probe_parts[j], "depth", [(t, (t + j) % depth_count) for t in range(depth_count)]))
        back.append(lax.ppermute(grads[j], "depth", [(t, (t + j) % depth_count) for t in (0, 1)]))

    half = jax.ShapeDtypeStruct(sums[0].shape, f32)
    ahead = [(i, (i + 1) % scan_count) for i in range(scan_count)]
    rounds = scan_count.bit_length() - 1
    paired = scan_count == 1 << rounds and rounds > 2
    spill = []

    def step(a, b, slices, after):
        outs = [half, jax.ShapeDtypeStruct((len(slices), 2, n, n), f32)] if slices else [half]
        return call(
            lambda *refs: step_kernel(depth_count, len(after), slices, *refs),
            "step",
            [],
            [a, b, *(back if slices else [])],
            outs,
            after=after,
        )

    (object_grad,) = call(
        lambda *refs: place_kernel(depth_count, *refs),
        "place",
        [offsets, offsets_prev],
        back,
        [whole],
        work=2 * 10**9,
    )
    turns = rounds - 1 if paired else 1
    cuts = [0, slab // 3] + [slab] * (turns - 1) if turns > 1 else [0, slab]
    share_of = [tuple(range(cuts[k], cuts[k + 1])) for k in range(turns)]
    total = sums[0]
    for x in sums[1:-1]:
        total = total + x
    other = sums[-1] if depth_count > 1 else jnp.zeros_like(total)
    for k, slices in enumerate(share_of):
        total, *payload = step(total, other, slices, spill[:1] if k == 2 else [])
        other = sum_round(total, k) if paired else jnp.zeros_like(total)
        spill += [lax.ppermute(x, "scan", ahead) for x in payload]
    if paired:
        (total,) = step(total, other, (), [object_grad])
        other = sum_round(total, rounds - 1)
    object_grad, token = call(
        spill_kernel, "spill", [offsets_prev], [object_grad, *spill], [whole, jax.ShapeDtypeStruct((8, n), f32)]
    )
    if paired:
        (total,) = step(total, other, (), [token])
    else:
        total = lax.psum(total, "scan")
    return object_grad, total


def solution(mesh):
    in_specs = (P("depth", None, "scan", None), P(), P("scan"), P("scan"), P("scan", None, None))
    out_specs = (P("depth", None, "scan", None), P(None, "depth", None))
    return jax.shard_map(body, mesh=mesh, in_specs=in_specs, out_specs=out_specs, check_vma=False)
```

```python
import math

import jax
import jax.numpy as jnp
import ml_dtypes
import numpy as np
from jax import lax
from jax.experimental import pallas as pl
from jax.experimental.pallas import tpu as pltpu
from jax.sharding import PartitionSpec as P

PROPAGATION = 0.5
VMEM_LIMIT = 48 * 1024 * 1024


def block_form(matrix):
    return np.block([[matrix.real, -matrix.imag], [matrix.imag, matrix.real]])


def constant_tables(width):
    grid = np.arange(width)
    frequency = np.where(grid < width // 2, grid, grid - width)
    dft = np.exp(-2j * np.pi * ((grid[:, None] * grid[None, :]) % width) / width) / math.sqrt(width)
    chirp = np.exp(-1j * PROPAGATION * np.pi * frequency.astype(np.float64) ** 2 / width)
    step = dft.conj() @ (chirp[:, None] * dft)
    step = 0.5 * (step + step.T)
    full = np.stack([block_form(m) for m in (step, step.conj(), dft, dft.conj())])
    high = full.astype(np.float32).astype(ml_dtypes.bfloat16)
    low = (full - high.astype(np.float64)).astype(np.float32).astype(ml_dtypes.bfloat16)
    return np.stack([high, low], axis=1)


def halves(x):
    high = x.astype(jnp.bfloat16)
    return high, (x - high.astype(jnp.float32)).astype(jnp.bfloat16)


def dot(a, b):
    return jnp.dot(a, b, preferred_element_type=jnp.float32)


def times_right(x, high, low):
    x_high, x_low = halves(x)
    return dot(jnp.concatenate([x_high, x_low, x_high], axis=1), jnp.concatenate([high, high, low], axis=0))


def times_left(high, low, x):
    x_high, x_low = halves(x)
    y = dot(jnp.concatenate([high, high, low], axis=1), jnp.concatenate([x_high, x_low, x_high], axis=0))
    n = x.shape[0]
    return y[:n, :n] - y[n:, n:], y[:n, n:] + y[n:, :n]


def both_sides(re, im, tables, which):
    n = re.shape[0]
    y = times_right(jnp.concatenate([re, im], axis=1), tables[which ^ 1, 0], tables[which ^ 1, 1])
    return times_left(tables[which, 0, :, :n], tables[which, 1, :, :n], y)


def share(offsets, tile_rows):
    a = jnp.where(offsets[1] >= offsets[0], 1, 0)
    return a, offsets[2 + a], offsets[1 - a] - offsets[a] + tile_rows, offsets[3 - a]


def cut(tile, row, col, width):
    rows, cols = tile.shape
    part = pltpu.roll(tile, lax.rem(cols - col, cols), 1)[:, :width]
    return pltpu.roll(part, lax.rem(rows - row, rows), 0)


def own_kernel(offsets, objects, tiles, window_b):
    slab, _, rows, _ = objects.shape
    _, _, row_b, col_b = share(offsets, rows)
    for s in range(slab):
        for p in range(2):
            tile = objects[s, p]
            tiles[s, p] = tile
            window_b[s, p] = cut(tile, row_b, col_b, window_b.shape[-1])


def prev_kernel(offsets_prev, after, tiles, window_a, halo):
    slab, _, rows, _ = tiles.shape
    width = halo.shape[-1]
    _, col_a, row_p, col_p = share(offsets_prev, rows)
    for s in range(slab):
        for p in range(2):
            halo[s, p] = cut(tiles[s, p], row_p, col_p, width)
            window_a[s, p] = cut(tiles[s, p], 0, col_a, width)


def hold_kernel(after, x, out):
    out[...] = x[...]


def load_kernel(offsets, offsets_prev, intensity, far, probe, measured, start):
    rows = probe.shape[-1]
    near_a, _, _, _ = share(offsets, rows)
    far_a, _, _, _ = share(offsets_prev, rows)
    measured[...] = jnp.where(lax.axis_index("depth") == 0, far[far_a], intensity[1 - near_a])
    start[...] = probe[...]


def wave_kernel(depth_count, offsets, tables, probe, measured, window_a, window_b, halo, *rest):
    others_a, others_b, halos = (rest[(depth_count - 1) * k : (depth_count - 1) * (k + 1)] for k in range(3))
    rest = rest[3 * depth_count - 3 :]
    grads, probe_parts = rest[:depth_count], rest[depth_count : 2 * depth_count]
    layers, waves = rest[2 * depth_count :]
    slab = window_a.shape[0]
    n = probe.shape[-1]
    count = slab * depth_count
    depth = lax.axis_index("depth")
    on_a = depth == 0
    _, _, row_b, _ = share(offsets, n)
    inside = lax.broadcasted_iota(jnp.int32, (n, n), 0) < n - row_b
    for q in range(depth_count):
        of_a = (window_a, *others_a)[-q % depth_count]
        of_b, below = (window_b, *others_b)[(1 - q) % depth_count], (halo, *halos)[(1 - q) % depth_count]
        for s in range(slab):
            for p in range(2):
                b_layer = jnp.where(inside, of_b[s, p], below[s, p])
                layers[q * slab + s, p] = jnp.where(on_a, of_a[s, p], b_layer)

    def enter(s, re, im):
        waves[s, 0] = re
        waves[s, 1] = im
        o_re, o_im = layers[s, 0], layers[s, 1]
        return re * o_re - im * o_im, re * o_im + im * o_re

    def forward(s, wave):
        return both_sides(*enter(s, *wave), tables, 0)

    wave = lax.fori_loop(0, count - 1, forward, (probe[0], probe[1]), unroll=True if count <= 8 else 1)
    far_re, far_im = both_sides(*enter(count - 1, *wave), tables, 2)
    misfit = 2.0 * (far_re * far_re + far_im * far_im - measured[...])
    chi = both_sides(misfit * far_re, misfit * far_im, tables, 3)

    def leave(s, chi_re, chi_im):
        w_re, w_im = waves[s, 0], waves[s, 1]
        o_re, o_im = layers[s, 0], layers[s, 1]
        waves[s, 0] = w_re * chi_re + w_im * chi_im
        waves[s, 1] = w_re * chi_im - w_im * chi_re
        return o_re * chi_re + o_im * chi_im, o_re * chi_im - o_im * chi_re

    def backward(t, chi):
        return both_sides(*leave(count - 1 - t, *chi), tables, 1)

    chi = lax.fori_loop(0, count - 1, backward, chi, unroll=True if count <= 8 else 1)
    grad = leave(0, *chi)
    turn = lax.rem(jnp.where(on_a, 0, row_b), n)
    for j in range(depth_count):
        base = lax.rem(depth + j, depth_count) * slab
        for s in range(slab):
            for p in range(2):
                grads[j][s, p] = pltpu.roll(waves[base + s, p], turn, 0)
    rows = n // depth_count
    waves[0, 0] = jnp.where(depth < 2, grad[0], 0.0)
    waves[0, 1] = jnp.where(depth < 2, grad[1], 0.0)
    for j in range(depth_count):
        start = pl.multiple_of(lax.rem(depth + j, depth_count) * rows, rows)
        for p in range(2):
            probe_parts[j][p] = waves[0, p, pl.ds(start, rows), :]


def placed(x, col, mask, cols):
    blank = jnp.zeros((x.shape[0], cols - x.shape[1]), x.dtype)
    return pltpu.roll(jnp.concatenate([jnp.where(mask, x, 0.0), blank], axis=1), col, 1)


def place_kernel(depth_count, offsets, offsets_prev, *refs):
    *parts, out = refs
    slab, _, rows, cols = out.shape
    depth = lax.axis_index("depth")
    _, _, row_b, col_b = share(offsets, rows)
    _, col_a, _, _ = share(offsets_prev, rows)
    row_index = lax.broadcasted_iota(jnp.int32, (rows, parts[0].shape[-1]), 0)
    corners = []
    for j in range(depth_count):
        is_a = depth == j
        is_b = lax.rem(depth + depth_count - 1, depth_count) == j
        first = jnp.where(is_a, 0, row_b)
        last = jnp.where(is_a | is_b, rows, 0)
        corners.append((jnp.where(is_a, col_a, col_b), (row_index >= first) & (row_index < last)))
    for s in range(slab):
        for p in range(2):
            total = None
            for (col, mask), part in zip(corners, parts):
                x = placed(part[s, p], col, mask, cols)
                total = x if total is None else total + x
            out[s, p] = total


def step_kernel(depth_count, later, slices, *refs):
    a, b, *parts = refs[later:-2] if slices else refs[later:-1]
    total = refs[-2] if slices else refs[-1]
    total[...] = a[...] + b[...]
    place = lax.rem(lax.axis_index("depth") + depth_count - 1, depth_count)
    for j, part in enumerate(parts):

        @pl.when(place == j)
        def _():
            for i, s in enumerate(slices):
                refs[-1][i] = part[s]


def spill_kernel(offsets_prev, before, a, b, *refs):
    *spills, out, total = refs
    total[...] = a[...] + b[...]
    slab, _, rows, cols = out.shape
    _, _, row_p, col_p = share(offsets_prev, rows)
    mask = lax.broadcasted_iota(jnp.int32, (rows, spills[0].shape[-1]), 0) < row_p
    came = [(spill, i) for spill in spills for i in range(spill.shape[0])]
    for s in range(slab):
        for p in range(2):
            out[s, p] = before[s, p] + placed(came[s][0][came[s][1], p], col_p, mask, cols)


def call(kernel, name, scalars, arrays, outs, scratch=(), work=10**9, after=()):
    vmem = pl.BlockSpec(memory_space=pltpu.VMEM)
    moved = sum(math.prod(x.shape) * x.dtype.itemsize for x in (*arrays, *outs))
    return pl.pallas_call(
        kernel,
        name=name,
        out_shape=outs,
        in_specs=[pl.BlockSpec(memory_space=pltpu.SMEM)] * len(scalars)
        + [pl.BlockSpec(memory_space=pl.ANY)] * len(after)
        + [vmem] * len(arrays),
        out_specs=[vmem] * len(outs),
        scratch_shapes=scratch,
        compiler_params=pltpu.CompilerParams(vmem_limit_bytes=VMEM_LIMIT),
        cost_estimate=pl.CostEstimate(flops=work, bytes_accessed=moved, transcendentals=0),
    )(*scalars, *after, *arrays)


def sum_round(x, level):
    depth_count, scan_count = lax.axis_size("depth"), lax.axis_size("scan")
    levels = scan_count.bit_length() - 1
    route = []
    for d in range(depth_count):
        middle = level + 1 if d % 2 else levels - level
        step = 1 << (0 if level == 0 else 1 if level == levels - 1 else middle)
        route += [(d * scan_count + i, d * scan_count + (i ^ step)) for i in range(scan_count)]
    return lax.ppermute(x, ("depth", "scan"), route)


def body(objects, probe, row_offsets, col_offsets, intensity):
    slab = objects.shape[0]
    n = probe.shape[-1]
    depth_count, scan_count = lax.axis_size("depth"), lax.axis_size("scan")
    f32 = jnp.float32

    def across(x, source, target, shift):
        route = [(source * scan_count + i, target * scan_count + (i + shift) % scan_count) for i in range(scan_count)]
        return lax.ppermute(x, ("depth", "scan"), route)

    offsets = jnp.concatenate([row_offsets, col_offsets])
    offsets_prev = lax.ppermute(offsets, "scan", [(i, (i + 1) % scan_count) for i in range(scan_count)])
    far = across(intensity, 0, 0, 1)
    window = jax.ShapeDtypeStruct((slab, 2, n, n), f32)
    whole = jax.ShapeDtypeStruct(objects.shape, f32)
    tiles, window_b = call(own_kernel, "own", [offsets], [objects], [whole, window])
    window_a, halo = call(prev_kernel, "prev", [offsets_prev], [tiles], [window] * 2, after=[far])
    halo = lax.ppermute(halo, "scan", [((i + 1) % scan_count, i) for i in range(scan_count)])

    def gathered(x, target):
        return [lax.ppermute(x, "depth", [((target - j) % depth_count, target)]) for j in range(1, depth_count)]

    others_a = gathered(window_a, 0)
    measured, start = call(
        load_kernel,
        "load",
        [offsets, offsets_prev],
        [intensity, far, probe],
        [jax.ShapeDtypeStruct((n, n), f32), jax.ShapeDtypeStruct(probe.shape, f32)],
    )

    (halo,) = call(hold_kernel, "hold", [], [halo], [window], after=[measured])
    others_b, halos = gathered(window_b, 1), gathered(halo, 1)

    tables = jnp.asarray(constant_tables(n))
    count = slab * depth_count
    parts = call(
        lambda *refs: wave_kernel(depth_count, *refs),
        "wave",
        [offsets],
        [tables, start, measured, window_a, window_b, halo, *others_a, *others_b, *halos],
        [window] * depth_count + [jax.ShapeDtypeStruct((2, n // depth_count, n), f32)] * depth_count,
        [pltpu.VMEM((count, 2, n, n), f32)] * 2,
        work=5 * 10**9,
    )
    grads, probe_parts = parts[:depth_count], parts[depth_count:]

    back, sums = [grads[0]], [probe_parts[0]]
    for j in range(1, depth_count):
        sums.append(lax.ppermute(probe_parts[j], "depth", [(t, (t + j) % depth_count) for t in range(depth_count)]))
        back.append(lax.ppermute(grads[j], "depth", [(t, (t + j) % depth_count) for t in (0, 1)]))

    half = jax.ShapeDtypeStruct(sums[0].shape, f32)
    ahead = [(i, (i + 1) % scan_count) for i in range(scan_count)]
    rounds = scan_count.bit_length() - 1
    paired = scan_count == 1 << rounds and rounds > 2
    spill = []

    def step(a, b, slices, after):
        outs = [half, jax.ShapeDtypeStruct((len(slices), 2, n, n), f32)] if slices else [half]
        return call(
            lambda *refs: step_kernel(depth_count, len(after), slices, *refs),
            "step",
            [],
            [a, b, *(back if slices else [])],
            outs,
            after=after,
        )

    (object_grad,) = call(
        lambda *refs: place_kernel(depth_count, *refs),
        "place",
        [offsets, offsets_prev],
        back,
        [whole],
        work=2 * 10**9,
    )
    turns = rounds - 1 if paired else 1
    cuts = [0, slab // 3] + [slab] * (turns - 1) if turns > 1 else [0, slab]
    share_of = [tuple(range(cuts[k], cuts[k + 1])) for k in range(turns)]
    total = sums[0]
    for x in sums[1:-1]:
        total = total + x
    other = sums[-1] if depth_count > 1 else jnp.zeros_like(total)
    for k, slices in enumerate(share_of):
        total, *payload = step(total, other, slices, spill[:1] if k == 2 else [])
        other = sum_round(total, k) if paired else jnp.zeros_like(total)
        spill += [lax.ppermute(x, "scan", ahead) for x in payload]
    if paired:
        (total,) = step(total, other, (), [object_grad])
        other = sum_round(total, rounds - 1)
    object_grad, total = call(
        spill_kernel, "spill", [offsets_prev], [object_grad, total, other, *spill], [whole, half]
    )
    if not paired:
        total = lax.psum(total, "scan")
    return object_grad, total


def solution(mesh):
    in_specs = (P("depth", None, "scan", None), P(), P("scan"), P("scan"), P("scan", None, None))
    out_specs = (P("depth", None, "scan", None), P(None, "depth", None))
    return jax.shard_map(body, mesh=mesh, in_specs=in_specs, out_specs=out_specs, check_vma=False)
```
